32 devices in a mesh: dp: 8 (over z, y), tensor: 4 (over x, core).
Axes of the slice: x: 2, y: 2, z: 4, core: 2. Of those that a mesh axis runs over, the one named last changes fastest.
Arguments:
- token_ids: int32 [64, 256], P('dp'), may hold values from 0 to 2023
- masked_at: int32 [64, 128], P('dp'), may hold values from 0 to 255, as said below
- live_counts: int32 [64], P('dp'), may hold values from 1 to 128
- tables: bfloat16 [2281, 768], P(None, 'tensor'), may hold values from -1 to 1
- table_mom: float32 [2281, 768], P(None, 'tensor'), may hold values from -0.0234375 to 0.0234375
- vec_whole: float32 [8, 768], replicated, may hold values from -1.5 to 1.6, as said below
- vec_mom: float32 [8, 768], replicated, may hold values from -0.0625 to 0.0625
- vec_split: float32 [4, 1152], P('tensor'), may hold values from -4 to 4
- split_mom: float32 [4, 1152], P('tensor'), may hold values from -0.046875 to 0.046875
- head_bias: float32 [2025], replicated, may hold values from -4 to 4
- bias_mom: float32 [2025], replicated, may hold values from -0.015625 to 0.015625
- w_qkv: bfloat16 [768, 2304], P(None, 'tensor'), may hold values from -0.21875 to 0.21875
- w_out: bfloat16 [768, 768], P('tensor'), may hold values from -0.875 to 0.875
- w_up: bfloat16 [768, 3072], P(None, 'tensor'), may hold values from -0.21875 to 0.21875
- w_down: bfloat16 [3072, 768], P('tensor'), may hold values from -0.109375 to 0.109375
- mom_qkv: float32 [768, 2304], P(None, 'tensor'), may hold values from -0.0048828125 to 0.0048828125
- mom_out: float32 [768, 768], P('tensor'), may hold values from -0.0048828125 to 0.0048828125
- mom_up: float32 [768, 3072], P(None, 'tensor'), may hold values from -0.0048828125 to 0.0048828125
- mom_down: float32 [3072, 768], P('tensor'), may hold values from -0.0048828125 to 0.0048828125
- err_qkv: float32 [8, 768, 2304], P('dp', None, 'tensor'), may hold values from -0.00390625 to 0.00390625
- err_out: float32 [8, 768, 768], P('dp', 'tensor'), may hold values from -0.00390625 to 0.00390625
- err_up: float32 [8, 768, 3072], P('dp', None, 'tensor'), may hold values from -0.00390625 to 0.00390625
- err_down: float32 [8, 3072, 768], P('dp', 'tensor'), may hold values from -0.00390625 to 0.00390625
- start_qkv: float32 [2304, 8], P('tensor'), may hold values from -6 to 6
- start_out: float32 [3072, 8], P('tensor'), may hold values from -6 to 6
- start_up: float32 [3072, 8], P('tensor'), may hold values from -6 to 6
- start_down: float32 [3072, 8], P('tensor'), may hold values from -6 to 6
Outputs:
- loss: float32 [2], replicated
- tables_new: float32 [2281, 768], P(None, 'tensor')
- table_mom_new: float32 [2281, 768], P(None, 'tensor')
- vec_whole_new: float32 [8, 768], replicated
- vec_mom_new: float32 [8, 768], replicated
- vec_split_new: float32 [4, 1152], P('tensor')
- split_mom_new: float32 [4, 1152], P('tensor')
- head_bias_new: float32 [2025], replicated
- bias_mom_new: float32 [2025], replicated
- qkv_new: float32 [768, 2304], P(None, 'tensor')
- qkv_mom_new: float32 [768, 2304], P(None, 'tensor')
- qkv_err_new: float32 [8, 768, 2304], P('dp', None, 'tensor')
- qkv_left: float32 [4, 768, 8], P('tensor')
- qkv_right: float32 [2304, 8], P('tensor')
- out_new: float32 [768, 768], P('tensor')
- out_mom_new: float32 [768, 768], P('tensor')
- out_err_new: float32 [8, 768, 768], P('dp', 'tensor')
- out_left: float32 [4, 192, 8], P('tensor')
- out_right: float32 [3072, 8], P('tensor')
- up_new: float32 [768, 3072], P(None, 'tensor')
- up_mom_new: float32 [768, 3072], P(None, 'tensor')
- up_err_new: float32 [8, 768, 3072], P('dp', None, 'tensor')
- up_left: float32 [4, 768, 8], P('tensor')
- up_right: float32 [3072, 8], P('tensor')
- down_new: float32 [3072, 768], P('tensor')
- down_mom_new: float32 [3072, 768], P('tensor')
- down_err_new: float32 [8, 3072, 768], P('dp', 'tensor')
- down_left: float32 [4, 768, 8], P('tensor')
- down_right: float32 [3072, 8], P('tensor')
The draws below stay inside these ranges and needn't reach their ends.
Inputs may be any that keep to these rules, and one draw needn't show every extreme that they name: `masked_at`: the positions of one image's slots are distinct. `vec_whole`: rows 0, 3 and 6 are gains, the others biases.
All inputs are finite; a program needn't handle non-finite values.
Results may differ from the reference program's by a relative error of at most 0.0078.
Values may be sent and summed in bfloat16 or wider, within the bound.
No kernel may reach another device: no remote copies, remote signals or barrier semaphores. Data moves between devices by JAX's collectives and lax.ppermute only.
A program may use at most 192 MiB of HBM per device.

```python
import jax
import jax.numpy as jnp
from jax import lax

D = 768
HEADS = 16
HD = 48
FF = 3072
VOCAB = 2025
LEN = 256
MASK_SLOTS = 128
RANK = 8
IMAGES = 64
N_DP = 8
N_TENSOR = 4


def draw_live_counts(key, part):
    key = jax.random.fold_in(key, 11)
    ranks = jnp.arange(IMAGES, dtype=jnp.int32)
    floor_count = MASK_SLOTS // 3 + 2 * MASK_SLOTS * ranks // (3 * IMAGES)
    extra = jax.random.randint(key, (IMAGES,), 0, MASK_SLOTS // 6 + 2)
    counts = jnp.maximum(jnp.minimum(floor_count + extra, MASK_SLOTS), 1)
    return counts.at[IMAGES - 1].set(MASK_SLOTS).astype(jnp.int32)


def draw_masked_at(key, part):
    key = jax.random.fold_in(key, 5)
    keys = jax.random.split(key, IMAGES)
    return jax.vmap(lambda one: jax.random.permutation(one, LEN)[:MASK_SLOTS])(keys).astype(jnp.int32)


def draw_vec_whole(key, part):
    key = jax.random.fold_in(key, 7)
    gain_key, shift_key = jax.random.split(key)
    gains = jax.random.uniform(gain_key, (8, D), jnp.float32, 0.6, 1.6)
    shifts = jnp.clip(0.3 * jax.random.normal(shift_key, (8, D), jnp.float32), -1.5, 1.5)
    is_gain = (jnp.arange(8) % 3 == 0)[:, None]
    return jnp.where(is_gain, gains, shifts)


def plant(result, stream_key, low, high):
    dims = result.shape
    spot = [jax.random.randint(jax.random.fold_in(stream_key, axis), (), 0, dims[axis]) for axis in range(len(dims))]
    result = result.at[tuple(spot)].set(low)
    longest = dims.index(max(dims))
    spot[longest] = (spot[longest] + 1) % dims[longest]
    return result.at[tuple(spot)].set(high)


def steps_of(key, shape, cuts, smallest, top_value):
    loudness, own = 1.0, jax.random.fold_in(key, 6)
    for dim, blocks in cuts:
        heights = jnp.exp(jax.random.uniform(jax.random.fold_in(own, dim), (blocks,), jnp.float32, smallest / len(cuts), top_value / len(cuts)))
        loudness = loudness * jnp.repeat(heights, shape[dim] // blocks).reshape([-1 if axis == dim else 1 for axis in range(len(shape))])
    return loudness


def centred(own_key, dims, scale, reach, cuts=(), kind=jnp.bfloat16):
    drawn = jax.random.normal(own_key, dims, jnp.float32) * scale
    if len(cuts) > 0:
        drawn = steps_of(own_key, dims, cuts, -0.22, 0.18) * drawn
    return jnp.clip(drawn, min=-reach, max=reach).astype(kind)


def setup_inputs(seed: int = 0) -> dict:
    splits = jax.random.split(jax.random.key(seed), 28)
    return {
        "token_ids": plant(jax.random.randint(splits[0], (IMAGES, LEN), 0, VOCAB - 1), jax.random.fold_in(splits[0], 1), 0, (VOCAB - 1) - 1).astype(jnp.int32),
        "masked_at": draw_masked_at(jax.random.fold_in(splits[27], 71), 0),
        "live_counts": draw_live_counts(jax.random.fold_in(splits[27], 71), 0),
        "tables": centred(splits[3], (VOCAB + LEN, D), (2.0 * D ** -0.5), 1.0, ((1, 4),)),
        "table_mom": centred(splits[4], (VOCAB + LEN, D), 0.0015, 0.0234375, ((1, 4),), jnp.float32),
        "vec_whole": draw_vec_whole(jax.random.fold_in(splits[27], 71), 0),
        "vec_mom": centred(splits[6], (8, D), 0.004, 0.0625, (), jnp.float32),
        "vec_split": centred(splits[7], (N_TENSOR, (2 * D + FF) // N_TENSOR), 0.3, 4.0, ((0, 4),), jnp.float32),
        "split_mom": centred(splits[8], (N_TENSOR, (2 * D + FF) // N_TENSOR), 0.003, 0.046875, ((0, 4),), jnp.float32),
        "head_bias": centred(splits[9], (VOCAB,), 0.5, 4.0, (), jnp.float32),
        "bias_mom": centred(splits[10], (VOCAB,), 0.001, 0.015625, (), jnp.float32),
        "w_qkv": centred(splits[11], (D, 3 * D), D ** -0.5, 0.21875, ((1, 4),)),
        "w_out": centred(splits[12], (D, D), (D // 16) ** -0.5, 0.875, ((0, 4),)),
        "w_up": centred(splits[13], (D, FF), D ** -0.5, 0.21875, ((1, 4),)),
        "w_down": centred(splits[14], (FF, D), FF ** -0.5, 0.109375, ((0, 4),)),
        "mom_qkv": centred(splits[15], (D, 3 * D), (0.001 * N_DP ** -0.5), 0.0048828125, ((1, 4),), jnp.float32),
        "mom_out": centred(splits[16], (D, D), (0.001 * N_DP ** -0.5), 0.0048828125, ((0, 4),), jnp.float32),
        "mom_up": centred(splits[17], (D, FF), (0.001 * N_DP ** -0.5), 0.0048828125, ((1, 4),), jnp.float32),
        "mom_down": centred(splits[18], (FF, D), (0.001 * N_DP ** -0.5), 0.0048828125, ((0, 4),), jnp.float32),
        "err_qkv": centred(splits[19], (N_DP, D, 3 * D), (0.002 * N_DP ** -1), 0.00390625, ((0, 8), (2, 4)), jnp.float32),
        "err_out": centred(splits[20], (N_DP, D, D), (0.002 * N_DP ** -1), 0.00390625, ((0, 8), (1, 4)), jnp.float32),
        "err_up": centred(splits[21], (N_DP, D, FF), (0.002 * N_DP ** -1), 0.00390625, ((0, 8), (2, 4)), jnp.float32),
        "err_down": centred(splits[22], (N_DP, FF, D), (0.002 * N_DP ** -1), 0.00390625, ((0, 8), (1, 4)), jnp.float32),
        "start_qkv": centred(splits[23], (3 * D, RANK), 1.0, 6.0, ((0, 4),), jnp.float32),
        "start_out": centred(splits[24], (N_TENSOR * D, RANK), 1.0, 6.0, ((0, 4),), jnp.float32),
        "start_up": centred(splits[25], (FF, RANK), 1.0, 6.0, ((0, 4),), jnp.float32),
        "start_down": centred(splits[26], (N_TENSOR * D, RANK), 1.0, 6.0, ((0, 4),), jnp.float32),
    }


@jax.custom_vjp
def low(v):
    return lax.optimization_barrier(v.astype(jnp.bfloat16)).astype(jnp.float32)

@jax.custom_vjp
def low_back(v):
    return v

def low_keep(v):
    return (low(v), None)

def low_pass(kept, grad):
    return (grad,)

def back_keep(v):
    return (v, None)

def back_low(kept, grad):
    return (low(grad),)
low.defvjp(low_keep, low_pass)
low_back.defvjp(back_keep, back_low)
HIGHEST = lax.Precision.HIGHEST
EPSILON = 1e-05
BETA = 0.9
RATE_MAT = 100.0
RATE_VEC = 10.0
RATE_TAB = 100.0

def dotf(left, right):
    return jnp.dot(left, right, precision=HIGHEST)

def layer_norm(x, gain, shift):
    center = x - lax.optimization_barrier(jnp.mean(x, -1, keepdims=True))
    spread = lax.optimization_barrier(jnp.mean(center * center, -1, keepdims=True))
    return center * lax.rsqrt(spread + EPSILON) * gain + shift

def orthonormal(panel):
    columns = []
    for number in range(panel.shape[-1]):
        column = panel[..., number]
        for earlier in columns:
            column = column - lax.optimization_barrier(jnp.sum(earlier * column, -1, keepdims=True)) * earlier
        column = column * lax.rsqrt(lax.optimization_barrier(jnp.sum(column * column, -1, keepdims=True)) + 1e-20)
        columns.append(column)
    return jnp.stack(columns, -1)

def forward(params, token_ids, masked_at, live_counts, count):
    tables, vec_whole, vec_split, head_bias, w_qkv, w_out, w_up, w_down = params
    groups = N_TENSOR
    width = HEADS // groups * HD
    images = token_ids.shape[0]
    positions = jnp.arange(LEN, dtype=jnp.int32)
    live_slot = jnp.arange(MASK_SLOTS, dtype=jnp.int32)[None, :] < live_counts[:, None]
    masked = jnp.any((masked_at[:, :, None] == positions[None, None, :]) & live_slot[:, :, None], axis=1)
    inputs = jnp.where(masked, VOCAB - 1, token_ids)
    embedded = (tables[inputs] + tables[VOCAB + positions][None]).reshape(-1, D)
    h_zero = layer_norm(embedded, vec_whole[0], vec_whole[1])
    q_bias = vec_split[:, :width].reshape(-1)
    v_bias = vec_split[:, width:2 * width].reshape(-1)
    u_bias = vec_split[:, 2 * width:].reshape(-1)
    mixed = low_back(dotf(low(h_zero), w_qkv)).reshape(-1, groups, 3, width)
    scale = HD ** (-0.5)
    queries = low((mixed[:, :, 0].reshape(-1, D) + q_bias) * scale)
    key_rows = low(mixed[:, :, 1].reshape(-1, D))
    value_rows = low(mixed[:, :, 2].reshape(-1, D) + v_bias)
    shape4 = (images, LEN, HEADS, HD)
    scores = low_back(jnp.einsum('bqhd,bkhd->bhqk', queries.reshape(shape4), key_rows.reshape(shape4), precision=HIGHEST))
    probs = low(jax.nn.softmax(scores, -1))
    context = jnp.einsum('bhqk,bkhd->bqhd', probs, value_rows.reshape(shape4), precision=HIGHEST).reshape(-1, D)
    context = low(low_back(context))
    attended = low_back(dotf(context, w_out)) + vec_whole[2]
    h_one = layer_norm(h_zero + attended, vec_whole[3], vec_whole[4])
    hidden_pre = low_back(dotf(low(h_one), w_up)) + u_bias
    active = low(jax.nn.gelu(hidden_pre))
    lowered = low_back(dotf(active, w_down)) + vec_whole[5]
    h_two = layer_norm(h_one + lowered, vec_whole[6], vec_whole[7])
    rows = (jnp.arange(images, dtype=jnp.int32)[:, None] * LEN + masked_at).reshape(-1)
    picked = low(h_two[rows])
    logits = low_back(dotf(picked, tables[:VOCAB].T)) + head_bias
    targets = jnp.take_along_axis(token_ids, masked_at, 1).reshape(-1)
    log_total = jax.nn.logsumexp(logits, -1)
    chosen = jnp.take_along_axis(logits, targets[:, None], 1)[:, 0]
    loss = jnp.sum(jnp.where(live_slot.reshape(-1), log_total - chosen, 0.0))
    return (loss / count, loss)

def to_shards(stack, cols):
    n, rows, width = stack.shape
    if cols:
        return stack.reshape(n, rows, N_TENSOR, width // N_TENSOR).transpose(2, 0, 1, 3)
    return stack.reshape(n, N_TENSOR, rows // N_TENSOR, width).transpose(1, 0, 2, 3)

def from_shards(shards, cols):
    groups, n, rows, width = shards.shape
    if cols:
        return shards.transpose(1, 2, 0, 3).reshape(n, rows, groups * width)
    return shards.transpose(1, 0, 2, 3).reshape(n, groups * rows, width)

def compress(grads, error, start, cols):
    merged = to_shards(grads + error, cols)
    factor = start.reshape(N_TENSOR, -1, RANK)
    left = orthonormal(jnp.einsum('tnab,tbr->tar', merged, factor, precision=HIGHEST))
    right = jnp.einsum('tnab,tar->tbr', merged, left, precision=HIGHEST) / N_DP
    approx = jnp.einsum('tar,tbr->tab', left, right, precision=HIGHEST)
    new_error = from_shards(merged - approx[:, None], cols)
    return (left, right.reshape(-1, RANK), new_error, from_shards(approx[:, None], cols)[0])

def momentum_step(weight, moment, grad, rate):
    new_moment = BETA * moment + grad
    return (weight.astype(jnp.float32) - rate * new_moment, new_moment)

def reference(token_ids, masked_at, live_counts, tables, table_mom, vec_whole, vec_mom, vec_split, split_mom, head_bias, bias_mom, w_qkv, w_out, w_up, w_down, mom_qkv, mom_out, mom_up, mom_down, err_qkv, err_out, err_up, err_down, start_qkv, start_out, start_up, start_down):
    params = tuple((a.astype(jnp.float32) for a in (tables, vec_whole, vec_split, head_bias, w_qkv, w_out, w_up, w_down)))
    count = jnp.sum(live_counts).astype(jnp.float32)

    def shard(pieces):
        shard_ids, shard_slots, shard_live = pieces
        objective, pull, loss = jax.vjp(lambda p: forward(p, shard_ids, shard_slots, shard_live, count), params, has_aux=True)
        return (loss, pull(jnp.ones((), jnp.float32))[0])
    losses, grads = lax.map(shard, (token_ids.reshape(N_DP, -1, LEN), masked_at.reshape(N_DP, -1, MASK_SLOTS), live_counts.reshape(N_DP, -1)))
    loss = jnp.stack([jnp.sum(losses), count])
    tables_new, table_mom_new = momentum_step(tables, table_mom, lax.optimization_barrier(jnp.sum(grads[0], 0)), RATE_TAB)
    vec_whole_new, vec_mom_new = momentum_step(vec_whole, vec_mom, lax.optimization_barrier(jnp.sum(grads[1], 0)), RATE_VEC)
    vec_split_new, split_mom_new = momentum_step(vec_split, split_mom, lax.optimization_barrier(jnp.sum(grads[2], 0)), RATE_VEC)
    head_bias_new, bias_mom_new = momentum_step(head_bias, bias_mom, lax.optimization_barrier(jnp.sum(grads[3], 0)), RATE_VEC)
    results = [loss, tables_new, table_mom_new, vec_whole_new, vec_mom_new, vec_split_new, split_mom_new, head_bias_new, bias_mom_new]
    plans = [(w_qkv, mom_qkv, err_qkv, start_qkv, grads[4], True), (w_out, mom_out, err_out, start_out, grads[5], False), (w_up, mom_up, err_up, start_up, grads[6], True), (w_down, mom_down, err_down, start_down, grads[7], False)]
    for weight, moment, error, start, grad_stack, cols in plans:
        left, right, new_error, approx = compress(grad_stack, error, start, cols)
        new_weight, new_moment = momentum_step(weight, moment, approx, RATE_MAT)
        results += [new_weight, new_moment, new_error, left, right]
    return tuple(results)
```

```python
import functools

import jax
import jax.numpy as jnp
from jax import lax
from jax.experimental import pallas as pl
from jax.experimental.pallas import tpu as pltpu
from jax.sharding import PartitionSpec as P

HD = 48
EPSILON = 1e-05
BETA = 0.9
RATE_MAT = 100.0
RATE_VEC = 10.0
RATE_TAB = 100.0
HIGHEST = lax.Precision.HIGHEST
BF16 = jnp.bfloat16
F32 = jnp.float32
MIB = 1024 * 1024


def bdot(left, right):
    return jnp.dot(left, right, preferred_element_type=F32)


def tdot(left, right):
    return lax.dot_general(left, right, (((0,), (0,)), ((), ())), preferred_element_type=F32)


def ndot(left, right):
    return lax.dot_general(left, right, (((1,), (1,)), ((), ())), preferred_element_type=F32)


def across(x, axis, bit):
    size = lax.axis_size(axis)
    return lax.ppermute(x, axis, [(i, i ^ bit) for i in range(size)])


def core_swap(x):
    return across(x, "tensor", 1)


def chip_swap(x):
    return across(x, "tensor", 2)


def dp_sum(x):
    size = lax.axis_size("dp")
    if size & (size - 1):
        return lax.psum(x, "dp")
    bit = 1
    while bit < size:
        x = x + across(x, "dp", bit)
        bit *= 2
    return x


def tie(x, *others):
    return lax.optimization_barrier((x,) + others)[0]


def gather_blocks(block):
    far = chip_swap(block)
    return [block, core_swap(block), far, core_swap(far)]


def head_mask(width, head):
    lane = lax.broadcasted_iota(jnp.int32, (1, width), 1)
    return ((lane >= head * HD) & (lane < (head + 1) * HD)).astype(BF16)


SCALE = 10.0
LIMITS = {
    "pack": (56, 3), "embed": (8, 5), "attention_first": (10, 7), "attention_second": (10, 8), "mlp_first": (12, 7),
    "mlp_second": (14, 7), "head": (24, 9), "down_send": (8, 3), "down_keep": (14, 4), "up_send": (14, 6),
    "up_keep": (20, 8), "attention_send": (14, 13), "attention_keep": (20, 15), "scatter": (8, 5),
    "orthonormal": (4, 3), "right_mlp": (16, 3), "right_attention": (12, 2), "update": (16, 4),
}


def call(kernel, name, out_shape, operands, in_specs=None, scratch=(), out_specs=None, **grid):
    limit, cost = LIMITS[name]
    if in_specs is None:
        in_specs = [pl.BlockSpec(memory_space=pltpu.VMEM)] * len(operands)
    if out_specs is not None:
        grid["out_specs"] = out_specs
    return pl.pallas_call(
        kernel,
        out_shape=out_shape,
        in_specs=in_specs,
        scratch_shapes=list(scratch),
        compiler_params=pltpu.CompilerParams(vmem_limit_bytes=limit * MIB),
        cost_estimate=pl.CostEstimate(flops=int(cost * SCALE * 1150000000), bytes_accessed=int(cost * SCALE * 1000000), transcendentals=0),
        name=name,
        **grid,
    )(*operands)


VMEM = pl.BlockSpec(memory_space=pltpu.VMEM)
SMEM = pl.BlockSpec(memory_space=pltpu.SMEM)
ANY = pl.BlockSpec(memory_space=pltpu.HBM)


def shape(*dims, dtype=F32):
    return jax.ShapeDtypeStruct(dims, dtype)


def normalize(x):
    center = x - jnp.mean(x, -1, keepdims=True)
    inverse = lax.rsqrt(jnp.mean(center * center, -1, keepdims=True) + EPSILON)
    return center * inverse, inverse


def norm_back(normed, inverse, gain, grad):
    inner = grad * gain
    first = jnp.mean(inner, -1, keepdims=True)
    second = jnp.mean(inner * normed, -1, keepdims=True)
    d_x = inverse * (inner - first - normed * second)
    return d_x, jnp.sum(grad * normed, 0, keepdims=True), jnp.sum(grad, 0, keepdims=True)


def split3(x):
    high = x.astype(BF16).astype(F32)
    rest = x - high
    middle = rest.astype(BF16).astype(F32)
    return jnp.concatenate([high, middle, rest - middle], 0).astype(BF16)


def fold3(x):
    rank = x.shape[0] // 3
    return x[:rank] + x[rank : 2 * rank] + x[2 * rank :]


def panel(start, right, left):
    return fold3(bdot(split3(fold3(ndot(split3(start), right))), left))


def split2(x):
    high = x.astype(BF16)
    return high, (x - high.astype(F32)).astype(BF16)


def wide(dot, start, x):
    parts = split3(start)
    high, rest = split2(x)
    return fold3(dot(parts, high) + dot(parts, rest))


class Fetch:
    def __init__(self, meta_ref, sems):
        self.half, self.sems, self.used = meta_ref[1], sems, 0

    def one(self, source, target):
        copy = pltpu.make_async_copy(source, target, self.sems.at[self.used])
        self.used += 1
        copy.start()
        return copy

    def block(self, pieces, target, first=0):
        if len(pieces) == 1:
            return [self.one(pieces[0], target.at[pl.ds(first, pieces[0].shape[0]), :])]
        size = pieces[0].shape[0]
        spots = (first + self.half * size, first + (1 - self.half) * size)
        return [
            self.one(piece, target.at[pl.ds(pl.multiple_of(spot, 32), size), :])
            for piece, spot in zip(pieces, spots)
        ]


def wait(copies):
    for copy in copies:
        copy.wait()


def pack_kernel(meta_ref, qkv_ref, out_ref, up_ref, down_ref, tables_ref, first_ref, first_half, up_half, down_half, table_ref, table_half, sems):
    near, rest = qkv_ref.shape[0], out_ref.shape[0]
    size = first_half.shape[0]
    half = meta_ref[1]
    at = pl.multiple_of(half * size, 32)
    fetch = Fetch(meta_ref, sems)
    firsts = [
        fetch.one(qkv_ref, first_ref.at[pl.ds(0, near), :]),
        fetch.one(out_ref, first_ref.at[pl.ds(near, rest), :]),
    ]
    copies = [
        fetch.one(up_ref.at[pl.ds(at, size), :], up_half),
        fetch.one(down_ref.at[pl.ds(at, size), :], down_half),
    ]
    total = tables_ref.shape[1]
    table_ref[...] = jnp.zeros_like(table_ref)
    table_ref[:, :total] = tables_ref[...]
    rows = table_half.shape[0]
    table_half[...] = table_ref[pl.ds(pl.multiple_of(half * rows, 32), rows), :]
    wait(firsts)
    first_half[...] = first_ref[pl.ds(at, size), :]
    wait(copies)


def embed_kernel(own, vocab, meta_ref, live_ref, ids_ref, slots_ref, table_ref, far_ref, near_ref, own_ref, rows_ref):
    images, length = ids_ref.shape
    slot_count = slots_ref.shape[1]
    total = table_ref.shape[1]
    member = meta_ref[0]
    ids_t = jnp.transpose(ids_ref[...].astype(F32))
    image_lane = lax.broadcasted_iota(jnp.int32, (length, images), 1)
    position = lax.broadcasted_iota(jnp.int32, (length, 1), 0)
    slot_lane = lax.broadcasted_iota(jnp.int32, (1, slot_count), 1)
    table_lane = lax.broadcasted_iota(jnp.int32, (1, total), 1)
    table = table_ref[...]

    def rows_of(ids):
        hot = jnp.where(ids == table_lane, 1.0, 0.0).astype(BF16)
        return ndot(hot, table).astype(BF16)

    targets = {
        0: (own_ref, 0), 1: (near_ref, 0), 2: (far_ref.at[0], 0), 3: (far_ref.at[1], 0),
    }
    for k in range(4):
        for i in range(own):
            image = (member ^ k) * own + i
            hit = (slots_ref[pl.ds(image, 1), :] == position) & (slot_lane < live_ref[image])
            masked = jnp.max(jnp.where(hit, 1.0, 0.0), 1, keepdims=True)
            ids = jnp.sum(jnp.where(image_lane == image, ids_t, 0.0), 1, keepdims=True)
            ids = jnp.where(masked > 0, float(vocab - 1), ids).astype(jnp.int32)
            place = k * own + i
            rows_ref[:, place : place + 1] = ids
            ref, first = targets[k]
            ref[first + i * length : first + (i + 1) * length, :] = rows_of(ids)
    at = rows_of(position + vocab)
    own_ref[own * length :, :] = at
    near_ref[own * length :, :] = at
    far_ref[0, own * length :, :] = at[: length // 2]
    far_ref[1, own * length :, :] = at[length // 2 :]


def attention_one(length, hb, w, bias_ref, qkv_ref, lse_ref, ctx_ref):
    width = ctx_ref.shape[1]
    mixed = ndot(hb, w)
    q_bias = bias_ref[8:9, :width]
    v_bias = bias_ref[8:9, width : 2 * width]
    qkv_ref[0] = ((mixed[:, :width] + q_bias) * HD ** (-0.5)).astype(BF16)
    qkv_ref[1] = mixed[:, width : 2 * width].astype(BF16)
    qkv_ref[2] = (mixed[:, 2 * width :] + v_bias).astype(BF16)
    for image in range(hb.shape[0] // length):
        rows = slice(image * length, (image + 1) * length)
        q, k, v = qkv_ref[0, rows, :], qkv_ref[1, rows, :], qkv_ref[2, rows, :]
        total = jnp.zeros((length, width), F32)
        for head in range(width // HD):
            mask = head_mask(width, head)
            scores = ndot(q * mask, k)
            top = jnp.max(scores, -1, keepdims=True)
            powers = jnp.exp(scores - top)
            weight = jnp.sum(powers, -1, keepdims=True)
            lse_ref[rows, head : head + 1] = top + jnp.log(weight)
            probs = (powers * (1.0 / weight)).astype(BF16)
            total = total + bdot(probs, v * mask)
        ctx_ref[rows, :] = total.astype(BF16)


def attention_first_kernel(
    length, meta_ref, e0, e1, e2, e3, vec_ref, b0, b1, c0, c1,
    normed_ref, inverse_ref, hb_ref, qkv0, lse0, ctx0, qkv1, lse1, ctx1, x_ref, w_ref, sems,
):
    rows, width = hb_ref.shape[0], e0.shape[1]
    member = meta_ref[0]
    fetch = Fetch(meta_ref, sems)
    used = 3 * width
    zero = fetch.one(c0.at[pl.ds(0, used), :], w_ref.at[0])
    one = fetch.one(c1.at[pl.ds(0, used), :], w_ref.at[1])
    slabs = ((e0, e0, e0), (e1, e1, e1), (e2.at[0], e2.at[0], e2.at[1]), (e3.at[1], e3.at[0], e3.at[1]))
    for t in range(4):

        @pl.when(member == t)
        def _():
            for k, (ref, low, high) in enumerate(slabs):
                at = low[rows:, :] if low is high else jnp.concatenate([low[rows:, :], high[rows:, :]], 0)
                at = at.astype(F32)
                for i in range(rows // length):
                    part = ref[i * length : (i + 1) * length, :].astype(F32)
                    x_ref[i * length : (i + 1) * length, (t ^ k) * width : ((t ^ k) + 1) * width] = part + at

    normed, inverse = normalize(x_ref[...])
    normed_ref[...] = normed
    inverse_ref[...] = inverse
    hb_ref[...] = (normed * vec_ref[0:1, :] + vec_ref[1:2, :]).astype(BF16)
    hb = hb_ref[...]
    zero.wait()
    attention_one(length, hb, w_ref[0], b0, qkv0, lse0, ctx0)
    one.wait()
    attention_one(length, hb, w_ref[1], b1, qkv1, lse1, ctx1)


def attention_second_kernel(
    length, meta_ref, normed_ref, hb_ref, vec_ref, b2, b3, ctx0, ctx1, c0, c1, c2a, c2b, c3a, c3b,
    normed1_ref, inverse1_ref, h1b_ref, qkv2, lse2, ctx2, qkv3, lse3, ctx3, w_ref, o_ref, sems,
):
    hb = hb_ref[...]
    width = ctx0.shape[1]
    used = 3 * width
    fetch = Fetch(meta_ref, sems)
    two = fetch.block((c2a, c2b), w_ref.at[0])
    three = fetch.block((c3a, c3b), w_ref.at[1])
    others = [fetch.one(c.at[pl.ds(used, width), :], o_ref.at[n]) for n, c in enumerate((c0, c1))]
    wait(two)
    attention_one(length, hb, w_ref[0, :used, :], b2, qkv2, lse2, ctx2)
    wait(three)
    attention_one(length, hb, w_ref[1, :used, :], b3, qkv3, lse3, ctx3)
    wait(others)
    total = bdot(ctx0[...], o_ref[0]) + bdot(ctx1[...], o_ref[1])
    total = total + bdot(ctx2[...], w_ref[0, used:, :]) + bdot(ctx3[...], w_ref[1, used:, :])
    z_one = normed_ref[...] * vec_ref[0:1, :] + vec_ref[1:2, :] + (total + vec_ref[2:3, :])
    normed, inverse = normalize(z_one)
    normed1_ref[...] = normed
    inverse1_ref[...] = inverse
    h1b_ref[...] = (normed * vec_ref[3:4, :] + vec_ref[4:5, :]).astype(BF16)


def gelu_pair(x):
    inner = 0.7978845608028654 * x * (1.0 + 0.044715 * x * x)
    curve = jnp.tanh(inner)
    value = 0.5 * x * (1.0 + curve)
    slope = 0.5 * (1.0 + curve) + 0.5 * x * (1.0 - curve * curve) * (
        0.7978845608028654 * (1.0 + 3 * 0.044715 * x * x)
    )
    return value, slope


def mlp_one(h1b, up_ref, bias_ref, active_ref, slope_ref):
    first = 2 * up_ref.shape[0] // 4
    step = 256
    for at in range(0, up_ref.shape[1], step):
        pre = bdot(h1b, up_ref[:, at : at + step]) + bias_ref[8:9, first + at : first + at + step]
        value, slope = gelu_pair(pre)
        active_ref[:, at : at + step] = value.astype(BF16)
        slope_ref[:, at : at + step] = slope


def mlp_first_kernel(meta_ref, h1b_ref, b0, b1, u0, u1, d0, d1, a0, a1, s0, s1, low_ref, w_ref, sems):
    fetch = Fetch(meta_ref, sems)
    copies = [fetch.one(ref, w_ref.at[n]) for n, ref in enumerate((u0, d0, u1, d1))]
    h1b = h1b_ref[...]
    copies[0].wait()
    mlp_one(h1b, w_ref.at[0], b0, a0, s0)
    copies[1].wait()
    low_ref[...] = bdot(a0[...], w_ref[1])
    copies[2].wait()
    mlp_one(h1b, w_ref.at[2], b1, a1, s1)
    copies[3].wait()
    low_ref[...] += bdot(a1[...], w_ref[3])


def mlp_second_kernel(
    meta_ref, h1b_ref, b2, b3, low_ref, normed1_ref, vec_ref, u2a, u2b, u3a, u3b, d2a, d2b, d3a, d3b,
    a2, a3, s2, s3, normed2_ref, inverse2_ref, h2b_ref, w_ref, sems,
):
    fetch = Fetch(meta_ref, sems)
    pieces = ((u2a, u2b), (d2a, d2b), (u3a, u3b), (d3a, d3b))
    copies = [fetch.block(piece, w_ref.at[n]) for n, piece in enumerate(pieces)]
    h1b = h1b_ref[...]
    wait(copies[0])
    mlp_one(h1b, w_ref.at[0], b2, a2, s2)
    wait(copies[1])
    normed2_ref[...] = low_ref[...] + bdot(a2[...], w_ref[1])
    wait(copies[2])
    mlp_one(h1b, w_ref.at[2], b3, a3, s3)
    wait(copies[3])
    total = normed2_ref[...] + bdot(a3[...], w_ref[3]) + vec_ref[5:6, :]
    normed, inverse = normalize(normed1_ref[...] * vec_ref[3:4, :] + vec_ref[4:5, :] + total)
    normed2_ref[...] = normed
    inverse2_ref[...] = inverse
    h2b_ref[...] = (normed * vec_ref[6:7, :] + vec_ref[7:8, :]).astype(BF16)


def head_kernel(
    own, vocab, meta_ref, live_ref, count_ref, ids_ref, slots_ref, bias_ref, vec_ref,
    h2b_ref, normed2_ref, inverse2_ref, t0, t1, t2a, t2b, t3a, t3b,
    dz_ref, dzb_ref, loss_ref, gbias_ref, gvec_ref, send_ref, keep_ref,
    table_ref, full_ref, grad_ref, sems,
):
    images, length = ids_ref.shape
    slot_count = slots_ref.shape[1]
    total = bias_ref.shape[1]
    member = meta_ref[0]
    columns = t0.shape[0]
    fetch = Fetch(meta_ref, sems)
    copies = []
    for k, pieces in enumerate(((t0,), (t1,), (t2a, t2b), (t3a, t3b))):
        copies += fetch.block(pieces, table_ref, pl.multiple_of((member ^ k) * columns, 64))
    slots_t = jnp.transpose(slots_ref[...].astype(F32))
    image_lane = lax.broadcasted_iota(jnp.int32, (slot_count, images), 1)
    slot_row = lax.broadcasted_iota(jnp.int32, (slot_count, 1), 0)
    position = lax.broadcasted_iota(jnp.int32, (1, length), 1).astype(F32)
    picks, targets, weights, picked = [], [], [], []
    for i in range(own):
        image = member * own + i
        at = jnp.sum(jnp.where(image_lane == image, slots_t, 0.0), 1, keepdims=True)
        hit = at == position
        ids = ids_ref[pl.ds(image, 1), :].astype(F32)
        targets.append(jnp.sum(jnp.where(hit, ids, 0.0), 1, keepdims=True).astype(jnp.int32))
        weights.append(jnp.where(slot_row < live_ref[image], 1.0, 0.0))
        picks.append(jnp.where(hit, 1.0, 0.0).astype(BF16))
        picked.append(bdot(picks[i], h2b_ref[i * length : (i + 1) * length, :]).astype(BF16))
    target = jnp.concatenate(targets, 0)
    weight = jnp.concatenate(weights, 0)
    rows = jnp.concatenate(picked, 0)
    wait(copies)
    lane = lax.broadcasted_iota(jnp.int32, (1, total), 1)
    logits = bdot(rows, table_ref[...]) + bias_ref[...]
    logits = jnp.where(lane < vocab, logits, -1e30)
    top = jnp.max(logits, -1, keepdims=True)
    log_total = top + jnp.log(jnp.sum(jnp.exp(logits - top), -1, keepdims=True))
    hot = jnp.where(lane == target, 1.0, 0.0)
    chosen = jnp.sum(hot * logits, -1, keepdims=True)
    loss_ref[...] = jnp.broadcast_to(jnp.sum(weight * (log_total - chosen), 0, keepdims=True), loss_ref.shape)
    d_logits = (jnp.exp(logits - log_total) - hot) * (weight / count_ref[0])
    gbias_ref[...] = jnp.sum(d_logits, 0, keepdims=True)
    dl = d_logits.astype(BF16)
    d_rows = ndot(dl, table_ref[...])
    high = d_rows.astype(BF16)
    rest = (d_rows - high.astype(F32)).astype(BF16)
    for i in range(own):
        part = slice(i * slot_count, (i + 1) * slot_count)
        grad_ref[i * length : (i + 1) * length, :] = tdot(picks[i], high[part]) + tdot(picks[i], rest[part])
    d_z2, d_gain, d_shift = norm_back(normed2_ref[...], inverse2_ref[...], vec_ref[6:7, :], grad_ref[...])
    dz_ref[...] = d_z2
    dzb_ref[...] = d_z2.astype(BF16)
    gvec_ref[0:1, :] = jnp.sum(d_z2, 0, keepdims=True)
    gvec_ref[1:2, :] = d_gain
    gvec_ref[2:3, :] = d_shift
    full_ref[...] = tdot(rows, dl).astype(BF16)
    for k, out in enumerate((keep_ref.at[0], send_ref.at[0], keep_ref.at[1], send_ref.at[1])):
        out[...] = full_ref[pl.ds(pl.multiple_of((member ^ k) * columns, 64), columns), :]


def down_send_kernel(dzb_ref, a1, a3, s1, s3, send_ref, left_ref):
    first = dzb_ref.shape[1]
    dzb = dzb_ref[...]
    for n, (active, start) in enumerate(((a1[...], s1), (a3[...], s3))):
        send_ref[n] = tdot(active, dzb).astype(BF16)
        left_ref[n] = panel(start[:8, first : 2 * first], dzb, active)


def close(n, grad, near_ref, err_ref, far_refs, part_ref):
    if n == 0:
        part_ref[...] = grad + near_ref[0].astype(F32) + err_ref[...]
    else:
        total = (grad + near_ref[1].astype(F32)).astype(BF16)
        size = total.shape[0] // len(far_refs)
        for place, far_ref in enumerate(far_refs):
            far_ref[...] = total[place * size : (place + 1) * size]


def down_keep_kernel(dzb_ref, a0, a2, s0, s2, near_ref, err_ref, far_a, far_b, part_ref, left_ref):
    first = dzb_ref.shape[1]
    dzb = dzb_ref[...]
    for n, (active, start) in ((1, (a2[...], s2)), (0, (a0[...], s0))):
        close(n, tdot(active, dzb), near_ref, err_ref, (far_a, far_b), part_ref)
        left_ref[n] = panel(start[:8, first : 2 * first], dzb, active)
    left_ref[0] += wide(ndot, s0[:8, first : 2 * first], err_ref[...])


def up_one(dzb, h1b, slope, up, down, start, hidden_ref, dpre_ref):
    step = 256
    for at in range(0, down.shape[0], step):
        d_pre = ndot(dzb, down[at : at + step, :]) * slope[:, at : at + step]
        hidden_ref[:, at : at + step] = jnp.sum(d_pre, 0, keepdims=True)
        dpre_ref[:, at : at + step] = d_pre.astype(BF16)
    d_pre = dpre_ref[...]
    return tdot(h1b, d_pre), ndot(d_pre, up[...]), panel(start[:8, : d_pre.shape[1]], d_pre, h1b)


def up_send_kernel(
    meta_ref, dzb_ref, h1b_ref, p1, p3, s1, s3, u1, u3a, u3b, d1, d3a, d3b,
    send_ref, left_ref, dh_ref, hidden_ref, dpre_ref, w_ref, sems,
):
    fetch = Fetch(meta_ref, sems)
    pieces = ((d1,), (u1,), (d3a, d3b), (u3a, u3b))
    copies = [fetch.block(piece, w_ref.at[n]) for n, piece in enumerate(pieces)]
    dzb, h1b = dzb_ref[...], h1b_ref[...]
    for n, (slope, start) in enumerate(((p1, s1), (p3, s3))):
        wait(copies[2 * n] + copies[2 * n + 1])
        grad, part, left_ref[n] = up_one(
            dzb, h1b, slope, w_ref.at[2 * n + 1], w_ref.at[2 * n], start, hidden_ref.at[n], dpre_ref
        )
        send_ref[n] = grad.astype(BF16)
        dh_ref[...] = part if n == 0 else dh_ref[...] + part


def up_keep_kernel(
    meta_ref, dz_ref, dzb_ref, h1b_ref, normed1_ref, inverse1_ref, vec_ref, dh_ref, p0, p2, s0, s2,
    near_ref, err_ref, u0, u2a, u2b, d0, d2a, d2b,
    far_ref, part_ref, left_ref, dz1_ref, dz1b_ref, gvec_ref, hidden_ref, dpre_ref, w_ref, sems,
):
    fetch = Fetch(meta_ref, sems)
    pieces = ((d0,), (u0,), (d2a, d2b), (u2a, u2b))
    copies = [fetch.block(piece, w_ref.at[n]) for n, piece in enumerate(pieces)]
    dzb, h1b = dzb_ref[...], h1b_ref[...]
    for n, (slope, start) in ((1, (p2, s2)), (0, (p0, s0))):
        wait(copies[2 * n] + copies[2 * n + 1])
        grad, part, left_ref[n] = up_one(
            dzb, h1b, slope, w_ref.at[2 * n + 1], w_ref.at[2 * n], start, hidden_ref.at[n], dpre_ref
        )
        close(n, grad, near_ref, err_ref, (far_ref,), part_ref)
        dz1_ref[...] = part + (dz_ref[...] + dh_ref[...] if n == 1 else dz1_ref[...])
    left_ref[0] += wide(ndot, s0[:8, : err_ref.shape[1]], err_ref[...])
    d_z1, d_gain, d_shift = norm_back(normed1_ref[...], inverse1_ref[...], vec_ref[3:4, :], dz1_ref[...])
    dz1_ref[...] = d_z1
    dz1b_ref[...] = d_z1.astype(BF16)
    gvec_ref[0:1, :] = jnp.sum(d_z1, 0, keepdims=True)
    gvec_ref[1:2, :] = d_gain
    gvec_ref[2:3, :] = d_shift


def attention_back_one(length, dz, hb, w_ref, qkv_ref, lse_ref, ctx_ref, start_ref, pack_ref, dm_ref, dc_ref):
    width, features = ctx_ref.shape[1], dz.shape[1]
    used = 3 * width
    dc_ref[...] = ndot(dz, w_ref[used:, :]).astype(BF16)
    ctx = ctx_ref[...]
    out_grad = tdot(ctx, dz)
    pack_ref[:8, 3 * features :] = panel(start_ref[:8, 2 * features : 3 * features], dz, ctx)
    q_sum = jnp.zeros((1, width), F32)
    v_sum = jnp.zeros((1, width), F32)
    for image in range(dz.shape[0] // length):
        rows = slice(image * length, (image + 1) * length)
        q, k, v, dc = qkv_ref[0, rows, :], qkv_ref[1, rows, :], qkv_ref[2, rows, :], dc_ref[rows, :]
        d_query = jnp.zeros((length, width), F32)
        d_key = jnp.zeros((length, width), F32)
        d_value = jnp.zeros((length, width), F32)
        for head in range(width // HD):
            mask = head_mask(width, head)
            q_head, k_head, c_head = q * mask, k * mask, dc * mask
            probs = jnp.exp(ndot(q_head, k) - lse_ref[rows, head : head + 1])
            d_value = d_value + tdot(probs.astype(BF16), c_head)
            d_probs = ndot(c_head, v)
            inner = jnp.sum(d_probs * probs, -1, keepdims=True)
            d_scores = (probs * (d_probs - inner)).astype(BF16)
            d_query = d_query + bdot(d_scores, k_head)
            d_key = d_key + tdot(d_scores, q_head)
        d_query = d_query * HD ** (-0.5)
        q_sum = q_sum + jnp.sum(d_query, 0, keepdims=True)
        v_sum = v_sum + jnp.sum(d_value, 0, keepdims=True)
        dm_ref[rows, :width] = d_query.astype(BF16)
        dm_ref[rows, width : 2 * width] = d_key.astype(BF16)
        dm_ref[rows, 2 * width :] = d_value.astype(BF16)
    pack_ref[8:9, :width] = q_sum
    pack_ref[8:9, width : 2 * width] = v_sum
    dm = dm_ref[...]
    pack_ref[:8, 2 * features : 3 * features] = panel(start_ref[:8, 3 * features :], dm, hb)
    return tdot(dm, hb), out_grad, bdot(dm, w_ref[:used, :])


def pack_rows(pack_ref, width, up, down, hidden):
    features = up.shape[1]
    pack_ref[...] = jnp.zeros_like(pack_ref)
    pack_ref[:8, :features] = up
    pack_ref[:8, features : 2 * features] = down
    pack_ref[8:9, 2 * width : 2 * width + features] = hidden


def pack_whole(pack_ref, vectors, bias, loss):
    pack_ref[9:10, : bias.shape[1]] = bias
    features = vectors[0].shape[1]
    for n, vector in enumerate(vectors + [loss]):
        row, place = 10 + n // 3, n % 3
        pack_ref[row : row + 1, place * features : place * features + vector.shape[1]] = vector


def attention_send_kernel(
    length, meta_ref, dz1b_ref, hb_ref, q1, q3, l1, l3, x1, x3, s1, s3, up_ref, down_ref, hidden_ref,
    c1, c3a, c3b, send_ref, pack_ref, dh_ref, dm_ref, dc_ref, w_ref, sems,
):
    fetch = Fetch(meta_ref, sems)
    copies = [fetch.block((c1,), w_ref.at[0]), fetch.block((c3a, c3b), w_ref.at[1])]
    dz, hb = dz1b_ref[...], hb_ref[...]
    used = dm_ref.shape[1]
    for n, (q, l, x, start) in enumerate(((q1, l1, x1, s1), (q3, l3, x3, s3))):
        wait(copies[n])
        pack_rows(pack_ref.at[n], x.shape[1], up_ref[n], down_ref[n], hidden_ref[n])
        qkv_grad, out_grad, part = attention_back_one(
            length, dz, hb, w_ref.at[n], q, l, x, start, pack_ref.at[n], dm_ref, dc_ref
        )
        send_ref[n, :used, :] = qkv_grad.astype(BF16)
        send_ref[n, used:, :] = out_grad.astype(BF16)
        dh_ref[...] = part if n == 0 else dh_ref[...] + part


def attention_keep_kernel(
    length, meta_ref, dz1b_ref, hb_ref, q0, q2, l0, l2, x0, x2, s0, s2, up_ref, down_ref, hidden_ref,
    near_ref, err_qkv, err_out, dz1_ref, dha_ref, normed_ref, inverse_ref, vec_ref, gvec1_ref, gvec2_ref, gbias_ref,
    loss_ref, send_pack_ref, c0, c2a, c2b,
    far_ref, part_ref, pack_ref, send_ref, d_far, d_near, d_own, dm_ref, dc_ref, dh_ref, w_ref, sems,
):
    fetch = Fetch(meta_ref, sems)
    copies = [fetch.block((c0,), w_ref.at[0]), fetch.block((c2a, c2b), w_ref.at[1])]
    dz, hb = dz1b_ref[...], hb_ref[...]
    used, width = dm_ref.shape[1], x0.shape[1]
    features = hb.shape[1]
    for n, (q, l, x, start) in ((1, (q2, l2, x2, s2)), (0, (q0, l0, x0, s0))):
        wait(copies[n])
        pack_rows(pack_ref.at[n], width, up_ref[n], down_ref[n], hidden_ref[n])
        qkv_grad, out_grad, part = attention_back_one(
            length, dz, hb, w_ref.at[n], q, l, x, start, pack_ref.at[n], dm_ref, dc_ref
        )
        if n == 0:
            part_ref[:used, :] = qkv_grad + near_ref[0, :used, :].astype(F32) + err_qkv[...]
            part_ref[used:, :] = out_grad + near_ref[0, used:, :].astype(F32) + err_out[...]
        else:
            far_ref[:used, :] = (qkv_grad + near_ref[1, :used, :].astype(F32)).astype(BF16)
            far_ref[used:, :] = (out_grad + near_ref[1, used:, :].astype(F32)).astype(BF16)
        dh_ref[...] = part + (dha_ref[...] + dz1_ref[...] if n == 1 else dh_ref[...])
    pack_ref[0, :8, 2 * features : 3 * features] += wide(bdot, s0[:8, 3 * features :], err_qkv[...])
    pack_ref[0, :8, 3 * features :] += wide(ndot, s0[:8, 2 * features : 3 * features], err_out[...])
    d_x, d_gain, d_shift = norm_back(normed_ref[...], inverse_ref[...], vec_ref[0:1, :], dh_ref[...])
    vectors = [d_gain, d_shift] + [gvec1_ref[i : i + 1, :] for i in range(3)] + [gvec2_ref[i : i + 1, :] for i in range(3)]
    send_ref[...] = send_pack_ref[...]
    for ref in (send_ref.at[0], send_ref.at[1], pack_ref.at[0], pack_ref.at[1]):
        pack_whole(ref, vectors, gbias_ref[...], loss_ref[...])
    dh_ref[...] = d_x
    rows, columns = d_own.shape
    for t in range(4):

        @pl.when(meta_ref[0] == t)
        def _():
            for k, out in enumerate((d_own, d_near, d_far.at[0], d_far.at[1])):
                out[...] = dh_ref[:, (t ^ k) * columns : ((t ^ k) + 1) * columns].astype(BF16)


def scatter_kernel(own, vocab, ids_ref, r0, r1, r2, r3, near_ref, keep_ref, far_ref, out_ref):
    length = ids_ref.shape[0]
    total = out_ref.shape[1]
    lane = lax.broadcasted_iota(jnp.int32, (1, total), 1)
    position = lax.broadcasted_iota(jnp.int32, (length, 1), 0) + vocab
    result = keep_ref[0].astype(F32) + near_ref[0].astype(F32) + far_ref[...].astype(F32)
    for k, rows in enumerate((r0[...], r1[...], r2[0], r3[1])):
        hots = []
        for i in range(own):
            ids = ids_ref[:, k * own + i : k * own + i + 1]
            hots.append(jnp.where((ids == lane) | (position == lane), 1.0, 0.0).astype(BF16))
        result = result + tdot(rows, jnp.concatenate(hots, 0))
    out_ref[...] = result.astype(out_ref.dtype)


def right_mlp_kernel(part_d, got_a, got_b, part_u, got_u, base_ref, rest_ref, out_ref):
    size = part_d.shape[1]
    rows = part_d.shape[0]
    merged = part_u[...] + got_u[...].astype(F32)
    out_ref[:, :size] = wide(bdot, base_ref[:, :rows], merged)
    merged = part_d[...] + jnp.concatenate([got_a[...].astype(F32), got_b[...].astype(F32)], 0)
    out_ref[:, size : 2 * size] = wide(bdot, base_ref[:, rows : 2 * rows], merged)
    out_ref[:, 2 * size :] = rest_ref[...]


def right_attention_kernel(used, part, got, base_ref, out_ref):
    features = part.shape[1]
    out_ref[:, :features] = wide(bdot, base_ref[:, 3 * features :], part[used:, :] + got[used:, :].astype(F32))
    merged = part[:used, :] + got[:used, :].astype(F32)
    out_ref[:, features:] = wide(ndot, base_ref[:, 2 * features : 3 * features], merged)


def update_kernel(replicas, part, weight, moment, first_ref, second_ref, *refs):
    gots, (weight_new, moment_new, error_new) = refs[:-3], refs[-3:]
    first, second = split3(first_ref[...] * (1.0 / replicas)), split3(second_ref[...])
    rank = first.shape[0] // 3
    parts = lambda x, order: jnp.concatenate([x[i * rank : (i + 1) * rank].astype(F32) for i in order], 0).astype(BF16)
    approx = tdot(parts(first, (0, 0, 1, 0, 2, 1)), parts(second, (0, 1, 0, 2, 0, 1)))
    new = BETA * moment[...] + approx
    moment_new[...] = new
    weight_new[...] = weight[...].astype(F32) - RATE_MAT * new
    got = [got[...].astype(F32) for got in gots]
    error_new[...] = part[...] + (got[0] if len(got) == 1 else jnp.concatenate(got, 0)) - approx


def update(replicas, part, gots, first_row, weight, moment, first, second):
    rows, cols = weight.shape
    block = 256
    spec = pl.BlockSpec((rows, block), lambda i: (0, i))
    out = shape(rows, cols)
    mine = lambda size: pl.BlockSpec((size, block), lambda i: (first_row // size, i))
    return call(
        functools.partial(update_kernel, replicas), "update", (out, out, out),
        (part, weight, moment, first, second, *gots),
        [mine(rows), spec, spec, pl.BlockSpec(first.shape, lambda i: (0, 0)),
         pl.BlockSpec((second.shape[0], block), lambda i: (0, i))] + [mine(rows // len(gots))] * len(gots),
        out_specs=[spec] * 3, grid=(cols // block,),
    )


def orthonormal_kernel(sizes, panel_ref, out_ref):
    rank = panel_ref.shape[0]
    place = lax.broadcasted_iota(jnp.int32, (rank, 1), 0)
    cuts = [sum(sizes[:i]) for i in range(len(sizes) + 1)]
    panels = [panel_ref[:, a:b] for a, b in zip(cuts, cuts[1:])]
    for number in range(rank):
        for which, (a, b) in enumerate(zip(cuts, cuts[1:])):
            part = panels[which]
            column = part[number : number + 1, :]
            column = column * lax.rsqrt(jnp.sum(column * column, -1, keepdims=True) + 1e-20)
            out_ref[number : number + 1, a:b] = column
            if number + 1 < rank:
                along = jnp.sum(part * column, -1, keepdims=True)
                panels[which] = part - jnp.where(place > number, along, 0.0) * column


def reduce_rows(x, bits, low):
    place = lax.axis_index("dp")
    for bit in bits[:2]:
        half = x.shape[0] // 2
        upper = (place & bit) != 0
        got = across(jnp.where(upper, x[:half], x[half:]), "dp", bit)
        x = (jnp.where(upper, x[half:], x[:half]).astype(F32) + got.astype(F32)).astype(BF16)
    for bit in bits[2:]:
        x = (x.astype(F32) + across(x, "dp", bit).astype(F32)).astype(BF16)
    for bit in reversed(bits[:2]):
        got = across(x, "dp", bit)
        upper = (place & bit) != 0
        x = jnp.concatenate([jnp.where(upper, got, x), jnp.where(upper, x, got)], 0)
    return x


def shards(
    token_ids, masked_at, live_counts, tables, table_mom, vec_whole, vec_mom, vec_split, split_mom,
    head_bias, bias_mom, w_qkv, w_out, w_up, w_down, mom_qkv, mom_out, mom_up, mom_down,
    err_qkv, err_out, err_up, err_down, start_qkv, start_out, start_up, start_down,
):
    groups = lax.axis_size("tensor")
    replicas = lax.axis_size("dp")
    images, length = token_ids.shape
    vocab = head_bias.shape[0]
    total_rows, columns = tables.shape
    features = w_qkv.shape[0]
    width = w_qkv.shape[1] // 3
    hidden = w_up.shape[1]
    own = images // groups
    rows = own * length
    rank = start_qkv.shape[1]
    total = total_rows + -total_rows % 128
    used = 3 * width
    all_rows = used + width
    meta = jnp.stack([lax.axis_index("tensor"), lax.axis_index("dp") & 1]).astype(jnp.int32)

    bf = functools.partial(shape, dtype=BF16)
    dma = lambda n: pltpu.SemaphoreType.DMA((n,))
    vm = lambda *dims: pltpu.VMEM(dims, BF16)
    first_own, first_half, up_half, down_half, table_own, table_half = call(
        pack_kernel, "pack",
        (bf(all_rows, features), bf(all_rows // 2, features), bf(features // 2, hidden), bf(hidden // 2, features),
         bf(columns, total), bf(columns // 2, total)),
        (meta, w_qkv.T, w_out, w_up, w_down, tables.T), [SMEM] + [ANY] * 4 + [VMEM], [dma(4)],
    )
    part = bf(rows + length, columns)
    e_far, e_near, e_own, ids_rows = call(
        functools.partial(embed_kernel, own, vocab), "embed",
        (bf(2, rows + length // 2, columns), part, part, shape(length, images, dtype=jnp.int32)),
        (meta, live_counts, token_ids, masked_at, table_own), [SMEM, SMEM, VMEM, VMEM, VMEM],
    )
    def cores(pieces):
        return tuple(core_swap(piece) for piece in pieces)

    def sums(value, steps):
        for bit in steps:
            value = value + across(value, "dp", bit)
        return value

    first_near, up_near, down_near, table_near = cores((first_own, w_up, w_down, table_own))
    own_starts = jnp.concatenate((start_up.T, start_down.T, start_out.T, start_qkv.T), 1)
    bias_row = jnp.pad(vec_split, ((0, 7), (0, own_starts.shape[1] - vec_split.shape[1])))
    small = [jnp.concatenate([own_starts, bias_row], 0)]
    small.append(core_swap(small[0]))
    bits = [1 << i for i in range(replicas.bit_length() - 1)]
    count = jnp.sum(live_counts).astype(F32).reshape(1, 1)

    first_far = [chip_swap(first_half)]
    e_two = chip_swap(e_far)
    e_one = core_swap(e_near)
    small.append(chip_swap(tie(small[0], first_far[0])))
    e_three = core_swap(tie(e_two, first_far[0]))
    first_far.append(across(first_far[0], "dp", 1))
    up_far = [chip_swap(tie(up_half, e_two))]
    count = sums(tie(count, e_two), bits[:1])
    starts = splits = small

    state = (shape(rows, features), shape(rows, 1), bf(rows, features))
    block = (bf(3, rows, width), shape(rows, width // HD), bf(rows, width))
    res = call(
        functools.partial(attention_first_kernel, length), "attention_first", state + block + block,
        (tie(meta, up_near, down_near, first_near, table_near), e_own, e_one, e_two, e_three, vec_whole,
         small[0], small[1], first_own, first_near),
        [SMEM] + [VMEM] * 7 + [ANY] * 2, [pltpu.VMEM((rows, features), F32), vm(2, used, features), dma(2)],
    )
    normed0, inverse0, h0b = res[:3]
    kept = [res[3:6], res[6:9]]
    first_both = cores([tie(x, h0b, up_far[0], count) for x in first_far])
    small.append(core_swap(tie(small[2], h0b, up_far[0])))
    down_far = [chip_swap(tie(down_half, up_far[0]))]
    up_far.append(across(up_far[0], "dp", 1))
    count = sums(tie(count, h0b), bits[1:2])
    res = call(
        functools.partial(attention_second_kernel, length), "attention_second", state + block + block,
        (meta, normed0, h0b, vec_whole, splits[2], splits[3], kept[0][2], kept[1][2], first_own, first_near,
         *first_far, *first_both),
        [SMEM] + [VMEM] * 7 + [ANY] * 6, [vm(2, all_rows, features), vm(2, width, features), dma(6)],
    )
    normed1, inverse1, h1b = res[:3]
    kept += [res[3:6], res[6:9]]
    up_both = cores([tie(x, h1b, down_far[0], up_far[1], count) for x in up_far])
    table_far = [chip_swap(tie(table_half, down_far[0]))]
    down_far.append(across(down_far[0], "dp", 1))
    count = sums(tie(count, h1b), bits[2:])
    act = bf(rows, hidden)
    slope = shape(rows, hidden)
    a0, a1, p0, p1, low = call(
        mlp_first_kernel, "mlp_first", (act, act, slope, slope, shape(rows, features)),
        (tie(meta, up_both[0]), h1b, splits[0], splits[1], w_up, up_near, w_down, down_near),
        [SMEM] + [VMEM] * 3 + [ANY] * 4, [vm(4, features, hidden), dma(4)],
    )
    down_both = cores([tie(x, low, table_far[0], down_far[1], count) for x in down_far])
    table_far.append(across(table_far[0], "dp", 1))
    a2, a3, p2, p3, normed2, inverse2, h2b = call(
        mlp_second_kernel, "mlp_second", (act, act, slope, slope) + state,
        (meta, h1b, splits[2], splits[3], low, normed1, vec_whole, *up_far, *up_both, *down_far, *down_both),
        [SMEM] + [VMEM] * 6 + [ANY] * 8, [vm(4, features, hidden), dma(8)],
    )
    table_both = cores([tie(x, h2b, table_far[1]) for x in table_far])
    count = count.reshape(1)
    pair = lambda a, b, dtype: shape(2, a, b, dtype=dtype)
    dz2, dz2b, loss_part, g_bias, g_vec2, head_send, head_keep = call(
        functools.partial(head_kernel, own, vocab), "head",
        (
            shape(rows, features), bf(rows, features), shape(1, 128), shape(1, total),
            shape(3, features), pair(columns, total, BF16), pair(columns, total, BF16),
        ),
        (
            meta, live_counts, count, token_ids, masked_at,
            jnp.pad(head_bias, (0, total - vocab)).reshape(1, total), vec_whole, h2b, normed2, inverse2,
            table_own, table_near, *table_far, *table_both,
        ),
        [SMEM] * 3 + [VMEM] * 7 + [ANY] * 6,
        [vm(features, total), vm(features, total), pltpu.VMEM((rows, features), F32), dma(6)],
    )

    head_near = core_swap(head_send)
    left = shape(2, rank, features)
    down_send, left_down_a = call(
        down_send_kernel, "down_send", (pair(hidden, features, BF16), left),
        (dz2b, a1, a3, starts[1], starts[3]),
    )
    down_got = core_swap(down_send)
    head_far = (head_keep[1].astype(F32) + head_near[1].astype(F32)).astype(BF16)
    head_in = chip_swap(head_far)
    up_send, left_up_a, dh_a, hidden_a = call(
        up_send_kernel, "up_send",
        (pair(features, hidden, BF16), left, shape(rows, features), shape(2, 1, hidden)),
        (meta, tie(dz2b, head_far, down_send), h1b, p1, p3, starts[1], starts[3], up_near, *up_both, down_near, *down_both),
        [SMEM] + [VMEM] * 6 + [ANY] * 6, [vm(rows, hidden), vm(4, features, hidden), dma(6)],
    )
    up_got = core_swap(up_send)
    down_a, down_b, down_part, left_down_b = call(
        down_keep_kernel, "down_keep",
        (bf(hidden // 2, features), bf(hidden // 2, features), shape(hidden, features), left),
        (tie(dz2b, dh_a), a0, a2, starts[0], starts[2], down_got, err_down[0]),
    )
    up_far_grad, up_part, left_up_b, dz1, dz1b, g_vec1, hidden_b = call(
        up_keep_kernel, "up_keep",
        (bf(features, hidden), shape(features, hidden), left, shape(rows, features), bf(rows, features),
         shape(3, features), shape(2, 1, hidden)),
        (meta, dz2, tie(dz2b, down_a), h1b, normed1, inverse1, vec_whole, dh_a, p0, p2, starts[0], starts[2],
         up_got, err_up[0], w_up, *up_far, w_down, *down_far),
        [SMEM] + [VMEM] * 13 + [ANY] * 6, [vm(rows, hidden), vm(4, features, hidden), dma(6)],
    )
    down_in_a = chip_swap(tie(down_a, head_in))
    down_in_b = chip_swap(tie(down_b, down_in_a))
    pack_width = 3 * features + width
    pack = shape(2, 16, pack_width)
    scratch = [vm(rows, used), vm(rows, width)]
    first_send, pack_a, dh_b = call(
        functools.partial(attention_send_kernel, length), "attention_send",
        (pair(all_rows, features, BF16), pack, shape(rows, features)),
        (meta, tie(dz1b, head_in), h0b, kept[1][0], kept[3][0], kept[1][1], kept[3][1], kept[1][2], kept[3][2],
         starts[1], starts[3], left_up_a, left_down_a, hidden_a, first_near, *first_both),
        [SMEM] + [VMEM] * 13 + [ANY] * 3, scratch + [vm(2, all_rows, features), dma(3)],
    )
    first_got = core_swap(tie(first_send, down_in_a))
    cols = bf(rows, columns)
    first_far_grad, first_part, pack_b, pack_a, d_far, d_near, d_own = call(
        functools.partial(attention_keep_kernel, length), "attention_keep",
        (bf(all_rows, features), shape(all_rows, features), pack, pack, pair(rows, columns, BF16), cols, cols),
        (meta, tie(dz1b, dh_b), h0b, kept[0][0], kept[2][0], kept[0][1], kept[2][1], kept[0][2], kept[2][2],
         starts[0], starts[2], left_up_b, left_down_b, hidden_b, first_got, err_qkv[0].T, err_out[0],
         dz1, dh_b, normed0, inverse0, vec_whole, g_vec1, g_vec2, g_bias, loss_part, pack_a,
         first_own, *first_far),
        [SMEM] + [VMEM] * 26 + [ANY] * 3,
        scratch + [pltpu.VMEM((rows, features), F32), vm(2, all_rows, features), dma(3)],
    )

    d_two = chip_swap(tie(d_far, down_in_b))
    d_one = core_swap(tie(d_near, down_in_b))
    d_three = core_swap(d_two)
    mine = pack_b + core_swap(tie(pack_a, down_in_b))
    up_in = chip_swap(tie(up_far_grad, d_two))
    first_in = chip_swap(tie(first_far_grad, up_in))
    mine = mine[0] + chip_swap(mine[1])
    panels = dp_sum(mine[:8])
    table_grad = call(
        functools.partial(scatter_kernel, own, vocab), "scatter", bf(columns, total),
        (ids_rows, d_own, d_one, d_two, d_three, head_near, head_keep, head_in),
    )
    order = ([bits[1], bits[0]] + bits[2:], bits)
    cut = columns // 2
    table_parts = [reduce_rows(table_grad[:cut], order[0], 0), reduce_rows(table_grad[cut:], order[1], 1)]
    sizes = (features, features, features, width)
    bases = call(
        functools.partial(orthonormal_kernel, sizes), "orthonormal", shape(rank, pack_width), (panels,),
    )
    packed = call(
        right_mlp_kernel, "right_mlp", shape(rank, 2 * features + pack_width),
        (down_part, down_in_a, down_in_b, up_part, up_in, bases, mine[8:]),
    )
    packed = dp_sum(packed)
    right_up, right_down = packed[:, :features], packed[:, features : 2 * features]
    rest = packed[:, 2 * features :]
    base_up, base_down = bases[:, :features], bases[:, features : 2 * features]
    base_qkv, base_out = bases[:, 2 * features : 3 * features], bases[:, 3 * features :]
    down = update(replicas, down_part, (down_in_a, down_in_b), 0, w_down, mom_down, base_down, right_down)
    up = update(replicas, up_part, (up_in,), 0, w_up, mom_up, base_up, right_up)
    rights = call(
        functools.partial(right_attention_kernel, used), "right_attention", shape(rank, features + used),
        (tie(first_part, up[0], down[0]), first_in, bases),
    )
    rights = dp_sum(rights)
    right_out, right_qkv = rights[:, :features], rights[:, features:]
    out = update(replicas, first_part, (first_in,), used, w_out, mom_out, base_out, right_out)
    qkv = update(replicas, first_part, (first_in,), 0, w_qkv.T, mom_qkv.T, right_qkv, base_qkv)

    table_grad = jnp.concatenate(table_parts, 0)[:, :total_rows].astype(F32)
    vectors = [rest[2 + n // 3, n % 3 * features : (n % 3 + 1) * features] for n in range(8)]
    results = [jnp.stack([rest[4, 2 * features], count[0]])]

    def momentum_step(weight, moment, grad, rate):
        new_moment = BETA * moment + grad
        return (weight.astype(F32) - rate * new_moment, new_moment)

    new = momentum_step(tables.T, table_mom.T, table_grad, RATE_TAB)
    results += [new[0].T, new[1].T]
    results += momentum_step(vec_whole, vec_mom, jnp.stack(vectors), RATE_VEC)
    results += momentum_step(vec_split, split_mom, rest[0:1, : vec_split.shape[1]], RATE_VEC)
    results += momentum_step(head_bias, bias_mom, rest[1, :vocab], RATE_VEC)
    one = 1.0 / replicas
    for (weight, moment, error), base, right, flip in (
        (qkv, base_qkv, right_qkv, True), (out, base_out, right_out, False),
        (up, base_up, right_up, False), (down, base_down, right_down, False),
    ):
        if flip:
            weight, moment, error = weight.T, moment.T, error.T
        results += [weight, moment, error[None], base.T[None], right.T * one]
    return tuple(results)


def solution(mesh):
    rows, cols = P("tensor", None), P(None, "tensor")
    batch = P("dp", None)
    in_specs = (
        batch, batch, P("dp"), cols, cols, P(), P(), rows, rows, P(), P(),
        cols, rows, cols, rows, cols, rows, cols, rows,
        P("dp", None, "tensor"), P("dp", "tensor", None), P("dp", None, "tensor"), P("dp", "tensor", None),
        rows, rows, rows, rows,
    )
    left = P("tensor", None, None)
    out_specs = (P(), cols, cols, P(), P(), rows, rows, P(), P())
    for side in (cols, rows, cols, rows):
        out_specs += (side, side, P("dp", *side), left, rows)
    return jax.shard_map(shards, mesh=mesh, in_specs=in_specs, out_specs=out_specs, check_vma=False)
```

```python
import functools

import jax
import jax.numpy as jnp
from jax import lax
from jax.experimental import pallas as pl
from jax.experimental.pallas import tpu as pltpu
from jax.sharding import PartitionSpec as P

HD = 48
EPSILON = 1e-05
BETA = 0.9
RATE_MAT = 100.0
RATE_VEC = 10.0
RATE_TAB = 100.0
HIGHEST = lax.Precision.HIGHEST
BF16 = jnp.bfloat16
F32 = jnp.float32
MIB = 1024 * 1024


def bdot(left, right):
    return jnp.dot(left, right, preferred_element_type=F32)


def tdot(left, right):
    return lax.dot_general(left, right, (((0,), (0,)), ((), ())), preferred_element_type=F32)


def ndot(left, right):
    return lax.dot_general(left, right, (((1,), (1,)), ((), ())), preferred_element_type=F32)


def across(x, axis, bit):
    size = lax.axis_size(axis)
    return lax.ppermute(x, axis, [(i, i ^ bit) for i in range(size)])


def core_swap(x):
    return across(x, "tensor", 1)


def chip_swap(x):
    return across(x, "tensor", 2)


def tie(x, *others):
    return lax.optimization_barrier((x,) + others)[0]


def head_mask(width, head):
    lane = lax.broadcasted_iota(jnp.int32, (1, width), 1)
    return ((lane >= head * HD) & (lane < (head + 1) * HD)).astype(BF16)


SCALE = 10.0
LIMITS = {
    "pack": (56, 3), "embed": (8, 5), "attention_first": (10, 7), "attention_second": (10, 8), "mlp_first": (12, 7),
    "mlp_second": (14, 7), "head": (24, 9), "down_send": (8, 3), "down_keep": (14, 4), "up_send": (14, 6),
    "up_keep": (20, 8), "attention_send": (14, 13), "attention_keep": (20, 15), "scatter": (8, 5),
    "orthonormal": (4, 3), "right_mlp": (16, 3), "right_attention": (12, 2), "update": (16, 4),
}


def call(kernel, name, out_shape, operands, in_specs=None, scratch=(), out_specs=None, **grid):
    limit, cost = LIMITS[name]
    cost *= 1.0 if name in ("scatter", "orthonormal", "right_mlp", "right_attention", "update") else SCALE
    if in_specs is None:
        in_specs = [pl.BlockSpec(memory_space=pltpu.VMEM)] * len(operands)
    if out_specs is not None:
        grid["out_specs"] = out_specs
    return pl.pallas_call(
        kernel,
        out_shape=out_shape,
        in_specs=in_specs,
        scratch_shapes=list(scratch),
        compiler_params=pltpu.CompilerParams(vmem_limit_bytes=limit * MIB),
        cost_estimate=pl.CostEstimate(flops=int(cost * 1150000000), bytes_accessed=int(cost * 1000000), transcendentals=0),
        name=name,
        **grid,
    )(*operands)


VMEM = pl.BlockSpec(memory_space=pltpu.VMEM)
SMEM = pl.BlockSpec(memory_space=pltpu.SMEM)
ANY = pl.BlockSpec(memory_space=pltpu.HBM)


def shape(*dims, dtype=F32):
    return jax.ShapeDtypeStruct(dims, dtype)


def normalize(x):
    center = x - jnp.mean(x, -1, keepdims=True)
    inverse = lax.rsqrt(jnp.mean(center * center, -1, keepdims=True) + EPSILON)
    return center * inverse, inverse


def norm_back(normed, inverse, gain, grad):
    inner = grad * gain
    first = jnp.mean(inner, -1, keepdims=True)
    second = jnp.mean(inner * normed, -1, keepdims=True)
    d_x = inverse * (inner - first - normed * second)
    return d_x, jnp.sum(grad * normed, 0, keepdims=True), jnp.sum(grad, 0, keepdims=True)


def split3(x):
    high = x.astype(BF16).astype(F32)
    rest = x - high
    middle = rest.astype(BF16).astype(F32)
    return jnp.concatenate([high, middle, rest - middle], 0).astype(BF16)


def fold3(x):
    rank = x.shape[0] // 3
    return x[:rank] + x[rank : 2 * rank] + x[2 * rank :]


def panel(start, right, left):
    return fold3(bdot(split3(fold3(ndot(split3(start), right))), left))


def split2(x):
    high = x.astype(BF16)
    return high, (x - high.astype(F32)).astype(BF16)


def wide(dot, start, x):
    parts = split3(start)
    high, rest = split2(x)
    return fold3(dot(parts, high) + dot(parts, rest))


class Fetch:
    def __init__(self, meta_ref, sems):
        self.half, self.sems, self.used = meta_ref[1], sems, 0

    def one(self, source, target):
        copy = pltpu.make_async_copy(source, target, self.sems.at[self.used])
        self.used += 1
        copy.start()
        return copy

    def block(self, pieces, target, first=0):
        if len(pieces) == 1:
            return [self.one(pieces[0], target.at[pl.ds(first, pieces[0].shape[0]), :])]
        size = pieces[0].shape[0]
        spots = (first + self.half * size, first + (1 - self.half) * size)
        return [
            self.one(piece, target.at[pl.ds(pl.multiple_of(spot, 32), size), :])
            for piece, spot in zip(pieces, spots)
        ]


def wait(copies):
    for copy in copies:
        copy.wait()


def pack_kernel(meta_ref, qkv_ref, out_ref, up_ref, down_ref, tables_ref, first_ref, first_half, up_half, down_half, table_ref, table_half, sems):
    near, rest = qkv_ref.shape[0], out_ref.shape[0]
    size = first_half.shape[0]
    half = meta_ref[1]
    at = pl.multiple_of(half * size, 32)
    fetch = Fetch(meta_ref, sems)
    firsts = [
        fetch.one(qkv_ref, first_ref.at[pl.ds(0, near), :]),
        fetch.one(out_ref, first_ref.at[pl.ds(near, rest), :]),
    ]
    copies = [
        fetch.one(up_ref.at[pl.ds(at, size), :], up_half),
        fetch.one(down_ref.at[pl.ds(at, size), :], down_half),
    ]
    total = tables_ref.shape[1]
    table_ref[...] = jnp.zeros_like(table_ref)
    table_ref[:, :total] = tables_ref[...]
    rows = table_half.shape[0]
    table_half[...] = table_ref[pl.ds(pl.multiple_of(half * rows, 32), rows), :]
    wait(firsts)
    first_half[...] = first_ref[pl.ds(at, size), :]
    wait(copies)


def embed_kernel(own, vocab, meta_ref, live_ref, ids_ref, slots_ref, table_ref, far_ref, near_ref, own_ref, rows_ref):
    images, length = ids_ref.shape
    slot_count = slots_ref.shape[1]
    total = table_ref.shape[1]
    member = meta_ref[0]
    ids_t = jnp.transpose(ids_ref[...].astype(F32))
    image_lane = lax.broadcasted_iota(jnp.int32, (length, images), 1)
    position = lax.broadcasted_iota(jnp.int32, (length, 1), 0)
    slot_lane = lax.broadcasted_iota(jnp.int32, (1, slot_count), 1)
    table_lane = lax.broadcasted_iota(jnp.int32, (1, total), 1)
    table = table_ref[...]

    def rows_of(ids):
        hot = jnp.where(ids == table_lane, 1.0, 0.0).astype(BF16)
        return ndot(table, hot).astype(BF16)

    targets = {
        0: (own_ref, 0), 1: (near_ref, 0), 2: (far_ref.at[0], 0), 3: (far_ref.at[1], 0),
    }
    for k in range(4):
        for i in range(own):
            image = (member ^ k) * own + i
            hit = (slots_ref[pl.ds(image, 1), :] == position) & (slot_lane < live_ref[image])
            masked = jnp.max(jnp.where(hit, 1.0, 0.0), 1, keepdims=True)
            ids = jnp.sum(jnp.where(image_lane == image, ids_t, 0.0), 1, keepdims=True)
            ids = jnp.where(masked > 0, float(vocab - 1), ids).astype(jnp.int32)
            place = k * own + i
            rows_ref[:, place : place + 1] = ids
            ref, first = targets[k]
            ref[:, first + i * length : first + (i + 1) * length] = rows_of(ids)
    at = rows_of(position + vocab)
    own_ref[:, own * length :] = at
    near_ref[:, own * length :] = at
    far_ref[0, :, own * length :] = at[:, : length // 2]
    far_ref[1, :, own * length :] = at[:, length // 2 :]


def attention_one(length, hb, w, bias_ref, qkv_ref, lse_ref, ctx_ref):
    width = ctx_ref.shape[1]
    mixed = ndot(hb, w)
    first = bias_ref.shape[1] - 6 * width
    q_bias = bias_ref[0:1, first : first + width]
    v_bias = bias_ref[0:1, first + width : first + 2 * width]
    qkv_ref[0] = ((mixed[:, :width] + q_bias) * HD ** (-0.5)).astype(BF16)
    qkv_ref[1] = mixed[:, width : 2 * width].astype(BF16)
    qkv_ref[2] = (mixed[:, 2 * width :] + v_bias).astype(BF16)
    for image in range(hb.shape[0] // length):
        rows = slice(image * length, (image + 1) * length)
        q, k, v = qkv_ref[0, rows, :], qkv_ref[1, rows, :], qkv_ref[2, rows, :]
        total = jnp.zeros((length, width), F32)
        for head in range(width // HD):
            mask = head_mask(width, head)
            scores = ndot(q * mask, k)
            top = jnp.max(scores, -1, keepdims=True)
            powers = jnp.exp(scores - top)
            weight = jnp.sum(powers, -1, keepdims=True)
            lse_ref[rows, head : head + 1] = top + jnp.log(weight)
            probs = (powers * (1.0 / weight)).astype(BF16)
            total = total + bdot(probs, v * mask)
        ctx_ref[rows, :] = total.astype(BF16)


def attention_first_kernel(
    length, meta_ref, e0, e1, e2, e3, vec_ref, b0, b1, c0, c1,
    normed_ref, inverse_ref, hb_ref, qkv0, lse0, ctx0, qkv1, lse1, ctx1, x_ref, w_ref, sems,
):
    rows, width = hb_ref.shape[0], e0.shape[0]
    member = meta_ref[0]
    fetch = Fetch(meta_ref, sems)
    used = 3 * width
    zero = fetch.one(c0.at[pl.ds(0, used), :], w_ref.at[0])
    one = fetch.one(c1.at[pl.ds(0, used), :], w_ref.at[1])
    slabs = ((e0, e0, e0), (e1, e1, e1), (e2.at[0], e2.at[0], e2.at[1]), (e3.at[1], e3.at[0], e3.at[1]))
    for k, (ref, low, high) in enumerate(slabs):
        at = low[:, rows:] if low is high else jnp.concatenate([low[:, rows:], high[:, rows:]], 1)
        at = at.astype(F32)
        place = pl.ds(pl.multiple_of((member ^ k) * width, 64), width)
        for i in range(rows // length):
            x_ref[place, i * length : (i + 1) * length] = ref[:, i * length : (i + 1) * length].astype(F32) + at
    normed, inverse = normalize(jnp.transpose(x_ref[...]))
    normed_ref[...] = normed
    inverse_ref[...] = inverse
    hb_ref[...] = (normed * vec_ref[0:1, :] + vec_ref[1:2, :]).astype(BF16)
    hb = hb_ref[...]
    zero.wait()
    attention_one(length, hb, w_ref[0], b0, qkv0, lse0, ctx0)
    one.wait()
    attention_one(length, hb, w_ref[1], b1, qkv1, lse1, ctx1)


def attention_second_kernel(
    length, meta_ref, normed_ref, hb_ref, vec_ref, b2, b3, ctx0, ctx1, c0, c1, c2a, c2b, c3a, c3b,
    normed1_ref, inverse1_ref, h1b_ref, qkv2, lse2, ctx2, qkv3, lse3, ctx3, w_ref, o_ref, sems,
):
    hb = hb_ref[...]
    width = ctx0.shape[1]
    used = 3 * width
    fetch = Fetch(meta_ref, sems)
    two = fetch.block((c2a, c2b), w_ref.at[0])
    three = fetch.block((c3a, c3b), w_ref.at[1])
    others = [fetch.one(c.at[pl.ds(used, width), :], o_ref.at[n]) for n, c in enumerate((c0, c1))]
    wait(two)
    attention_one(length, hb, w_ref[0, :used, :], b2, qkv2, lse2, ctx2)
    wait(three)
    attention_one(length, hb, w_ref[1, :used, :], b3, qkv3, lse3, ctx3)
    wait(others)
    total = bdot(ctx0[...], o_ref[0]) + bdot(ctx1[...], o_ref[1])
    total = total + bdot(ctx2[...], w_ref[0, used:, :]) + bdot(ctx3[...], w_ref[1, used:, :])
    z_one = normed_ref[...] * vec_ref[0:1, :] + vec_ref[1:2, :] + (total + vec_ref[2:3, :])
    normed, inverse = normalize(z_one)
    normed1_ref[...] = normed
    inverse1_ref[...] = inverse
    h1b_ref[...] = (normed * vec_ref[3:4, :] + vec_ref[4:5, :]).astype(BF16)


def gelu_pair(x):
    inner = 0.7978845608028654 * x * (1.0 + 0.044715 * x * x)
    curve = jnp.tanh(inner)
    value = 0.5 * x * (1.0 + curve)
    slope = 0.5 * (1.0 + curve) + 0.5 * x * (1.0 - curve * curve) * (
        0.7978845608028654 * (1.0 + 3 * 0.044715 * x * x)
    )
    return value, slope


def mlp_one(h1b, up_ref, bias_ref, active_ref, slope_ref):
    first = bias_ref.shape[1] - up_ref.shape[1]
    step = 256
    for at in range(0, up_ref.shape[1], step):
        pre = bdot(h1b, up_ref[:, at : at + step]) + bias_ref[0:1, first + at : first + at + step]
        value, slope = gelu_pair(pre)
        active_ref[:, at : at + step] = value.astype(BF16)
        slope_ref[:, at : at + step] = slope


def mlp_first_kernel(meta_ref, h1b_ref, b0, b1, u0, u1, d0, d1, a0, a1, s0, s1, low_ref, w_ref, sems):
    fetch = Fetch(meta_ref, sems)
    copies = [fetch.one(ref, w_ref.at[n]) for n, ref in enumerate((u0, d0, u1, d1))]
    h1b = h1b_ref[...]
    copies[0].wait()
    mlp_one(h1b, w_ref.at[0], b0, a0, s0)
    copies[1].wait()
    low_ref[...] = bdot(a0[...], w_ref[1])
    copies[2].wait()
    mlp_one(h1b, w_ref.at[2], b1, a1, s1)
    copies[3].wait()
    low_ref[...] += bdot(a1[...], w_ref[3])


def mlp_second_kernel(
    meta_ref, h1b_ref, b2, b3, low_ref, normed1_ref, vec_ref, u2a, u2b, u3a, u3b, d2a, d2b, d3a, d3b,
    a2, a3, s2, s3, normed2_ref, inverse2_ref, h2b_ref, w_ref, sems,
):
    fetch = Fetch(meta_ref, sems)
    pieces = ((u2a, u2b), (d2a, d2b), (u3a, u3b), (d3a, d3b))
    copies = [fetch.block(piece, w_ref.at[n]) for n, piece in enumerate(pieces)]
    h1b = h1b_ref[...]
    wait(copies[0])
    mlp_one(h1b, w_ref.at[0], b2, a2, s2)
    wait(copies[1])
    normed2_ref[...] = low_ref[...] + bdot(a2[...], w_ref[1])
    wait(copies[2])
    mlp_one(h1b, w_ref.at[2], b3, a3, s3)
    wait(copies[3])
    total = normed2_ref[...] + bdot(a3[...], w_ref[3]) + vec_ref[5:6, :]
    normed, inverse = normalize(normed1_ref[...] * vec_ref[3:4, :] + vec_ref[4:5, :] + total)
    normed2_ref[...] = normed
    inverse2_ref[...] = inverse
    h2b_ref[...] = (normed * vec_ref[6:7, :] + vec_ref[7:8, :]).astype(BF16)


def head_kernel(
    own, vocab, meta_ref, live_ref, count_ref, ids_ref, slots_ref, bias_ref, vec_ref,
    h2b_ref, normed2_ref, inverse2_ref, t0, t1, t2a, t2b, t3a, t3b,
    dz_ref, dzb_ref, loss_ref, gbias_ref, gvec_ref, send_ref, keep_ref,
    table_ref, full_ref, grad_ref, sems,
):
    images, length = ids_ref.shape
    slot_count = slots_ref.shape[1]
    total = bias_ref.shape[1]
    member = meta_ref[0]
    columns = t0.shape[0]
    fetch = Fetch(meta_ref, sems)
    copies = []
    for k, pieces in enumerate(((t0,), (t1,), (t2a, t2b), (t3a, t3b))):
        copies += fetch.block(pieces, table_ref, pl.multiple_of((member ^ k) * columns, 64))
    slots_t = jnp.transpose(slots_ref[...].astype(F32))
    image_lane = lax.broadcasted_iota(jnp.int32, (slot_count, images), 1)
    slot_row = lax.broadcasted_iota(jnp.int32, (slot_count, 1), 0)
    position = lax.broadcasted_iota(jnp.int32, (1, length), 1).astype(F32)
    picks, targets, weights, picked = [], [], [], []
    for i in range(own):
        image = member * own + i
        at = jnp.sum(jnp.where(image_lane == image, slots_t, 0.0), 1, keepdims=True)
        hit = at == position
        ids = ids_ref[pl.ds(image, 1), :].astype(F32)
        targets.append(jnp.sum(jnp.where(hit, ids, 0.0), 1, keepdims=True).astype(jnp.int32))
        weights.append(jnp.where(slot_row < live_ref[image], 1.0, 0.0))
        picks.append(jnp.where(hit, 1.0, 0.0).astype(BF16))
        picked.append(bdot(picks[i], h2b_ref[i * length : (i + 1) * length, :]).astype(BF16))
    target = jnp.concatenate(targets, 0)
    weight = jnp.concatenate(weights, 0)
    rows = jnp.concatenate(picked, 0)
    wait(copies)
    lane = lax.broadcasted_iota(jnp.int32, (1, total), 1)
    logits = bdot(rows, table_ref[...]) + bias_ref[...]
    logits = jnp.where(lane < vocab, logits, -1e30)
    top = jnp.max(logits, -1, keepdims=True)
    log_total = top + jnp.log(jnp.sum(jnp.exp(logits - top), -1, keepdims=True))
    hot = jnp.where(lane == target, 1.0, 0.0)
    chosen = jnp.sum(hot * logits, -1, keepdims=True)
    loss_ref[...] = jnp.broadcast_to(jnp.sum(weight * (log_total - chosen), 0, keepdims=True), loss_ref.shape)
    d_logits = (jnp.exp(logits - log_total) - hot) * (weight / count_ref[0])
    gbias_ref[...] = jnp.sum(d_logits, 0, keepdims=True)
    dl = d_logits.astype(BF16)
    d_rows = ndot(dl, table_ref[...])
    high = d_rows.astype(BF16)
    rest = (d_rows - high.astype(F32)).astype(BF16)
    for i in range(own):
        part = slice(i * slot_count, (i + 1) * slot_count)
        grad_ref[i * length : (i + 1) * length, :] = tdot(picks[i], high[part]) + tdot(picks[i], rest[part])
    d_z2, d_gain, d_shift = norm_back(normed2_ref[...], inverse2_ref[...], vec_ref[6:7, :], grad_ref[...])
    dz_ref[...] = d_z2
    dzb_ref[...] = d_z2.astype(BF16)
    gvec_ref[0:1, :] = jnp.sum(d_z2, 0, keepdims=True)
    gvec_ref[1:2, :] = d_gain
    gvec_ref[2:3, :] = d_shift
    full_ref[...] = tdot(rows, dl).astype(BF16)
    for k, out in enumerate((keep_ref.at[0], send_ref.at[0], keep_ref.at[1], send_ref.at[1])):
        out[...] = full_ref[pl.ds(pl.multiple_of((member ^ k) * columns, 64), columns), :]


def down_send_kernel(dzb_ref, a1, a3, s1, s3, send_ref, left_ref):
    first = dzb_ref.shape[1]
    dzb = dzb_ref[...]
    for n, (active, start) in enumerate(((a1[...], s1), (a3[...], s3))):
        send_ref[n] = tdot(active, dzb).astype(BF16)
        left_ref[n] = panel(start[:8, first : 2 * first], dzb, active)


def close(n, grad, near_ref, err_ref, far_refs, part_ref):
    if n == 0:
        part_ref[...] = grad + near_ref[0].astype(F32) + err_ref[...]
    else:
        total = (grad + near_ref[1].astype(F32)).astype(BF16)
        size = total.shape[0] // len(far_refs)
        for place, far_ref in enumerate(far_refs):
            far_ref[...] = total[place * size : (place + 1) * size]


def down_keep_kernel(dzb_ref, a0, a2, s0, s2, near_ref, err_ref, far_ref, part_ref, left_ref):
    first = dzb_ref.shape[1]
    dzb = dzb_ref[...]
    for n, (active, start) in ((1, (a2[...], s2)), (0, (a0[...], s0))):
        close(n, tdot(active, dzb), near_ref, err_ref, (far_ref,), part_ref)
        left_ref[n] = panel(start[:8, first : 2 * first], dzb, active)
    left_ref[0] += wide(ndot, s0[:8, first : 2 * first], err_ref[...])


def up_one(dzb, h1b, slope, up, down, start, hidden_ref, dpre_ref):
    step = 256
    for at in range(0, down.shape[0], step):
        d_pre = ndot(dzb, down[at : at + step, :]) * slope[:, at : at + step]
        hidden_ref[:, at : at + step] = jnp.sum(d_pre, 0, keepdims=True)
        dpre_ref[:, at : at + step] = d_pre.astype(BF16)
    d_pre = dpre_ref[...]
    return tdot(h1b, d_pre), ndot(d_pre, up[...]), panel(start[:8, : d_pre.shape[1]], d_pre, h1b)


def up_send_kernel(
    meta_ref, dzb_ref, h1b_ref, p1, p3, s1, s3, u1, u3a, u3b, d1, d3a, d3b,
    send_ref, left_ref, dh_ref, hidden_ref, dpre_ref, w_ref, sems,
):
    fetch = Fetch(meta_ref, sems)
    pieces = ((d1,), (u1,), (d3a, d3b), (u3a, u3b))
    copies = [fetch.block(piece, w_ref.at[n]) for n, piece in enumerate(pieces)]
    dzb, h1b = dzb_ref[...], h1b_ref[...]
    for n, (slope, start) in enumerate(((p1, s1), (p3, s3))):
        wait(copies[2 * n] + copies[2 * n + 1])
        grad, part, left_ref[n] = up_one(
            dzb, h1b, slope, w_ref.at[2 * n + 1], w_ref.at[2 * n], start, hidden_ref.at[n], dpre_ref
        )
        send_ref[n] = grad.astype(BF16)
        dh_ref[...] = part if n == 0 else dh_ref[...] + part


def up_keep_kernel(
    meta_ref, dz_ref, dzb_ref, h1b_ref, normed1_ref, inverse1_ref, vec_ref, dh_ref, p0, p2, s0, s2,
    near_ref, err_ref, u0, u2a, u2b, d0, d2a, d2b,
    far_a, far_b, part_ref, left_ref, dz1_ref, dz1b_ref, gvec_ref, hidden_ref, dpre_ref, w_ref, sems,
):
    fetch = Fetch(meta_ref, sems)
    pieces = ((d0,), (u0,), (d2a, d2b), (u2a, u2b))
    copies = [fetch.block(piece, w_ref.at[n]) for n, piece in enumerate(pieces)]
    dzb, h1b = dzb_ref[...], h1b_ref[...]
    for n, (slope, start) in ((1, (p2, s2)), (0, (p0, s0))):
        wait(copies[2 * n] + copies[2 * n + 1])
        grad, part, left_ref[n] = up_one(
            dzb, h1b, slope, w_ref.at[2 * n + 1], w_ref.at[2 * n], start, hidden_ref.at[n], dpre_ref
        )
        close(n, grad, near_ref, err_ref, (far_a, far_b), part_ref)
        dz1_ref[...] = part + (dz_ref[...] + dh_ref[...] if n == 1 else dz1_ref[...])
    left_ref[0] += wide(ndot, s0[:8, : err_ref.shape[1]], err_ref[...])
    d_z1, d_gain, d_shift = norm_back(normed1_ref[...], inverse1_ref[...], vec_ref[3:4, :], dz1_ref[...])
    dz1_ref[...] = d_z1
    dz1b_ref[...] = d_z1.astype(BF16)
    gvec_ref[0:1, :] = jnp.sum(d_z1, 0, keepdims=True)
    gvec_ref[1:2, :] = d_gain
    gvec_ref[2:3, :] = d_shift


def attention_back_one(length, dz, hb, w_ref, qkv_ref, lse_ref, ctx_ref, start_ref, pack_ref, dm_ref, dc_ref):
    width, features = ctx_ref.shape[1], dz.shape[1]
    used = 3 * width
    dc_ref[...] = ndot(dz, w_ref[used:, :]).astype(BF16)
    ctx = ctx_ref[...]
    out_grad = tdot(ctx, dz)
    pack_ref[:8, 3 * features :] = panel(start_ref[:8, 2 * features : 3 * features], dz, ctx)
    q_sum = jnp.zeros((1, width), F32)
    v_sum = jnp.zeros((1, width), F32)
    for image in range(dz.shape[0] // length):
        rows = slice(image * length, (image + 1) * length)
        q, k, v, dc = qkv_ref[0, rows, :], qkv_ref[1, rows, :], qkv_ref[2, rows, :], dc_ref[rows, :]
        d_query = jnp.zeros((length, width), F32)
        d_key = jnp.zeros((length, width), F32)
        d_value = jnp.zeros((length, width), F32)
        for head in range(width // HD):
            mask = head_mask(width, head)
            q_head, k_head, c_head = q * mask, k * mask, dc * mask
            probs = jnp.exp(ndot(q_head, k) - lse_ref[rows, head : head + 1])
            d_value = d_value + tdot(probs.astype(BF16), c_head)
            d_probs = ndot(c_head, v)
            inner = jnp.sum(d_probs * probs, -1, keepdims=True)
            d_scores = (probs * (d_probs - inner)).astype(BF16)
            d_query = d_query + bdot(d_scores, k_head)
            d_key = d_key + tdot(d_scores, q_head)
        d_query = d_query * HD ** (-0.5)
        q_sum = q_sum + jnp.sum(d_query, 0, keepdims=True)
        v_sum = v_sum + jnp.sum(d_value, 0, keepdims=True)
        dm_ref[rows, :width] = d_query.astype(BF16)
        dm_ref[rows, width : 2 * width] = d_key.astype(BF16)
        dm_ref[rows, 2 * width :] = d_value.astype(BF16)
    pack_ref[8:9, :width] = q_sum
    pack_ref[8:9, width : 2 * width] = v_sum
    dm = dm_ref[...]
    pack_ref[:8, 2 * features : 3 * features] = panel(start_ref[:8, 3 * features : 3 * features + dm_ref.shape[1]], dm, hb)
    return tdot(dm, hb), out_grad, bdot(dm, w_ref[:used, :])


def pack_rows(pack_ref, width, up, down, hidden):
    features = up.shape[1]
    pack_ref[...] = jnp.zeros_like(pack_ref)
    pack_ref[:8, :features] = up
    pack_ref[:8, features : 2 * features] = down
    pack_ref[8:9, 2 * width : 2 * width + features] = hidden


def pack_whole(pack_ref, vectors, bias, loss):
    pack_ref[9:10, : bias.shape[1]] = bias
    features = vectors[0].shape[1]
    for n, vector in enumerate(vectors + [loss]):
        row, place = 10 + n // 3, n % 3
        pack_ref[row : row + 1, place * features : place * features + vector.shape[1]] = vector


def attention_send_kernel(
    length, meta_ref, dz1b_ref, hb_ref, q1, q3, l1, l3, x1, x3, s1, s3, up_ref, down_ref, hidden_ref,
    c1, c3a, c3b, send_ref, pack_ref, dh_ref, dm_ref, dc_ref, w_ref, sems,
):
    fetch = Fetch(meta_ref, sems)
    copies = [fetch.block((c1,), w_ref.at[0]), fetch.block((c3a, c3b), w_ref.at[1])]
    dz, hb = dz1b_ref[...], hb_ref[...]
    used = dm_ref.shape[1]
    for n, (q, l, x, start) in enumerate(((q1, l1, x1, s1), (q3, l3, x3, s3))):
        wait(copies[n])
        pack_rows(pack_ref.at[n], x.shape[1], up_ref[n], down_ref[n], hidden_ref[n])
        qkv_grad, out_grad, part = attention_back_one(
            length, dz, hb, w_ref.at[n], q, l, x, start, pack_ref.at[n], dm_ref, dc_ref
        )
        send_ref[n, :used, :] = qkv_grad.astype(BF16)
        send_ref[n, used:, :] = out_grad.astype(BF16)
        dh_ref[...] = part if n == 0 else dh_ref[...] + part


def attention_keep_kernel(
    length, meta_ref, dz1b_ref, hb_ref, q0, q2, l0, l2, x0, x2, s0, s2, up_ref, down_ref, hidden_ref,
    near_ref, err_qkv, err_out, dz1_ref, dha_ref, normed_ref, inverse_ref, vec_ref, gvec1_ref, gvec2_ref, gbias_ref,
    loss_ref, send_pack_ref, c0, c2a, c2b,
    far_ref, part_ref, pack_ref, send_ref, d_far, d_near, d_own, dm_ref, dc_ref, dh_ref, w_ref, sems,
):
    fetch = Fetch(meta_ref, sems)
    copies = [fetch.block((c0,), w_ref.at[0]), fetch.block((c2a, c2b), w_ref.at[1])]
    dz, hb = dz1b_ref[...], hb_ref[...]
    used, width = dm_ref.shape[1], x0.shape[1]
    features = hb.shape[1]
    for n, (q, l, x, start) in ((1, (q2, l2, x2, s2)), (0, (q0, l0, x0, s0))):
        wait(copies[n])
        pack_rows(pack_ref.at[n], width, up_ref[n], down_ref[n], hidden_ref[n])
        qkv_grad, out_grad, part = attention_back_one(
            length, dz, hb, w_ref.at[n], q, l, x, start, pack_ref.at[n], dm_ref, dc_ref
        )
        if n == 0:
            part_ref[:used, :] = qkv_grad + near_ref[0, :used, :].astype(F32) + err_qkv[...]
            part_ref[used:, :] = out_grad + near_ref[0, used:, :].astype(F32) + err_out[...]
        else:
            far_ref[:used, :] = (qkv_grad + near_ref[1, :used, :].astype(F32)).astype(BF16)
            far_ref[used:, :] = (out_grad + near_ref[1, used:, :].astype(F32)).astype(BF16)
        dh_ref[...] = part + (dha_ref[...] + dz1_ref[...] if n == 1 else dh_ref[...])
    pack_ref[0, :8, 2 * features : 3 * features] += wide(bdot, s0[:8, 3 * features : 3 * features + used], err_qkv[...])
    pack_ref[0, :8, 3 * features :] += wide(ndot, s0[:8, 2 * features : 3 * features], err_out[...])
    d_x, d_gain, d_shift = norm_back(normed_ref[...], inverse_ref[...], vec_ref[0:1, :], dh_ref[...])
    vectors = [d_gain, d_shift] + [gvec1_ref[i : i + 1, :] for i in range(3)] + [gvec2_ref[i : i + 1, :] for i in range(3)]
    send_ref[...] = send_pack_ref[...]
    for ref in (send_ref.at[0], send_ref.at[1], pack_ref.at[0], pack_ref.at[1]):
        pack_whole(ref, vectors, gbias_ref[...], loss_ref[...])
    dh_ref[...] = d_x
    rows, columns = d_own.shape
    for t in range(4):

        @pl.when(meta_ref[0] == t)
        def _():
            for k, out in enumerate((d_own, d_near, d_far.at[0], d_far.at[1])):
                out[...] = dh_ref[:, (t ^ k) * columns : ((t ^ k) + 1) * columns].astype(BF16)


def scatter_kernel(own, vocab, ids_ref, r0, r1, r2, r3, near_ref, keep_ref, far_ref, out_ref):
    length = ids_ref.shape[0]
    total = out_ref.shape[1]
    lane = lax.broadcasted_iota(jnp.int32, (1, total), 1)
    position = lax.broadcasted_iota(jnp.int32, (length, 1), 0) + vocab
    result = keep_ref[0].astype(F32) + near_ref[0].astype(F32) + far_ref[...].astype(F32)
    for k, rows in enumerate((r0[...], r1[...], r2[0], r3[1])):
        hots = []
        for i in range(own):
            ids = ids_ref[:, k * own + i : k * own + i + 1]
            hots.append(jnp.where((ids == lane) | (position == lane), 1.0, 0.0).astype(BF16))
        result = result + tdot(rows, jnp.concatenate(hots, 0))
    out_ref[...] = result.astype(out_ref.dtype)


def joined(refs):
    parts = [ref[...].astype(F32) for ref in refs]
    return parts[0] if len(parts) == 1 else jnp.concatenate(parts, 0)


def right_mlp_kernel(part_d, got_d, part_u, got_a, got_b, base_ref, rest_ref, out_ref):
    size = part_d.shape[1]
    rows = part_d.shape[0]
    for n, (part, gots) in enumerate(((part_u, (got_a, got_b)), (part_d, (got_d,)))):
        merged = part[...] + joined(gots)
        out_ref[:, n * size : (n + 1) * size] = wide(bdot, base_ref[:, n * rows : (n + 1) * rows], merged)
    out_ref[:, 2 * size :] = rest_ref[...]


def right_attention_kernel(used, part, got, base_ref, out_ref):
    features = part.shape[1]
    out_ref[:, :features] = wide(bdot, base_ref[:, 3 * features :], part[used:, :] + got[used:, :].astype(F32))
    merged = part[:used, :] + got[:used, :].astype(F32)
    out_ref[:, features:] = wide(ndot, base_ref[:, 2 * features : 3 * features], merged)


def update_kernel(replicas, part, weight, moment, first_ref, second_ref, *refs):
    gots, (weight_new, moment_new, error_new) = refs[:-3], refs[-3:]
    first, second = split3(first_ref[...] * (1.0 / replicas)), split3(second_ref[...])
    rank = first.shape[0] // 3
    parts = lambda x, order: jnp.concatenate([x[i * rank : (i + 1) * rank].astype(F32) for i in order], 0).astype(BF16)
    approx = tdot(parts(first, (0, 0, 1, 0, 2, 1)), parts(second, (0, 1, 0, 2, 0, 1)))
    new = BETA * moment[...] + approx
    moment_new[...] = new
    weight_new[...] = weight[...].astype(F32) - RATE_MAT * new
    error_new[...] = part[...] + joined(gots) - approx


def update(replicas, part, gots, first_row, weight, moment, first, second):
    rows, cols = weight.shape
    block = 256
    spec = pl.BlockSpec((rows, block), lambda i: (0, i))
    out = shape(rows, cols)
    mine = lambda size: pl.BlockSpec((size, block), lambda i: (first_row // size, i))
    return call(
        functools.partial(update_kernel, replicas), "update", (out, out, out),
        (part, weight, moment, first, second, *gots),
        [mine(rows), spec, spec, pl.BlockSpec(first.shape, lambda i: (0, 0)),
         pl.BlockSpec((second.shape[0], block), lambda i: (0, i))] + [mine(rows // len(gots))] * len(gots),
        out_specs=[spec] * 3, grid=(cols // block,),
    )


def orthonormal_kernel(sizes, panel_ref, out_ref):
    rank = panel_ref.shape[0]
    place = lax.broadcasted_iota(jnp.int32, (rank, 1), 0)
    cuts = [sum(sizes[:i]) for i in range(len(sizes) + 1)]
    panels = [panel_ref[:, a:b] for a, b in zip(cuts, cuts[1:])]
    for number in range(rank):
        for which, (a, b) in enumerate(zip(cuts, cuts[1:])):
            part = panels[which]
            column = part[number : number + 1, :]
            column = column * lax.rsqrt(jnp.sum(column * column, -1, keepdims=True) + 1e-20)
            out_ref[number : number + 1, a:b] = column
            if number + 1 < rank:
                along = jnp.sum(part * column, -1, keepdims=True)
                panels[which] = part - jnp.where(place > number, along, 0.0) * column


class Order:
    def __init__(self):
        self.last = None

    def __call__(self, x):
        if self.last is not None:
            x = tie(x, self.last)
        self.last = x
        return x

    def mark(self, x):
        self.last = x


def exchange(x, bit):
    return across(x, "dp", bit)


class RowSum:
    def __init__(self, x, bits):
        self.x, self.bits, self.step = x, bits, 0
        self.steps = bits[:2] + bits[2:] + bits[1::-1]
        self.place = lax.axis_index("dp")

    def send(self):
        step, bit, x = self.step, self.steps[self.step], self.x
        self.upper = (self.place & bit) != 0
        if step < 2:
            half = x.shape[0] // 2
            x = jnp.where(self.upper, x[:half], x[half:])
        self.got = across(x, "dp", bit)

    def receive(self, order):
        step, x, upper = self.step, self.x, self.upper
        got = order(self.got)
        if step < 2:
            half = x.shape[0] // 2
            x = (jnp.where(upper, x[half:], x[:half]).astype(F32) + got.astype(F32)).astype(BF16)
        elif step < len(self.bits):
            x = (x.astype(F32) + got.astype(F32)).astype(BF16)
        else:
            x = jnp.concatenate([jnp.where(upper, got, x), jnp.where(upper, x, got)], 0)
        self.x = x
        self.step += 1
        return self.step < len(self.steps)


class WholeSum:
    def __init__(self, x, bits):
        self.x, self.steps, self.step = x, bits, 0

    def send(self):
        self.got = across(self.x, "dp", self.steps[self.step])

    def receive(self, order):
        self.x = self.x + order(self.got)
        self.step += 1
        return self.step < len(self.steps)


def advance(order, *sums):
    for one in sums:
        if one.step < len(one.steps) and one.receive(order):
            one.send()


def shards(
    token_ids, masked_at, live_counts, tables, table_mom, vec_whole, vec_mom, vec_split, split_mom,
    head_bias, bias_mom, w_qkv, w_out, w_up, w_down, mom_qkv, mom_out, mom_up, mom_down,
    err_qkv, err_out, err_up, err_down, start_qkv, start_out, start_up, start_down,
):
    groups = lax.axis_size("tensor")
    replicas = lax.axis_size("dp")
    images, length = token_ids.shape
    vocab = head_bias.shape[0]
    total_rows, columns = tables.shape
    features = w_qkv.shape[0]
    width = w_qkv.shape[1] // 3
    hidden = w_up.shape[1]
    own = images // groups
    rows = own * length
    rank = start_qkv.shape[1]
    total = total_rows + -total_rows % 128
    used = 3 * width
    all_rows = used + width
    bits = [1 << i for i in range(replicas.bit_length() - 1)]
    meta = jnp.stack([lax.axis_index("tensor"), lax.axis_index("dp") & 1]).astype(jnp.int32)
    order = Order()

    bf = functools.partial(shape, dtype=BF16)
    dma = lambda n: pltpu.SemaphoreType.DMA((n,))
    vm = lambda *dims: pltpu.VMEM(dims, BF16)

    def cores(pieces):
        return tuple(core_swap(piece) for piece in pieces)

    first_own, first_half, up_half, down_half, table_own, table_half = call(
        pack_kernel, "pack",
        (bf(all_rows, features), bf(all_rows // 2, features), bf(features // 2, hidden), bf(hidden // 2, features),
         bf(columns, total), bf(columns // 2, total)),
        (meta, w_qkv.T, w_out, w_up, w_down, tables.T), [SMEM] + [ANY] * 4 + [VMEM], [dma(4)],
    )
    order.mark(first_half)
    first_far = [chip_swap(first_half)]
    part = bf(columns, rows + length)
    e_far, e_near, e_own, ids_rows = call(
        functools.partial(embed_kernel, own, vocab), "embed",
        (bf(2, columns, rows + length // 2), part, part, shape(length, images, dtype=jnp.int32)),
        (meta, live_counts, token_ids, masked_at, order(table_own)), [SMEM, SMEM, VMEM, VMEM, VMEM],
    )
    order.mark(e_far)
    first_near, up_near, down_near, table_near = cores((first_own, w_up, w_down, table_own))
    own_starts = jnp.concatenate((start_up.T, start_down.T, start_out.T, start_qkv.T), 1)
    gap = -own_starts.shape[1] % 128
    bias_row = jnp.pad(vec_split, ((0, rank - 1), (gap, 0)))
    small = [jnp.concatenate([own_starts, bias_row], 1)]
    small.append(core_swap(small[0]))
    e_one = core_swap(e_near)
    e_two = chip_swap(e_far)
    first_far[0] = order(first_far[0])
    first_far.append(exchange(first_far[0], 1))
    count = WholeSum(tie(jnp.broadcast_to(jnp.sum(live_counts).astype(F32), (8, 128)), first_far[0]), bits)
    count.send()
    e_two = order(e_two)
    up_far = [chip_swap(tie(up_half, e_two))]
    small.append(chip_swap(tie(small[0], e_two)))
    e_three = core_swap(e_two)
    advance(order, count)
    starts = splits = small

    state = (shape(rows, features), shape(rows, 1), bf(rows, features))
    block = (bf(3, rows, width), shape(rows, width // HD), bf(rows, width))
    res = call(
        functools.partial(attention_first_kernel, length), "attention_first", state + block + block,
        (tie(meta, up_near, down_near, first_near, table_near), order(e_own), e_one, e_two, e_three, vec_whole,
         small[0], small[1], first_own, first_near),
        [SMEM] + [VMEM] * 7 + [ANY] * 2, [pltpu.VMEM((features, rows), F32), vm(2, used, features), dma(2)],
    )
    normed0, inverse0, h0b = res[:3]
    order.mark(h0b)
    kept = [res[3:6], res[6:9]]
    small[2] = order(small[2])
    first_far[1] = order(first_far[1])
    first_both = cores([tie(x, first_far[1]) for x in first_far])
    small.append(core_swap(small[2]))
    up_far[0] = order(up_far[0])
    down_far = [chip_swap(tie(down_half, up_far[0]))]
    up_far.append(exchange(up_far[0], 1))
    advance(order, count)
    res = call(
        functools.partial(attention_second_kernel, length), "attention_second", state + block + block,
        (meta, order(normed0), h0b, vec_whole, splits[2], splits[3], kept[0][2], kept[1][2], first_own, first_near,
         *first_far, *first_both),
        [SMEM] + [VMEM] * 7 + [ANY] * 6, [vm(2, all_rows, features), vm(2, width, features), dma(6)],
    )
    normed1, inverse1, h1b = res[:3]
    order.mark(h1b)
    kept += [res[3:6], res[6:9]]
    while count.step < len(bits):
        advance(order, count)
    act = bf(rows, hidden)
    slope = shape(rows, hidden)
    a0, a1, p0, p1, low = call(
        mlp_first_kernel, "mlp_first", (act, act, slope, slope, shape(rows, features)),
        (meta, order(h1b), splits[0], splits[1], w_up, up_near, w_down, down_near),
        [SMEM] + [VMEM] * 3 + [ANY] * 4, [vm(4, features, hidden), dma(4)],
    )
    order.mark(low)
    down_far[0] = order(down_far[0])
    down_far.append(exchange(down_far[0], 1))
    table_far = [chip_swap(tie(table_half, down_far[0]))]
    up_far[1] = order(up_far[1])
    up_both = cores([tie(x, up_far[1]) for x in up_far])
    table_far[0] = order(table_far[0])
    table_far.append(exchange(table_far[0], 1))
    down_far[1] = order(down_far[1])
    down_both = cores([tie(x, down_far[1]) for x in down_far])
    a2, a3, p2, p3, normed2, inverse2, h2b = call(
        mlp_second_kernel, "mlp_second", (act, act, slope, slope) + state,
        (meta, order(h1b), splits[2], splits[3], low, normed1, vec_whole, *up_far, *up_both, *down_far, *down_both),
        [SMEM] + [VMEM] * 6 + [ANY] * 8, [vm(4, features, hidden), dma(8)],
    )
    order.mark(h2b)
    table_far[1] = order(table_far[1])
    table_both = cores([tie(x, table_far[1]) for x in table_far])
    count = count.x[0, :1]
    pair = lambda a, b, dtype: shape(2, a, b, dtype=dtype)
    dz2, dz2b, loss_part, g_bias, g_vec2, head_send, head_keep = call(
        functools.partial(head_kernel, own, vocab), "head",
        (
            shape(rows, features), bf(rows, features), shape(1, 128), shape(1, total),
            shape(3, features), pair(columns, total, BF16), pair(columns, total, BF16),
        ),
        (
            meta, live_counts, count, token_ids, masked_at,
            jnp.pad(head_bias, (0, total - vocab)).reshape(1, total), vec_whole, order(h2b), normed2, inverse2,
            table_own, table_near, *table_far, *table_both,
        ),
        [SMEM] * 3 + [VMEM] * 7 + [ANY] * 6,
        [vm(features, total), vm(features, total), pltpu.VMEM((rows, features), F32), dma(6)],
    )
    order.mark(dz2b)

    head_near = core_swap(head_send)
    left = shape(2, rank, features)
    down_send, left_down_a = call(
        down_send_kernel, "down_send", (pair(hidden, features, BF16), left),
        (order(dz2b), a1, a3, starts[1], starts[3]),
    )
    order.mark(down_send)
    down_got = core_swap(down_send)
    head_far = order((head_keep[1].astype(F32) + head_near[1].astype(F32)).astype(BF16))
    head_in = chip_swap(head_far)
    up_send, left_up_a, dh_a, hidden_a = call(
        up_send_kernel, "up_send",
        (pair(features, hidden, BF16), left, shape(rows, features), shape(2, 1, hidden)),
        (meta, order(dz2b), h1b, p1, p3, starts[1], starts[3], up_near, *up_both, down_near, *down_both),
        [SMEM] + [VMEM] * 6 + [ANY] * 6, [vm(rows, hidden), vm(4, features, hidden), dma(6)],
    )
    order.mark(dh_a)
    up_got = core_swap(up_send)
    down_far_grad, down_part, left_down_b = call(
        down_keep_kernel, "down_keep", (bf(hidden, features), shape(hidden, features), left),
        (order(dz2b), a0, a2, starts[0], starts[2], down_got, err_down[0]),
    )
    order.mark(left_down_b)
    down_in = chip_swap(down_far_grad)
    up_a, up_b, up_part, left_up_b, dz1, dz1b, g_vec1, hidden_b = call(
        up_keep_kernel, "up_keep",
        (bf(features // 2, hidden), bf(features // 2, hidden), shape(features, hidden), left, shape(rows, features), bf(rows, features),
         shape(3, features), shape(2, 1, hidden)),
        (meta, dz2, order(dz2b), h1b, normed1, inverse1, vec_whole, dh_a, p0, p2, starts[0], starts[2],
         up_got, err_up[0], w_up, *up_far, w_down, *down_far),
        [SMEM] + [VMEM] * 13 + [ANY] * 6, [vm(rows, hidden), vm(4, features, hidden), dma(6)],
    )
    order.mark(dz1b)
    pack_width = 3 * features + width
    pack = shape(2, 16, pack_width)
    scratch = [vm(rows, used), vm(rows, width)]
    first_send, pack_a, dh_b = call(
        functools.partial(attention_send_kernel, length), "attention_send",
        (pair(all_rows, features, BF16), pack, shape(rows, features)),
        (meta, order(dz1b), h0b, kept[1][0], kept[3][0], kept[1][1], kept[3][1], kept[1][2], kept[3][2],
         starts[1], starts[3], left_up_a, left_down_a, hidden_a, first_near, *first_both),
        [SMEM] + [VMEM] * 13 + [ANY] * 3, scratch + [vm(2, all_rows, features), dma(3)],
    )
    order.mark(dh_b)
    head_in, down_in = order(head_in), order(down_in)
    first_got = core_swap(tie(first_send, down_in))
    up_in_a = chip_swap(tie(up_a, down_in))
    cols = bf(rows, columns)
    first_far_grad, first_part, pack_b, pack_a, d_far, d_near, d_own = call(
        functools.partial(attention_keep_kernel, length), "attention_keep",
        (bf(all_rows, features), shape(all_rows, features), pack, pack, pair(rows, columns, BF16), cols, cols),
        (meta, order(dz1b), h0b, kept[0][0], kept[2][0], kept[0][1], kept[2][1], kept[0][2], kept[2][2],
         starts[0], starts[2], left_up_b, left_down_b, hidden_b, first_got, err_qkv[0].T, err_out[0],
         dz1, dh_b, normed0, inverse0, vec_whole, g_vec1, g_vec2, g_bias, loss_part, pack_a,
         first_own, *first_far),
        [SMEM] + [VMEM] * 26 + [ANY] * 3,
        scratch + [pltpu.VMEM((rows, features), F32), vm(2, all_rows, features), dma(3)],
    )
    order.mark(d_far)

    d_two = chip_swap(d_far)
    up_in_a = order(up_in_a)
    up_in_b = chip_swap(tie(up_b, up_in_a))
    mine = order(pack_b + core_swap(tie(pack_a, up_in_a)))
    d_one = core_swap(tie(d_near, up_in_a))
    mine_in = chip_swap(mine[1])
    mine = order(mine[0] + mine_in)
    panels = WholeSum(mine[:8], bits)
    panels.send()
    advance(order, panels)
    d_two = order(d_two)
    d_three = core_swap(d_two)
    first_in = chip_swap(tie(first_far_grad, d_two))
    advance(order, panels)
    table_grad = call(
        functools.partial(scatter_kernel, own, vocab), "scatter", bf(columns, total),
        (ids_rows, order(d_own), d_one, d_two, d_three, head_near, head_keep, head_in),
    )
    order.mark(table_grad)
    cut = columns // 2
    table_sums = (
        RowSum(table_grad[:cut], [bits[1], bits[0]] + bits[2:]), RowSum(table_grad[cut:], bits),
    )
    for one in table_sums:
        one.send()
    while panels.step < len(bits):
        advance(order, panels)
    sizes = (features, features, features, width)
    bases = call(
        functools.partial(orthonormal_kernel, sizes), "orthonormal", shape(rank, pack_width), (order(panels.x),),
    )
    order.mark(bases)
    packed = call(
        right_mlp_kernel, "right_mlp", shape(rank, 2 * features + pack_width),
        (down_part, down_in, up_part, up_in_a, order(up_in_b), bases, mine[8:]),
    )
    packed = WholeSum(packed, bits)
    packed.send()
    for _ in range(2):
        advance(order, *table_sums, packed)
    rights = call(
        functools.partial(right_attention_kernel, used), "right_attention", shape(rank, features + used),
        (first_part, order(first_in), bases),
    )
    order.mark(rights)
    rights = WholeSum(rights, bits)
    rights.send()
    while packed.step < len(bits):
        advance(order, *table_sums, packed)
    base_up, base_down = bases[:, :features], bases[:, features : 2 * features]
    base_qkv, base_out = bases[:, 2 * features : 3 * features], bases[:, 3 * features :]
    right_up, right_down = packed.x[:, :features], packed.x[:, features : 2 * features]
    rest = packed.x[:, 2 * features :]
    down = update(replicas, down_part, [down_in], 0, w_down, mom_down, order(base_down), right_down)
    order.mark(down[0])
    advance(order, *table_sums, rights)
    up = update(replicas, up_part, [up_in_a, up_in_b], 0, w_up, mom_up, order(base_up), right_up)
    order.mark(up[0])
    while rights.step < len(bits) or table_sums[1].step < len(table_sums[1].steps):
        advance(order, *table_sums, rights)
    right_out, right_qkv = rights.x[:, :features], rights.x[:, features:]
    out = update(replicas, first_part, [first_in], used, w_out, mom_out, base_out, right_out)
    qkv = update(replicas, first_part, [first_in], 0, w_qkv.T, mom_qkv.T, right_qkv, base_qkv)

    table_grad = jnp.concatenate([one.x for one in table_sums], 0)[:, :total_rows].astype(F32)
    vectors = [rest[2 + n // 3, n % 3 * features : (n % 3 + 1) * features] for n in range(8)]
    results = [jnp.stack([rest[4, 2 * features], count[0]])]

    def momentum_step(weight, moment, grad, rate):
        new_moment = BETA * moment + grad
        return (weight.astype(F32) - rate * new_moment, new_moment)

    new = momentum_step(tables.T, table_mom.T, table_grad, RATE_TAB)
    results += [new[0].T, new[1].T]
    results += momentum_step(vec_whole, vec_mom, jnp.stack(vectors), RATE_VEC)
    results += momentum_step(vec_split, split_mom, rest[0:1, : vec_split.shape[1]], RATE_VEC)
    results += momentum_step(head_bias, bias_mom, rest[1, :vocab], RATE_VEC)
    one = 1.0 / replicas
    for (weight, moment, error), base, right, flip in (
        (qkv, base_qkv, right_qkv, True), (out, base_out, right_out, False),
        (up, base_up, right_up, False), (down, base_down, right_down, False),
    ):
        if flip:
            weight, moment, error = weight.T, moment.T, error.T
        results += [weight, moment, error[None], base.T[None], right.T * one]
    return tuple(results)


def solution(mesh):
    rows, cols = P("tensor", None), P(None, "tensor")
    batch = P("dp", None)
    in_specs = (
        batch, batch, P("dp"), cols, cols, P(), P(), rows, rows, P(), P(),
        cols, rows, cols, rows, cols, rows, cols, rows,
        P("dp", None, "tensor"), P("dp", "tensor", None), P("dp", None, "tensor"), P("dp", "tensor", None),
        rows, rows, rows, rows,
    )
    left = P("tensor", None, None)
    out_specs = (P(), cols, cols, P(), P(), rows, rows, P(), P())
    for side in (cols, rows, cols, rows):
        out_specs += (side, side, P("dp", *side), left, rows)
    return jax.shard_map(shards, mesh=mesh, in_specs=in_specs, out_specs=out_specs, check_vma=False)
```

```python
import functools

import jax
import jax.numpy as jnp
from jax import lax
from jax.experimental import pallas as pl
from jax.experimental.pallas import tpu as pltpu
from jax.sharding import PartitionSpec as P

HD = 48
EPSILON = 1e-05
BETA = 0.9
RATE_MAT = 100.0
RATE_VEC = 10.0
RATE_TAB = 100.0
HIGHEST = lax.Precision.HIGHEST
BF16 = jnp.bfloat16
F32 = jnp.float32
MIB = 1024 * 1024


def bdot(left, right):
    return jnp.dot(left, right, preferred_element_type=F32)


def tdot(left, right):
    return lax.dot_general(left, right, (((0,), (0,)), ((), ())), preferred_element_type=F32)


def ndot(left, right):
    return lax.dot_general(left, right, (((1,), (1,)), ((), ())), preferred_element_type=F32)


def across(x, axis, bit):
    size = lax.axis_size(axis)
    return lax.ppermute(x, axis, [(i, i ^ bit) for i in range(size)])


def core_swap(x):
    return across(x, "tensor", 1)


def chip_swap(x):
    return across(x, "tensor", 2)


def tie(x, *others):
    return lax.optimization_barrier((x,) + others)[0]


def head_mask(width, head):
    lane = lax.broadcasted_iota(jnp.int32, (1, width), 1)
    return ((lane >= head * HD) & (lane < (head + 1) * HD)).astype(BF16)


SCALE = 10.0
LIMITS = {
    "pack": (56, 3), "embed": (8, 5), "attention_first": (10, 7), "attention_second": (10, 8), "mlp_first": (12, 7),
    "mlp_second": (14, 7), "head": (24, 9), "down_send": (8, 3), "down_keep": (14, 4), "up_send": (14, 6),
    "up_keep": (20, 8), "attention_send": (14, 13), "attention_keep": (20, 15), "scatter": (8, 5),
    "orthonormal": (4, 3), "right_mlp": (16, 3), "right_attention": (12, 2), "update": (16, 4),
}


def call(kernel, name, out_shape, operands, in_specs=None, scratch=(), out_specs=None, **grid):
    limit, cost = LIMITS[name]
    cost *= 1.0 if name in ("scatter", "orthonormal", "right_mlp", "right_attention", "update") else SCALE
    if in_specs is None:
        in_specs = [pl.BlockSpec(memory_space=pltpu.VMEM)] * len(operands)
    if out_specs is not None:
        grid["out_specs"] = out_specs
    return pl.pallas_call(
        kernel,
        out_shape=out_shape,
        in_specs=in_specs,
        scratch_shapes=list(scratch),
        compiler_params=pltpu.CompilerParams(vmem_limit_bytes=limit * MIB),
        cost_estimate=pl.CostEstimate(flops=int(cost * 1150000000), bytes_accessed=int(cost * 1000000), transcendentals=0),
        name=name,
        **grid,
    )(*operands)


VMEM = pl.BlockSpec(memory_space=pltpu.VMEM)
SMEM = pl.BlockSpec(memory_space=pltpu.SMEM)
ANY = pl.BlockSpec(memory_space=pltpu.HBM)


def shape(*dims, dtype=F32):
    return jax.ShapeDtypeStruct(dims, dtype)


def normalize(x):
    center = x - jnp.mean(x, -1, keepdims=True)
    inverse = lax.rsqrt(jnp.mean(center * center, -1, keepdims=True) + EPSILON)
    return center * inverse, inverse


def norm_back(normed, inverse, gain, grad):
    inner = grad * gain
    first = jnp.mean(inner, -1, keepdims=True)
    second = jnp.mean(inner * normed, -1, keepdims=True)
    d_x = inverse * (inner - first - normed * second)
    return d_x, jnp.sum(grad * normed, 0, keepdims=True), jnp.sum(grad, 0, keepdims=True)


def split3(x):
    high = x.astype(BF16).astype(F32)
    rest = x - high
    middle = rest.astype(BF16).astype(F32)
    return jnp.concatenate([high, middle, rest - middle], 0).astype(BF16)


def fold3(x):
    rank = x.shape[0] // 3
    return x[:rank] + x[rank : 2 * rank] + x[2 * rank :]


def panel(start, right, left):
    return fold3(bdot(split3(fold3(ndot(split3(start), right))), left))


def split2(x):
    high = x.astype(BF16)
    return high, (x - high.astype(F32)).astype(BF16)


def wide(dot, start, x):
    parts = split3(start)
    high, rest = split2(x)
    return fold3(dot(parts, high) + dot(parts, rest))


class Fetch:
    def __init__(self, meta_ref, sems):
        self.half, self.sems, self.used = meta_ref[1], sems, 0

    def one(self, source, target):
        copy = pltpu.make_async_copy(source, target, self.sems.at[self.used])
        self.used += 1
        copy.start()
        return copy

    def block(self, pieces, target, first=0):
        if len(pieces) == 1:
            return [self.one(pieces[0], target.at[pl.ds(first, pieces[0].shape[0]), :])]
        size = pieces[0].shape[0]
        spots = (first + self.half * size, first + (1 - self.half) * size)
        return [
            self.one(piece, target.at[pl.ds(pl.multiple_of(spot, 32), size), :])
            for piece, spot in zip(pieces, spots)
        ]


def wait(copies):
    for copy in copies:
        copy.wait()


def pack_kernel(meta_ref, qkv_ref, out_ref, up_ref, down_ref, tables_ref, first_ref, first_half, up_half, down_half, table_ref, table_half, sems):
    near, rest = qkv_ref.shape[0], out_ref.shape[0]
    size = first_half.shape[0]
    half = meta_ref[1]
    at = pl.multiple_of(half * size, 32)
    fetch = Fetch(meta_ref, sems)
    firsts = [
        fetch.one(qkv_ref, first_ref.at[pl.ds(0, near), :]),
        fetch.one(out_ref, first_ref.at[pl.ds(near, rest), :]),
    ]
    copies = [
        fetch.one(up_ref.at[pl.ds(at, size), :], up_half),
        fetch.one(down_ref.at[pl.ds(at, size), :], down_half),
    ]
    total = tables_ref.shape[1]
    table_ref[...] = jnp.zeros_like(table_ref)
    table_ref[:, :total] = tables_ref[...]
    rows = table_half.shape[0]
    table_half[...] = table_ref[pl.ds(pl.multiple_of(half * rows, 32), rows), :]
    wait(firsts)
    first_half[...] = first_ref[pl.ds(at, size), :]
    wait(copies)


def embed_kernel(own, vocab, meta_ref, live_ref, ids_ref, slots_ref, table_ref, far_ref, near_ref, own_ref, rows_ref):
    images, length = ids_ref.shape
    slot_count = slots_ref.shape[1]
    total = table_ref.shape[1]
    member = meta_ref[0]
    ids_t = jnp.transpose(ids_ref[...].astype(F32))
    image_lane = lax.broadcasted_iota(jnp.int32, (length, images), 1)
    position = lax.broadcasted_iota(jnp.int32, (length, 1), 0)
    slot_lane = lax.broadcasted_iota(jnp.int32, (1, slot_count), 1)
    table_lane = lax.broadcasted_iota(jnp.int32, (1, total), 1)
    table = table_ref[...]

    def rows_of(ids):
        hot = jnp.where(ids == table_lane, 1.0, 0.0).astype(BF16)
        return ndot(table, hot).astype(BF16)

    targets = {
        0: (own_ref, 0), 1: (near_ref, 0), 2: (far_ref.at[0], 0), 3: (far_ref.at[1], 0),
    }
    for k in range(4):
        for i in range(own):
            image = (member ^ k) * own + i
            hit = (slots_ref[pl.ds(image, 1), :] == position) & (slot_lane < live_ref[image])
            masked = jnp.max(jnp.where(hit, 1.0, 0.0), 1, keepdims=True)
            ids = jnp.sum(jnp.where(image_lane == image, ids_t, 0.0), 1, keepdims=True)
            ids = jnp.where(masked > 0, float(vocab - 1), ids).astype(jnp.int32)
            place = k * own + i
            rows_ref[:, place : place + 1] = ids
            ref, first = targets[k]
            ref[:, first + i * length : first + (i + 1) * length] = rows_of(ids)
    at = rows_of(position + vocab)
    own_ref[:, own * length :] = at
    near_ref[:, own * length :] = at
    far_ref[0, :, own * length :] = at[:, : length // 2]
    far_ref[1, :, own * length :] = at[:, length // 2 :]


def attention_one(length, hb, w, bias_ref, qkv_ref, lse_ref, ctx_ref):
    width = ctx_ref.shape[1]
    mixed = ndot(hb, w)
    first = bias_ref.shape[1] - 6 * width
    q_bias = bias_ref[0:1, first : first + width]
    v_bias = bias_ref[0:1, first + width : first + 2 * width]
    qkv_ref[0] = ((mixed[:, :width] + q_bias) * HD ** (-0.5)).astype(BF16)
    qkv_ref[1] = mixed[:, width : 2 * width].astype(BF16)
    qkv_ref[2] = (mixed[:, 2 * width :] + v_bias).astype(BF16)
    for image in range(hb.shape[0] // length):
        rows = slice(image * length, (image + 1) * length)
        q, k, v = qkv_ref[0, rows, :], qkv_ref[1, rows, :], qkv_ref[2, rows, :]
        total = jnp.zeros((length, width), F32)
        for head in range(width // HD):
            mask = head_mask(width, head)
            scores = ndot(q * mask, k)
            top = jnp.max(scores, -1, keepdims=True)
            powers = jnp.exp(scores - top)
            weight = jnp.sum(powers, -1, keepdims=True)
            lse_ref[rows, head : head + 1] = top + jnp.log(weight)
            probs = (powers * (1.0 / weight)).astype(BF16)
            total = total + bdot(probs, v * mask)
        ctx_ref[rows, :] = total.astype(BF16)


def attention_first_kernel(
    length, meta_ref, e0, e1, e2, e3, vec_ref, b0, b1, c0, c1,
    normed_ref, inverse_ref, hb_ref, qkv0, lse0, ctx0, qkv1, lse1, ctx1, x_ref, w_ref, sems,
):
    rows, width = hb_ref.shape[0], e0.shape[0]
    member = meta_ref[0]
    fetch = Fetch(meta_ref, sems)
    used = 3 * width
    zero = fetch.one(c0.at[pl.ds(0, used), :], w_ref.at[0])
    one = fetch.one(c1.at[pl.ds(0, used), :], w_ref.at[1])
    slabs = ((e0, e0, e0), (e1, e1, e1), (e2.at[0], e2.at[0], e2.at[1]), (e3.at[1], e3.at[0], e3.at[1]))
    for k, (ref, low, high) in enumerate(slabs):
        at = low[:, rows:] if low is high else jnp.concatenate([low[:, rows:], high[:, rows:]], 1)
        at = at.astype(F32)
        place = pl.ds(pl.multiple_of((member ^ k) * width, 64), width)
        for i in range(rows // length):
            x_ref[place, i * length : (i + 1) * length] = ref[:, i * length : (i + 1) * length].astype(F32) + at
    normed, inverse = normalize(jnp.transpose(x_ref[...]))
    normed_ref[...] = normed
    inverse_ref[...] = inverse
    hb_ref[...] = (normed * vec_ref[0:1, :] + vec_ref[1:2, :]).astype(BF16)
    hb = hb_ref[...]
    zero.wait()
    attention_one(length, hb, w_ref[0], b0, qkv0, lse0, ctx0)
    one.wait()
    attention_one(length, hb, w_ref[1], b1, qkv1, lse1, ctx1)


def attention_second_kernel(
    length, meta_ref, normed_ref, hb_ref, vec_ref, b2, b3, ctx0, ctx1, c0, c1, c2a, c2b, c3a, c3b,
    normed1_ref, inverse1_ref, h1b_ref, qkv2, lse2, ctx2, qkv3, lse3, ctx3, w_ref, o_ref, sems,
):
    hb = hb_ref[...]
    width = ctx0.shape[1]
    used = 3 * width
    fetch = Fetch(meta_ref, sems)
    two = fetch.block((c2a, c2b), w_ref.at[0])
    three = fetch.block((c3a, c3b), w_ref.at[1])
    others = [fetch.one(c.at[pl.ds(used, width), :], o_ref.at[n]) for n, c in enumerate((c0, c1))]
    wait(two)
    attention_one(length, hb, w_ref[0, :used, :], b2, qkv2, lse2, ctx2)
    wait(three)
    attention_one(length, hb, w_ref[1, :used, :], b3, qkv3, lse3, ctx3)
    wait(others)
    total = bdot(ctx0[...], o_ref[0]) + bdot(ctx1[...], o_ref[1])
    total = total + bdot(ctx2[...], w_ref[0, used:, :]) + bdot(ctx3[...], w_ref[1, used:, :])
    z_one = normed_ref[...] * vec_ref[0:1, :] + vec_ref[1:2, :] + (total + vec_ref[2:3, :])
    normed, inverse = normalize(z_one)
    normed1_ref[...] = normed
    inverse1_ref[...] = inverse
    h1b_ref[...] = (normed * vec_ref[3:4, :] + vec_ref[4:5, :]).astype(BF16)


def gelu_pair(x):
    inner = 0.7978845608028654 * x * (1.0 + 0.044715 * x * x)
    curve = jnp.tanh(inner)
    value = 0.5 * x * (1.0 + curve)
    slope = 0.5 * (1.0 + curve) + 0.5 * x * (1.0 - curve * curve) * (
        0.7978845608028654 * (1.0 + 3 * 0.044715 * x * x)
    )
    return value, slope


def mlp_one(h1b, up_ref, bias_ref, active_ref, slope_ref):
    first = bias_ref.shape[1] - up_ref.shape[1]
    step = 256
    for at in range(0, up_ref.shape[1], step):
        pre = bdot(h1b, up_ref[:, at : at + step]) + bias_ref[0:1, first + at : first + at + step]
        value, slope = gelu_pair(pre)
        active_ref[:, at : at + step] = value.astype(BF16)
        slope_ref[:, at : at + step] = slope


def mlp_first_kernel(meta_ref, h1b_ref, b0, b1, u0, u1, d0, d1, a0, a1, s0, s1, low_ref, w_ref, sems):
    fetch = Fetch(meta_ref, sems)
    copies = [fetch.one(ref, w_ref.at[n]) for n, ref in enumerate((u0, d0, u1, d1))]
    h1b = h1b_ref[...]
    copies[0].wait()
    mlp_one(h1b, w_ref.at[0], b0, a0, s0)
    copies[1].wait()
    low_ref[...] = bdot(a0[...], w_ref[1])
    copies[2].wait()
    mlp_one(h1b, w_ref.at[2], b1, a1, s1)
    copies[3].wait()
    low_ref[...] += bdot(a1[...], w_ref[3])


def mlp_second_kernel(
    meta_ref, h1b_ref, b2, b3, low_ref, normed1_ref, vec_ref, u2a, u2b, u3a, u3b, d2a, d2b, d3a, d3b,
    a2, a3, s2, s3, normed2_ref, inverse2_ref, h2b_ref, w_ref, sems,
):
    fetch = Fetch(meta_ref, sems)
    pieces = ((u2a, u2b), (d2a, d2b), (u3a, u3b), (d3a, d3b))
    copies = [fetch.block(piece, w_ref.at[n]) for n, piece in enumerate(pieces)]
    h1b = h1b_ref[...]
    wait(copies[0])
    mlp_one(h1b, w_ref.at[0], b2, a2, s2)
    wait(copies[1])
    normed2_ref[...] = low_ref[...] + bdot(a2[...], w_ref[1])
    wait(copies[2])
    mlp_one(h1b, w_ref.at[2], b3, a3, s3)
    wait(copies[3])
    total = normed2_ref[...] + bdot(a3[...], w_ref[3]) + vec_ref[5:6, :]
    normed, inverse = normalize(normed1_ref[...] * vec_ref[3:4, :] + vec_ref[4:5, :] + total)
    normed2_ref[...] = normed
    inverse2_ref[...] = inverse
    h2b_ref[...] = (normed * vec_ref[6:7, :] + vec_ref[7:8, :]).astype(BF16)


def head_kernel(
    own, vocab, meta_ref, live_ref, count_ref, ids_ref, slots_ref, bias_ref, vec_ref,
    h2b_ref, normed2_ref, inverse2_ref, t0, t1, t2a, t2b, t3a, t3b,
    dz_ref, dzb_ref, loss_ref, gbias_ref, gvec_ref, send_ref, keep_ref,
    table_ref, full_ref, grad_ref, sems,
):
    images, length = ids_ref.shape
    slot_count = slots_ref.shape[1]
    total = bias_ref.shape[1]
    member = meta_ref[0]
    columns = t0.shape[0]
    fetch = Fetch(meta_ref, sems)
    copies = []
    for k, pieces in enumerate(((t0,), (t1,), (t2a, t2b), (t3a, t3b))):
        copies += fetch.block(pieces, table_ref, pl.multiple_of((member ^ k) * columns, 64))
    slots_t = jnp.transpose(slots_ref[...].astype(F32))
    image_lane = lax.broadcasted_iota(jnp.int32, (slot_count, images), 1)
    slot_row = lax.broadcasted_iota(jnp.int32, (slot_count, 1), 0)
    position = lax.broadcasted_iota(jnp.int32, (1, length), 1).astype(F32)
    picks, targets, weights, picked = [], [], [], []
    for i in range(own):
        image = member * own + i
        at = jnp.sum(jnp.where(image_lane == image, slots_t, 0.0), 1, keepdims=True)
        hit = at == position
        ids = ids_ref[pl.ds(image, 1), :].astype(F32)
        targets.append(jnp.sum(jnp.where(hit, ids, 0.0), 1, keepdims=True).astype(jnp.int32))
        weights.append(jnp.where(slot_row < live_ref[image], 1.0, 0.0))
        picks.append(jnp.where(hit, 1.0, 0.0).astype(BF16))
        picked.append(bdot(picks[i], h2b_ref[i * length : (i + 1) * length, :]).astype(BF16))
    target = jnp.concatenate(targets, 0)
    weight = jnp.concatenate(weights, 0)
    rows = jnp.concatenate(picked, 0)
    wait(copies)
    lane = lax.broadcasted_iota(jnp.int32, (1, total), 1)
    logits = bdot(rows, table_ref[...]) + bias_ref[...]
    logits = jnp.where(lane < vocab, logits, -1e30)
    top = jnp.max(logits, -1, keepdims=True)
    log_total = top + jnp.log(jnp.sum(jnp.exp(logits - top), -1, keepdims=True))
    hot = jnp.where(lane == target, 1.0, 0.0)
    chosen = jnp.sum(hot * logits, -1, keepdims=True)
    loss_ref[...] = jnp.broadcast_to(jnp.sum(weight * (log_total - chosen), 0, keepdims=True), loss_ref.shape)
    d_logits = (jnp.exp(logits - log_total) - hot) * (weight / count_ref[0])
    gbias_ref[...] = jnp.sum(d_logits, 0, keepdims=True)
    dl = d_logits.astype(BF16)
    d_rows = ndot(dl, table_ref[...])
    high = d_rows.astype(BF16)
    rest = (d_rows - high.astype(F32)).astype(BF16)
    for i in range(own):
        part = slice(i * slot_count, (i + 1) * slot_count)
        grad_ref[i * length : (i + 1) * length, :] = tdot(picks[i], high[part]) + tdot(picks[i], rest[part])
    d_z2, d_gain, d_shift = norm_back(normed2_ref[...], inverse2_ref[...], vec_ref[6:7, :], grad_ref[...])
    dz_ref[...] = d_z2
    dzb_ref[...] = d_z2.astype(BF16)
    gvec_ref[0:1, :] = jnp.sum(d_z2, 0, keepdims=True)
    gvec_ref[1:2, :] = d_gain
    gvec_ref[2:3, :] = d_shift
    full_ref[...] = tdot(rows, dl).astype(BF16)
    for k, out in enumerate((keep_ref.at[0], send_ref.at[0], keep_ref.at[1], send_ref.at[1])):
        out[...] = full_ref[pl.ds(pl.multiple_of((member ^ k) * columns, 64), columns), :]


def down_send_kernel(dzb_ref, a1, a3, s1, s3, send_ref, left_ref):
    first = dzb_ref.shape[1]
    dzb = dzb_ref[...]
    for n, (active, start) in enumerate(((a1[...], s1), (a3[...], s3))):
        send_ref[n] = tdot(active, dzb).astype(BF16)
        left_ref[n] = panel(start[:8, first : 2 * first], dzb, active)


def close(n, grad, near_ref, err_ref, far_refs, part_ref):
    if n == 0:
        part_ref[...] = grad + near_ref[0].astype(F32) + err_ref[...]
    else:
        total = (grad + near_ref[1].astype(F32)).astype(BF16)
        first = 0
        for far_ref in far_refs:
            far_ref[...] = total[first : first + far_ref.shape[0]]
            first += far_ref.shape[0]


def down_keep_kernel(dzb_ref, a0, a2, s0, s2, near_ref, err_ref, far_a, far_b, part_ref, left_ref):
    first = dzb_ref.shape[1]
    dzb = dzb_ref[...]
    for n, (active, start) in ((1, (a2[...], s2)), (0, (a0[...], s0))):
        close(n, tdot(active, dzb), near_ref, err_ref, (far_a, far_b), part_ref)
        left_ref[n] = panel(start[:8, first : 2 * first], dzb, active)
    left_ref[0] += wide(ndot, s0[:8, first : 2 * first], err_ref[...])


def up_one(dzb, h1b, slope, up, down, start, hidden_ref, dpre_ref):
    step = 256
    for at in range(0, down.shape[0], step):
        d_pre = ndot(dzb, down[at : at + step, :]) * slope[:, at : at + step]
        hidden_ref[:, at : at + step] = jnp.sum(d_pre, 0, keepdims=True)
        dpre_ref[:, at : at + step] = d_pre.astype(BF16)
    d_pre = dpre_ref[...]
    return tdot(h1b, d_pre), ndot(d_pre, up[...]), panel(start[:8, : d_pre.shape[1]], d_pre, h1b)


def up_send_kernel(
    meta_ref, dzb_ref, h1b_ref, p1, p3, s1, s3, u1, u3a, u3b, d1, d3a, d3b,
    send_ref, left_ref, dh_ref, hidden_ref, dpre_ref, w_ref, sems,
):
    fetch = Fetch(meta_ref, sems)
    pieces = ((d1,), (u1,), (d3a, d3b), (u3a, u3b))
    copies = [fetch.block(piece, w_ref.at[n]) for n, piece in enumerate(pieces)]
    dzb, h1b = dzb_ref[...], h1b_ref[...]
    for n, (slope, start) in enumerate(((p1, s1), (p3, s3))):
        wait(copies[2 * n] + copies[2 * n + 1])
        grad, part, left_ref[n] = up_one(
            dzb, h1b, slope, w_ref.at[2 * n + 1], w_ref.at[2 * n], start, hidden_ref.at[n], dpre_ref
        )
        send_ref[n] = grad.astype(BF16)
        dh_ref[...] = part if n == 0 else dh_ref[...] + part


def up_keep_kernel(
    meta_ref, dz_ref, dzb_ref, h1b_ref, normed1_ref, inverse1_ref, vec_ref, dh_ref, p0, p2, s0, s2,
    near_ref, err_ref, other_ref, u0, u2a, u2b, d0, d2a, d2b,
    far_a, far_b, part_ref, left_ref, dz1_ref, dz1b_ref, gvec_ref, hidden_ref, dpre_ref, w_ref, sems,
):
    other = other_ref.shape[0]
    far_a[:other, :] = other_ref[...]
    fetch = Fetch(meta_ref, sems)
    pieces = ((d0,), (u0,), (d2a, d2b), (u2a, u2b))
    copies = [fetch.block(piece, w_ref.at[n]) for n, piece in enumerate(pieces)]
    dzb, h1b = dzb_ref[...], h1b_ref[...]
    for n, (slope, start) in ((1, (p2, s2)), (0, (p0, s0))):
        wait(copies[2 * n] + copies[2 * n + 1])
        grad, part, left_ref[n] = up_one(
            dzb, h1b, slope, w_ref.at[2 * n + 1], w_ref.at[2 * n], start, hidden_ref.at[n], dpre_ref
        )
        close(n, grad, near_ref, err_ref, (far_a.at[pl.ds(other, far_a.shape[0] - other), :], far_b), part_ref)
        dz1_ref[...] = part + (dz_ref[...] + dh_ref[...] if n == 1 else dz1_ref[...])
    left_ref[0] += wide(ndot, s0[:8, : err_ref.shape[1]], err_ref[...])
    d_z1, d_gain, d_shift = norm_back(normed1_ref[...], inverse1_ref[...], vec_ref[3:4, :], dz1_ref[...])
    dz1_ref[...] = d_z1
    dz1b_ref[...] = d_z1.astype(BF16)
    gvec_ref[0:1, :] = jnp.sum(d_z1, 0, keepdims=True)
    gvec_ref[1:2, :] = d_gain
    gvec_ref[2:3, :] = d_shift


def attention_back_one(length, dz, hb, w_ref, qkv_ref, lse_ref, ctx_ref, start_ref, pack_ref, dm_ref, dc_ref):
    width, features = ctx_ref.shape[1], dz.shape[1]
    used = 3 * width
    dc_ref[...] = ndot(dz, w_ref[used:, :]).astype(BF16)
    ctx = ctx_ref[...]
    out_grad = tdot(ctx, dz)
    pack_ref[:8, 3 * features :] = panel(start_ref[:8, 2 * features : 3 * features], dz, ctx)
    q_sum = jnp.zeros((1, width), F32)
    v_sum = jnp.zeros((1, width), F32)
    for image in range(dz.shape[0] // length):
        rows = slice(image * length, (image + 1) * length)
        q, k, v, dc = qkv_ref[0, rows, :], qkv_ref[1, rows, :], qkv_ref[2, rows, :], dc_ref[rows, :]
        d_query = jnp.zeros((length, width), F32)
        d_key = jnp.zeros((length, width), F32)
        d_value = jnp.zeros((length, width), F32)
        for head in range(width // HD):
            mask = head_mask(width, head)
            q_head, k_head, c_head = q * mask, k * mask, dc * mask
            probs = jnp.exp(ndot(q_head, k) - lse_ref[rows, head : head + 1])
            d_value = d_value + tdot(probs.astype(BF16), c_head)
            d_probs = ndot(c_head, v)
            inner = jnp.sum(d_probs * probs, -1, keepdims=True)
            d_scores = (probs * (d_probs - inner)).astype(BF16)
            d_query = d_query + bdot(d_scores, k_head)
            d_key = d_key + tdot(d_scores, q_head)
        d_query = d_query * HD ** (-0.5)
        q_sum = q_sum + jnp.sum(d_query, 0, keepdims=True)
        v_sum = v_sum + jnp.sum(d_value, 0, keepdims=True)
        dm_ref[rows, :width] = d_query.astype(BF16)
        dm_ref[rows, width : 2 * width] = d_key.astype(BF16)
        dm_ref[rows, 2 * width :] = d_value.astype(BF16)
    pack_ref[8:9, :width] = q_sum
    pack_ref[8:9, width : 2 * width] = v_sum
    dm = dm_ref[...]
    pack_ref[:8, 2 * features : 3 * features] = panel(start_ref[:8, 3 * features : 3 * features + dm_ref.shape[1]], dm, hb)
    return tdot(dm, hb), out_grad, bdot(dm, w_ref[:used, :])


def pack_rows(pack_ref, width, up, down, hidden):
    features = up.shape[1]
    pack_ref[...] = jnp.zeros_like(pack_ref)
    pack_ref[:8, :features] = up
    pack_ref[:8, features : 2 * features] = down
    pack_ref[8:9, 2 * width : 2 * width + features] = hidden


def pack_whole(pack_ref, vectors, bias, loss):
    pack_ref[9:10, : bias.shape[1]] = bias
    features = vectors[0].shape[1]
    for n, vector in enumerate(vectors + [loss]):
        row, place = 10 + n // 3, n % 3
        pack_ref[row : row + 1, place * features : place * features + vector.shape[1]] = vector


def attention_send_kernel(
    length, meta_ref, dz1b_ref, hb_ref, q1, q3, l1, l3, x1, x3, s1, s3, up_ref, down_ref, hidden_ref,
    c1, c3a, c3b, send_ref, pack_ref, dh_ref, dm_ref, dc_ref, w_ref, sems,
):
    fetch = Fetch(meta_ref, sems)
    copies = [fetch.block((c1,), w_ref.at[0]), fetch.block((c3a, c3b), w_ref.at[1])]
    dz, hb = dz1b_ref[...], hb_ref[...]
    used = dm_ref.shape[1]
    for n, (q, l, x, start) in enumerate(((q1, l1, x1, s1), (q3, l3, x3, s3))):
        wait(copies[n])
        pack_rows(pack_ref.at[n], x.shape[1], up_ref[n], down_ref[n], hidden_ref[n])
        qkv_grad, out_grad, part = attention_back_one(
            length, dz, hb, w_ref.at[n], q, l, x, start, pack_ref.at[n], dm_ref, dc_ref
        )
        send_ref[n, :used, :] = qkv_grad.astype(BF16)
        send_ref[n, used:, :] = out_grad.astype(BF16)
        dh_ref[...] = part if n == 0 else dh_ref[...] + part


def attention_keep_kernel(
    length, meta_ref, dz1b_ref, hb_ref, q0, q2, l0, l2, x0, x2, s0, s2, up_ref, down_ref, hidden_ref,
    near_ref, err_qkv, err_out, dz1_ref, dha_ref, normed_ref, inverse_ref, vec_ref, gvec1_ref, gvec2_ref, gbias_ref,
    loss_ref, send_pack_ref, c0, c2a, c2b,
    far_ref, part_ref, pack_ref, send_ref, d_far, d_near, d_own, dm_ref, dc_ref, dh_ref, w_ref, sems,
):
    fetch = Fetch(meta_ref, sems)
    copies = [fetch.block((c0,), w_ref.at[0]), fetch.block((c2a, c2b), w_ref.at[1])]
    dz, hb = dz1b_ref[...], hb_ref[...]
    used, width = dm_ref.shape[1], x0.shape[1]
    features = hb.shape[1]
    for n, (q, l, x, start) in ((1, (q2, l2, x2, s2)), (0, (q0, l0, x0, s0))):
        wait(copies[n])
        pack_rows(pack_ref.at[n], width, up_ref[n], down_ref[n], hidden_ref[n])
        qkv_grad, out_grad, part = attention_back_one(
            length, dz, hb, w_ref.at[n], q, l, x, start, pack_ref.at[n], dm_ref, dc_ref
        )
        if n == 0:
            part_ref[:used, :] = qkv_grad + near_ref[0, :used, :].astype(F32) + err_qkv[...]
            part_ref[used:, :] = out_grad + near_ref[0, used:, :].astype(F32) + err_out[...]
        else:
            far_ref[:used, :] = (qkv_grad + near_ref[1, :used, :].astype(F32)).astype(BF16)
            far_ref[used:, :] = (out_grad + near_ref[1, used:, :].astype(F32)).astype(BF16)
        dh_ref[...] = part + (dha_ref[...] + dz1_ref[...] if n == 1 else dh_ref[...])
    pack_ref[0, :8, 2 * features : 3 * features] += wide(bdot, s0[:8, 3 * features : 3 * features + used], err_qkv[...])
    pack_ref[0, :8, 3 * features :] += wide(ndot, s0[:8, 2 * features : 3 * features], err_out[...])
    d_x, d_gain, d_shift = norm_back(normed_ref[...], inverse_ref[...], vec_ref[0:1, :], dh_ref[...])
    vectors = [d_gain, d_shift] + [gvec1_ref[i : i + 1, :] for i in range(3)] + [gvec2_ref[i : i + 1, :] for i in range(3)]
    send_ref[...] = send_pack_ref[...]
    for ref in (send_ref.at[0], send_ref.at[1], pack_ref.at[0], pack_ref.at[1]):
        pack_whole(ref, vectors, gbias_ref[...], loss_ref[...])
    dh_ref[...] = d_x
    rows, columns = d_own.shape
    for t in range(4):

        @pl.when(meta_ref[0] == t)
        def _():
            for k, out in enumerate((d_own, d_near, d_far.at[0], d_far.at[1])):
                out[...] = dh_ref[:, (t ^ k) * columns : ((t ^ k) + 1) * columns].astype(BF16)


def scatter_kernel(own, vocab, ids_ref, r0, r1, r2, r3, near_ref, keep_ref, far_ref, out_ref):
    length = ids_ref.shape[0]
    total = out_ref.shape[1]
    lane = lax.broadcasted_iota(jnp.int32, (1, total), 1)
    position = lax.broadcasted_iota(jnp.int32, (length, 1), 0) + vocab
    result = keep_ref[0].astype(F32) + near_ref[0].astype(F32) + far_ref[...].astype(F32)
    for k, rows in enumerate((r0[...], r1[...], r2[0], r3[1])):
        hots = []
        for i in range(own):
            ids = ids_ref[:, k * own + i : k * own + i + 1]
            hots.append(jnp.where((ids == lane) | (position == lane), 1.0, 0.0).astype(BF16))
        result = result + tdot(rows, jnp.concatenate(hots, 0))
    out_ref[...] = result.astype(out_ref.dtype)


def joined(refs):
    parts = [ref[...].astype(F32) for ref in refs]
    return parts[0] if len(parts) == 1 else jnp.concatenate(parts, 0)


def right_mlp_kernel(part_d, got_c, both, part_u, got_b, base_ref, rest_ref, out_ref):
    size = part_d.shape[1]
    rows = part_d.shape[0]
    rest = rows - got_c.shape[0]
    got_d, got_a = both.at[pl.ds(0, rest), :], both.at[pl.ds(rest, both.shape[0] - rest), :]
    for n, (part, gots) in enumerate(((part_u, (got_a, got_b)), (part_d, (got_c, got_d)))):
        merged = part[...] + joined(gots)
        out_ref[:, n * size : (n + 1) * size] = wide(bdot, base_ref[:, n * rows : (n + 1) * rows], merged)
    out_ref[:, 2 * size :] = rest_ref[...]


def right_attention_kernel(used, part, got, base_ref, out_ref):
    features = part.shape[1]
    out_ref[:, :features] = wide(bdot, base_ref[:, 3 * features :], part[used:, :] + got[used:, :].astype(F32))
    merged = part[:used, :] + got[:used, :].astype(F32)
    out_ref[:, features:] = wide(ndot, base_ref[:, 2 * features : 3 * features], merged)


def update_kernel(replicas, part, weight, moment, first_ref, second_ref, *refs):
    gots, (weight_new, moment_new, error_new) = refs[:-3], refs[-3:]
    first, second = split3(first_ref[...] * (1.0 / replicas)), split3(second_ref[...])
    rank = first.shape[0] // 3
    parts = lambda x, order: jnp.concatenate([x[i * rank : (i + 1) * rank].astype(F32) for i in order], 0).astype(BF16)
    approx = tdot(parts(first, (0, 0, 1, 0, 2, 1)), parts(second, (0, 1, 0, 2, 0, 1)))
    new = BETA * moment[...] + approx
    moment_new[...] = new
    weight_new[...] = weight[...].astype(F32) - RATE_MAT * new
    error_new[...] = part[...] + joined(gots) - approx


def update(replicas, part, gots, first_row, weight, moment, first, second):
    rows, cols = weight.shape
    block = 256
    spec = pl.BlockSpec((rows, block), lambda i: (0, i))
    out = shape(rows, cols)
    mine = lambda size: pl.BlockSpec((size, block), lambda i: (first_row // size, i))
    rows_of = lambda size, first: pl.BlockSpec((size, block), lambda i: (first, i))
    own = [mine(rows)] if len(gots) == 1 else [rows_of(*got[1:]) for got in gots]
    gots = gots if len(gots) == 1 else [got[0] for got in gots]
    return call(
        functools.partial(update_kernel, replicas), "update", (out, out, out),
        (part, weight, moment, first, second, *gots),
        [mine(rows), spec, spec, pl.BlockSpec(first.shape, lambda i: (0, 0)),
         pl.BlockSpec((second.shape[0], block), lambda i: (0, i))] + own,
        out_specs=[spec] * 3, grid=(cols // block,),
    )


def orthonormal_kernel(sizes, panel_ref, out_ref, *outs):
    rank = panel_ref.shape[0]
    place = lax.broadcasted_iota(jnp.int32, (rank, 1), 0)
    cuts = [sum(sizes[:i]) for i in range(len(sizes) + 1)]
    panels = [panel_ref[:, a:b] for a, b in zip(cuts, cuts[1:])]
    for number in range(rank):
        for which, (a, b) in enumerate(zip(cuts, cuts[1:])):
            part = panels[which]
            column = part[number : number + 1, :]
            column = column * lax.rsqrt(jnp.sum(column * column, -1, keepdims=True) + 1e-20)
            out_ref[number : number + 1, a:b] = column
            outs[which][number : number + 1, :] = column
            if number + 1 < rank:
                along = jnp.sum(part * column, -1, keepdims=True)
                panels[which] = part - jnp.where(place > number, along, 0.0) * column


class Order:
    def __init__(self):
        self.last = None

    def __call__(self, x):
        if self.last is not None:
            x = tie(x, self.last)
        self.last = x
        return x

    def mark(self, x):
        self.last = x


def exchange(x, bit):
    return across(x, "dp", bit)


class RowSum:
    def __init__(self, x, bits):
        self.x, self.bits, self.step = x, bits, 0
        self.steps = bits[:2] + bits[2:] + bits[1::-1]
        self.place = lax.axis_index("dp")

    def send(self):
        step, bit, x = self.step, self.steps[self.step], self.x
        self.upper = (self.place & bit) != 0
        if step < 2:
            half = x.shape[0] // 2
            x = jnp.where(self.upper, x[:half], x[half:])
        self.got = across(x, "dp", bit)

    def receive(self, order):
        step, x, upper = self.step, self.x, self.upper
        got = order(self.got)
        if step < 2:
            half = x.shape[0] // 2
            x = (jnp.where(upper, x[half:], x[:half]).astype(F32) + got.astype(F32)).astype(BF16)
        elif step < len(self.bits):
            x = (x.astype(F32) + got.astype(F32)).astype(BF16)
        else:
            x = jnp.concatenate([jnp.where(upper, got, x), jnp.where(upper, x, got)], 0)
        self.x = x
        self.step += 1
        return self.step < len(self.steps)


class WholeSum:
    def __init__(self, x, bits):
        self.x, self.steps, self.step = x, bits, 0

    def send(self):
        self.got = across(self.x, "dp", self.steps[self.step])

    def receive(self, order):
        self.x = self.x + order(self.got)
        self.step += 1
        return self.step < len(self.steps)


def advance(order, *sums):
    for one in sums:
        if one.step < len(one.steps) and one.receive(order):
            one.send()


def shards(
    token_ids, masked_at, live_counts, tables, table_mom, vec_whole, vec_mom, vec_split, split_mom,
    head_bias, bias_mom, w_qkv, w_out, w_up, w_down, mom_qkv, mom_out, mom_up, mom_down,
    err_qkv, err_out, err_up, err_down, start_qkv, start_out, start_up, start_down,
):
    groups = lax.axis_size("tensor")
    replicas = lax.axis_size("dp")
    images, length = token_ids.shape
    vocab = head_bias.shape[0]
    total_rows, columns = tables.shape
    features = w_qkv.shape[0]
    width = w_qkv.shape[1] // 3
    hidden = w_up.shape[1]
    own = images // groups
    rows = own * length
    rank = start_qkv.shape[1]
    total = total_rows + -total_rows % 128
    used = 3 * width
    all_rows = used + width
    bits = [1 << i for i in range(replicas.bit_length() - 1)]
    meta = jnp.stack([lax.axis_index("tensor"), lax.axis_index("dp") & 1]).astype(jnp.int32)
    order = Order()

    bf = functools.partial(shape, dtype=BF16)
    dma = lambda n: pltpu.SemaphoreType.DMA((n,))
    vm = lambda *dims: pltpu.VMEM(dims, BF16)

    def cores(pieces):
        return tuple(core_swap(piece) for piece in pieces)

    first_own, first_half, up_half, down_half, table_own, table_half = call(
        pack_kernel, "pack",
        (bf(all_rows, features), bf(all_rows // 2, features), bf(features // 2, hidden), bf(hidden // 2, features),
         bf(columns, total), bf(columns // 2, total)),
        (meta, w_qkv.T, w_out, w_up, w_down, tables.T), [SMEM] + [ANY] * 4 + [VMEM], [dma(4)],
    )
    order.mark(first_half)
    first_far = [chip_swap(first_half)]
    part = bf(columns, rows + length)
    e_far, e_near, e_own, ids_rows = call(
        functools.partial(embed_kernel, own, vocab), "embed",
        (bf(2, columns, rows + length // 2), part, part, shape(length, images, dtype=jnp.int32)),
        (meta, live_counts, token_ids, masked_at, order(table_own)), [SMEM, SMEM, VMEM, VMEM, VMEM],
    )
    order.mark(e_far)
    first_near, up_near, down_near, table_near = cores((first_own, w_up, w_down, table_own))
    own_starts = jnp.concatenate((start_up.T, start_down.T, start_out.T, start_qkv.T), 1)
    gap = -own_starts.shape[1] % 128
    bias_row = jnp.pad(vec_split, ((0, rank - 1), (gap, 0)))
    small = [jnp.concatenate([own_starts, bias_row], 1)]
    small.append(core_swap(small[0]))
    e_one = core_swap(e_near)
    e_two = chip_swap(e_far)
    first_far[0] = order(first_far[0])
    first_far.append(exchange(first_far[0], 1))
    count = WholeSum(tie(jnp.broadcast_to(jnp.sum(live_counts).astype(F32), (8, 128)), first_far[0]), bits)
    count.send()
    e_two = order(e_two)
    up_far = [chip_swap(tie(up_half, e_two))]
    small.append(chip_swap(tie(small[0], e_two)))
    e_three = core_swap(e_two)
    advance(order, count)
    starts = splits = small

    state = (shape(rows, features), shape(rows, 1), bf(rows, features))
    block = (bf(3, rows, width), shape(rows, width // HD), bf(rows, width))
    res = call(
        functools.partial(attention_first_kernel, length), "attention_first", state + block + block,
        (tie(meta, up_near, down_near, first_near, table_near), order(e_own), e_one, e_two, e_three, vec_whole,
         small[0], small[1], first_own, first_near),
        [SMEM] + [VMEM] * 7 + [ANY] * 2, [pltpu.VMEM((features, rows), F32), vm(2, used, features), dma(2)],
    )
    normed0, inverse0, h0b = res[:3]
    order.mark(h0b)
    kept = [res[3:6], res[6:9]]
    small[2] = order(small[2])
    first_far[1] = order(first_far[1])
    first_both = cores([tie(x, first_far[1]) for x in first_far])
    small.append(core_swap(small[2]))
    up_far[0] = order(up_far[0])
    down_far = [chip_swap(tie(down_half, up_far[0]))]
    up_far.append(exchange(up_far[0], 1))
    advance(order, count)
    res = call(
        functools.partial(attention_second_kernel, length), "attention_second", state + block + block,
        (meta, order(normed0), h0b, vec_whole, splits[2], splits[3], kept[0][2], kept[1][2], first_own, first_near,
         *first_far, *first_both),
        [SMEM] + [VMEM] * 7 + [ANY] * 6, [vm(2, all_rows, features), vm(2, width, features), dma(6)],
    )
    normed1, inverse1, h1b = res[:3]
    order.mark(h1b)
    kept += [res[3:6], res[6:9]]
    while count.step < len(bits):
        advance(order, count)
    down_far[0] = order(down_far[0])
    down_far.append(exchange(down_far[0], 1))
    table_far = [chip_swap(tie(table_half, down_far[0]))]
    act = bf(rows, hidden)
    slope = shape(rows, hidden)
    a0, a1, p0, p1, low = call(
        mlp_first_kernel, "mlp_first", (act, act, slope, slope, shape(rows, features)),
        (meta, order(h1b), splits[0], splits[1], w_up, up_near, w_down, down_near),
        [SMEM] + [VMEM] * 3 + [ANY] * 4, [vm(4, features, hidden), dma(4)],
    )
    order.mark(low)
    up_far[1] = order(up_far[1])
    up_both = cores([tie(x, up_far[1]) for x in up_far])
    table_far[0] = order(table_far[0])
    table_far.append(exchange(table_far[0], 1))
    down_far[1] = order(down_far[1])
    down_both = cores([tie(x, down_far[1]) for x in down_far])
    a2, a3, p2, p3, normed2, inverse2, h2b = call(
        mlp_second_kernel, "mlp_second", (act, act, slope, slope) + state,
        (meta, order(h1b), splits[2], splits[3], low, normed1, vec_whole, *up_far, *up_both, *down_far, *down_both),
        [SMEM] + [VMEM] * 6 + [ANY] * 8, [vm(4, features, hidden), dma(8)],
    )
    order.mark(h2b)
    table_far[1] = order(table_far[1])
    table_both = cores([tie(x, table_far[1]) for x in table_far])
    count = count.x[0, :1]
    pair = lambda a, b, dtype: shape(2, a, b, dtype=dtype)
    dz2, dz2b, loss_part, g_bias, g_vec2, head_send, head_keep = call(
        functools.partial(head_kernel, own, vocab), "head",
        (
            shape(rows, features), bf(rows, features), shape(1, 128), shape(1, total),
            shape(3, features), pair(columns, total, BF16), pair(columns, total, BF16),
        ),
        (
            meta, live_counts, count, token_ids, masked_at,
            jnp.pad(head_bias, (0, total - vocab)).reshape(1, total), vec_whole, order(h2b), normed2, inverse2,
            table_own, table_near, *table_far, *table_both,
        ),
        [SMEM] * 3 + [VMEM] * 7 + [ANY] * 6,
        [vm(features, total), vm(features, total), pltpu.VMEM((rows, features), F32), dma(6)],
    )
    order.mark(dz2b)

    head_near = core_swap(head_send)
    left = shape(2, rank, features)
    down_send, left_down_a = call(
        down_send_kernel, "down_send", (pair(hidden, features, BF16), left),
        (order(dz2b), a1, a3, starts[1], starts[3]),
    )
    order.mark(down_send)
    down_got = core_swap(down_send)
    head_far = order((head_keep[1].astype(F32) + head_near[1].astype(F32)).astype(BF16))
    head_in = chip_swap(head_far)
    up_send, left_up_a, dh_a, hidden_a = call(
        up_send_kernel, "up_send",
        (pair(features, hidden, BF16), left, shape(rows, features), shape(2, 1, hidden)),
        (meta, order(dz2b), h1b, p1, p3, starts[1], starts[3], up_near, *up_both, down_near, *down_both),
        [SMEM] + [VMEM] * 6 + [ANY] * 6, [vm(rows, hidden), vm(4, features, hidden), dma(6)],
    )
    order.mark(dh_a)
    up_got = core_swap(up_send)
    down_a, down_b, down_part, left_down_b = call(
        down_keep_kernel, "down_keep",
        (bf(hidden // 2, features), bf(hidden // 2, features), shape(hidden, features), left),
        (order(dz2b), a0, a2, starts[0], starts[2], down_got, err_down[0]),
    )
    order.mark(left_down_b)
    down_in_a = chip_swap(down_a)
    both, up_b, up_part, left_up_b, dz1, dz1b, g_vec1, hidden_b = call(
        up_keep_kernel, "up_keep",
        (bf(hidden // 2 + features // 4, hidden), bf(features - features // 4, hidden), shape(features, hidden), left, shape(rows, features), bf(rows, features),
         shape(3, features), shape(2, 1, hidden)),
        (meta, dz2, order(dz2b), h1b, normed1, inverse1, vec_whole, dh_a, p0, p2, starts[0], starts[2],
         up_got, err_up[0], down_b, w_up, *up_far, w_down, *down_far),
        [SMEM] + [VMEM] * 14 + [ANY] * 6, [vm(rows, hidden), vm(4, features, hidden), dma(6)],
    )
    order.mark(dz1b)
    pack_width = 3 * features + width
    pack = shape(2, 16, pack_width)
    scratch = [vm(rows, used), vm(rows, width)]
    first_send, pack_a, dh_b = call(
        functools.partial(attention_send_kernel, length), "attention_send",
        (pair(all_rows, features, BF16), pack, shape(rows, features)),
        (meta, order(dz1b), h0b, kept[1][0], kept[3][0], kept[1][1], kept[3][1], kept[1][2], kept[3][2],
         starts[1], starts[3], left_up_a, left_down_a, hidden_a, first_near, *first_both),
        [SMEM] + [VMEM] * 13 + [ANY] * 3, scratch + [vm(2, all_rows, features), dma(3)],
    )
    order.mark(dh_b)
    head_in, down_in_a = order(head_in), order(down_in_a)
    first_got = core_swap(tie(first_send, down_in_a))
    both_in = chip_swap(tie(both, down_in_a))
    cols = bf(rows, columns)
    first_far_grad, first_part, pack_b, pack_a, d_far, d_near, d_own = call(
        functools.partial(attention_keep_kernel, length), "attention_keep",
        (bf(all_rows, features), shape(all_rows, features), pack, pack, pair(rows, columns, BF16), cols, cols),
        (meta, order(dz1b), h0b, kept[0][0], kept[2][0], kept[0][1], kept[2][1], kept[0][2], kept[2][2],
         starts[0], starts[2], left_up_b, left_down_b, hidden_b, first_got, err_qkv[0].T, err_out[0],
         dz1, dh_b, normed0, inverse0, vec_whole, g_vec1, g_vec2, g_bias, loss_part, pack_a,
         first_own, *first_far),
        [SMEM] + [VMEM] * 26 + [ANY] * 3,
        scratch + [pltpu.VMEM((rows, features), F32), vm(2, all_rows, features), dma(3)],
    )
    order.mark(d_far)

    d_two = chip_swap(d_far)
    both_in = order(both_in)
    mine = order(pack_b + core_swap(tie(pack_a, both_in)))
    d_one = core_swap(tie(d_near, both_in))
    mine_in = chip_swap(mine[1])
    mine = order(mine[0] + mine_in)
    panels = WholeSum(mine[:8], bits)
    panels.send()
    advance(order, panels)
    d_two = order(d_two)
    d_three = core_swap(d_two)
    up_in_b = chip_swap(tie(up_b, d_two))
    advance(order, panels)
    table_grad = call(
        functools.partial(scatter_kernel, own, vocab), "scatter", bf(columns, total),
        (ids_rows, order(d_own), d_one, d_two, d_three, head_near, head_keep, head_in),
    )
    order.mark(table_grad)
    table_sum = RowSum(table_grad, bits)
    table_sum.send()
    first_in = chip_swap(tie(first_far_grad, table_grad))
    while panels.step < len(bits):
        advance(order, panels)
    sizes = (features, features, features, width)
    bases, base_up, base_down, base_qkv, base_out = call(
        functools.partial(orthonormal_kernel, sizes), "orthonormal",
        (shape(rank, pack_width),) + tuple(shape(rank, size) for size in sizes), (order(panels.x),),
    )
    order.mark(bases)
    packed = call(
        right_mlp_kernel, "right_mlp", shape(rank, 2 * features + pack_width),
        (down_part, down_in_a, both_in, up_part, order(up_in_b), bases, mine[8:]),
    )
    order.mark(packed)
    packed = WholeSum(packed, bits[2:] + bits[:2])
    packed.send()
    advance(order, table_sum)
    advance(order, packed)
    advance(order, packed)
    advance(order, table_sum)
    while packed.step < len(bits):
        advance(order, packed)
    right_up, right_down = packed.x[:, :features], packed.x[:, features : 2 * features]
    rest = packed.x[:, 2 * features :]
    rights = call(
        functools.partial(right_attention_kernel, used), "right_attention", shape(rank, features + used),
        (first_part, order(first_in), bases),
    )
    order.mark(rights)
    rights = WholeSum(rights, bits[2:] + bits[:2])
    rights.send()
    advance(order, table_sum)
    down = update(replicas, down_part, [(down_in_a, hidden // 2, 0), (both_in, hidden // 2, 0)], 0, w_down, mom_down, order(base_down), right_down)
    order.mark(down[0])
    advance(order, rights)
    advance(order, table_sum)
    up = update(replicas, up_part, [(both_in, features // 4, 2 * hidden // features), (up_in_b, features - features // 4, 0)], 0, w_up, mom_up, order(base_up), right_up)
    order.mark(up[0])
    rest = tie(rest, up[0])
    while rights.step < len(bits):
        advance(order, rights)
    right_out, right_qkv = rights.x[:, :features], rights.x[:, features:]
    out = update(replicas, first_part, [first_in], used, w_out, mom_out, order(base_out), right_out)
    qkv = update(replicas, first_part, [first_in], 0, w_qkv.T, mom_qkv.T, right_qkv, base_qkv)
    order.mark(qkv[0])
    while table_sum.step < len(table_sum.steps):
        advance(order, table_sum)

    table_grad = table_sum.x[:, :total_rows].astype(F32)
    vectors = [rest[2 + n // 3, n % 3 * features : (n % 3 + 1) * features] for n in range(8)]
    results = [jnp.where(jnp.arange(2) == 0, rest[4, 2 * features : 2 * features + 1], count)]

    def momentum_step(weight, moment, grad, rate):
        new_moment = BETA * moment + grad
        return (weight.astype(F32) - rate * new_moment, new_moment)

    new = momentum_step(tables.T, table_mom.T, table_grad, RATE_TAB)
    results += [new[0].T, new[1].T]
    results += momentum_step(vec_whole, vec_mom, jnp.stack(vectors), RATE_VEC)
    results += momentum_step(vec_split, split_mom, rest[0:1, : vec_split.shape[1]], RATE_VEC)
    results += momentum_step(head_bias, bias_mom, rest[1, :vocab], RATE_VEC)
    one = 1.0 / replicas
    for (weight, moment, error), base, right, flip in (
        (qkv, base_qkv, right_qkv, True), (out, base_out, right_out, False),
        (up, base_up, right_up, False), (down, base_down, right_down, False),
    ):
        if flip:
            weight, moment, error = weight.T, moment.T, error.T
        results += [weight, moment, error[None], base.T[None], right.T * one]
    return tuple(results)


def solution(mesh):
    rows, cols = P("tensor", None), P(None, "tensor")
    batch = P("dp", None)
    in_specs = (
        batch, batch, P("dp"), cols, cols, P(), P(), rows, rows, P(), P(),
        cols, rows, cols, rows, cols, rows, cols, rows,
        P("dp", None, "tensor"), P("dp", "tensor", None), P("dp", None, "tensor"), P("dp", "tensor", None),
        rows, rows, rows, rows,
    )
    left = P("tensor", None, None)
    out_specs = (P(), cols, cols, P(), P(), rows, rows, P(), P())
    for side in (cols, rows, cols, rows):
        out_specs += (side, side, P("dp", *side), left, rows)
    return jax.shard_map(shards, mesh=mesh, in_specs=in_specs, out_specs=out_specs, check_vma=False)
```

```python
import functools

import jax
import jax.numpy as jnp
from jax import lax
from jax.experimental import pallas as pl
from jax.experimental.pallas import tpu as pltpu
from jax.sharding import PartitionSpec as P

HD = 48
EPSILON = 1e-05
BETA = 0.9
RATE_MAT = 100.0
RATE_VEC = 10.0
RATE_TAB = 100.0
HIGHEST = lax.Precision.HIGHEST
BF16 = jnp.bfloat16
F32 = jnp.float32
MIB = 1024 * 1024


def bdot(left, right):
    return jnp.dot(left, right, preferred_element_type=F32)


def tdot(left, right):
    return lax.dot_general(left, right, (((0,), (0,)), ((), ())), preferred_element_type=F32)


def ndot(left, right):
    return lax.dot_general(left, right, (((1,), (1,)), ((), ())), preferred_element_type=F32)


def across(x, axis, bit):
    size = lax.axis_size(axis)
    return lax.ppermute(x, axis, [(i, i ^ bit) for i in range(size)])


def core_swap(x):
    return across(x, "tensor", 1)


def chip_swap(x):
    return across(x, "tensor", 2)


def tie(x, *others):
    return lax.optimization_barrier((x,) + others)[0]


def head_mask(width, head):
    lane = lax.broadcasted_iota(jnp.int32, (1, width), 1)
    return ((lane >= head * HD) & (lane < (head + 1) * HD)).astype(BF16)


SCALE = 10.0
LIMITS = {
    "pack_first": (56, 2), "pack_rest": (50, 3), "embed": (8, 5), "attention_first": (10, 7), "attention_second": (10, 8), "mlp_first": (12, 7),
    "mlp_second": (14, 7), "head": (24, 9), "down_send": (8, 3), "down_keep": (14, 4), "up_send": (14, 6),
    "up_keep": (20, 8), "attention_send": (14, 13), "attention_keep": (20, 15), "scatter": (8, 5),
    "orthonormal": (4, 3), "right_mlp": (16, 3), "right_attention": (12, 2), "update": (16, 4),
}


def call(kernel, name, out_shape, operands, in_specs=None, scratch=(), out_specs=None, **grid):
    limit, cost = LIMITS[name]
    cost *= 1.0 if name in ("scatter", "orthonormal", "right_mlp", "right_attention", "update") else SCALE
    if in_specs is None:
        in_specs = [pl.BlockSpec(memory_space=pltpu.VMEM)] * len(operands)
    if out_specs is not None:
        grid["out_specs"] = out_specs
    return pl.pallas_call(
        kernel,
        out_shape=out_shape,
        in_specs=in_specs,
        scratch_shapes=list(scratch),
        compiler_params=pltpu.CompilerParams(vmem_limit_bytes=limit * MIB),
        cost_estimate=pl.CostEstimate(flops=int(cost * 1150000000), bytes_accessed=int(cost * 1000000), transcendentals=0),
        name=name,
        **grid,
    )(*operands)


VMEM = pl.BlockSpec(memory_space=pltpu.VMEM)
SMEM = pl.BlockSpec(memory_space=pltpu.SMEM)
ANY = pl.BlockSpec(memory_space=pltpu.HBM)


def shape(*dims, dtype=F32):
    return jax.ShapeDtypeStruct(dims, dtype)


def normalize(x):
    center = x - jnp.mean(x, -1, keepdims=True)
    inverse = lax.rsqrt(jnp.mean(center * center, -1, keepdims=True) + EPSILON)
    return center * inverse, inverse


def norm_back(normed, inverse, gain, grad):
    inner = grad * gain
    first = jnp.mean(inner, -1, keepdims=True)
    second = jnp.mean(inner * normed, -1, keepdims=True)
    d_x = inverse * (inner - first - normed * second)
    return d_x, jnp.sum(grad * normed, 0, keepdims=True), jnp.sum(grad, 0, keepdims=True)


def split3(x):
    high = x.astype(BF16).astype(F32)
    rest = x - high
    middle = rest.astype(BF16).astype(F32)
    return jnp.concatenate([high, middle, rest - middle], 0).astype(BF16)


def fold3(x):
    rank = x.shape[0] // 3
    return x[:rank] + x[rank : 2 * rank] + x[2 * rank :]


def panel(start, right, left):
    return fold3(bdot(split3(fold3(ndot(split3(start), right))), left))


def split2(x):
    high = x.astype(BF16)
    return high, (x - high.astype(F32)).astype(BF16)


def wide(dot, start, x):
    parts = split3(start)
    high, rest = split2(x)
    return fold3(dot(parts, high) + dot(parts, rest))


class Fetch:
    def __init__(self, meta_ref, sems):
        self.half, self.sems, self.used = meta_ref[1], sems, 0

    def one(self, source, target):
        copy = pltpu.make_async_copy(source, target, self.sems.at[self.used])
        self.used += 1
        copy.start()
        return copy

    def block(self, pieces, target, first=0):
        if len(pieces) == 1:
            return [self.one(pieces[0], target.at[pl.ds(first, pieces[0].shape[0]), :])]
        size = pieces[0].shape[0]
        spots = (first + self.half * size, first + (1 - self.half) * size)
        return [
            self.one(piece, target.at[pl.ds(pl.multiple_of(spot, 32), size), :])
            for piece, spot in zip(pieces, spots)
        ]


def wait(copies):
    for copy in copies:
        copy.wait()


def pack_first_kernel(meta_ref, qkv_ref, out_ref, first_ref, first_half, sems):
    near, rest = qkv_ref.shape[0], out_ref.shape[0]
    size = first_half.shape[0]
    fetch = Fetch(meta_ref, sems)
    wait([
        fetch.one(qkv_ref, first_ref.at[pl.ds(0, near), :]),
        fetch.one(out_ref, first_ref.at[pl.ds(near, rest), :]),
    ])
    first_half[...] = first_ref[pl.ds(pl.multiple_of(meta_ref[1] * size, 32), size), :]


def pack_rest_kernel(meta_ref, up_ref, down_ref, tables_ref, up_half, down_half, table_ref, table_half, sems):
    half = meta_ref[1]
    size = up_half.shape[0]
    at = pl.multiple_of(half * size, 32)
    fetch = Fetch(meta_ref, sems)
    copies = [
        fetch.one(up_ref.at[pl.ds(at, size), :], up_half),
        fetch.one(down_ref.at[pl.ds(at, size), :], down_half),
    ]
    total = tables_ref.shape[1]
    table_ref[...] = jnp.zeros_like(table_ref)
    table_ref[:, :total] = tables_ref[...]
    rows = table_half.shape[0]
    table_half[...] = table_ref[pl.ds(pl.multiple_of(half * rows, 32), rows), :]
    wait(copies)


def embed_kernel(own, vocab, meta_ref, live_ref, ids_ref, slots_ref, table_ref, far_ref, near_ref, own_ref, rows_ref):
    images, length = ids_ref.shape
    slot_count = slots_ref.shape[1]
    total = table_ref.shape[1]
    member = meta_ref[0]
    ids_t = jnp.transpose(ids_ref[...].astype(F32))
    image_lane = lax.broadcasted_iota(jnp.int32, (length, images), 1)
    position = lax.broadcasted_iota(jnp.int32, (length, 1), 0)
    slot_lane = lax.broadcasted_iota(jnp.int32, (1, slot_count), 1)
    table_lane = lax.broadcasted_iota(jnp.int32, (1, total), 1)
    table = table_ref[...]

    def rows_of(ids):
        hot = jnp.where(ids == table_lane, 1.0, 0.0).astype(BF16)
        return ndot(table, hot).astype(BF16)

    targets = {
        0: (own_ref, 0), 1: (near_ref, 0), 2: (far_ref.at[0], 0), 3: (far_ref.at[1], 0),
    }
    for k in range(4):
        for i in range(own):
            image = (member ^ k) * own + i
            hit = (slots_ref[pl.ds(image, 1), :] == position) & (slot_lane < live_ref[image])
            masked = jnp.max(jnp.where(hit, 1.0, 0.0), 1, keepdims=True)
            ids = jnp.sum(jnp.where(image_lane == image, ids_t, 0.0), 1, keepdims=True)
            ids = jnp.where(masked > 0, float(vocab - 1), ids).astype(jnp.int32)
            place = k * own + i
            rows_ref[:, place : place + 1] = ids
            ref, first = targets[k]
            ref[:, first + i * length : first + (i + 1) * length] = rows_of(ids)
    at = rows_of(position + vocab)
    own_ref[:, own * length :] = at
    near_ref[:, own * length :] = at
    far_ref[0, :, own * length :] = at[:, : length // 2]
    far_ref[1, :, own * length :] = at[:, length // 2 :]


def attention_one(length, hb, w, bias_ref, qkv_ref, lse_ref, ctx_ref):
    width = ctx_ref.shape[1]
    mixed = ndot(hb, w)
    first = bias_ref.shape[1] - 6 * width
    q_bias = bias_ref[0:1, first : first + width]
    v_bias = bias_ref[0:1, first + width : first + 2 * width]
    qkv_ref[0] = ((mixed[:, :width] + q_bias) * HD ** (-0.5)).astype(BF16)
    qkv_ref[1] = mixed[:, width : 2 * width].astype(BF16)
    qkv_ref[2] = (mixed[:, 2 * width :] + v_bias).astype(BF16)
    for image in range(hb.shape[0] // length):
        rows = slice(image * length, (image + 1) * length)
        q, k, v = qkv_ref[0, rows, :], qkv_ref[1, rows, :], qkv_ref[2, rows, :]
        total = jnp.zeros((length, width), F32)
        for head in range(width // HD):
            mask = head_mask(width, head)
            scores = ndot(q * mask, k)
            top = jnp.max(scores, -1, keepdims=True)
            powers = jnp.exp(scores - top)
            weight = jnp.sum(powers, -1, keepdims=True)
            lse_ref[rows, head : head + 1] = top + jnp.log(weight)
            probs = (powers * (1.0 / weight)).astype(BF16)
            total = total + bdot(probs, v * mask)
        ctx_ref[rows, :] = total.astype(BF16)


def attention_first_kernel(
    length, meta_ref, e0, e1, e2, e3, vec_ref, b0, b1, c0, c1,
    normed_ref, inverse_ref, hb_ref, qkv0, lse0, ctx0, qkv1, lse1, ctx1, x_ref, w_ref, sems,
):
    rows, width = hb_ref.shape[0], e0.shape[0]
    member = meta_ref[0]
    fetch = Fetch(meta_ref, sems)
    used = 3 * width
    zero = fetch.one(c0.at[pl.ds(0, used), :], w_ref.at[0])
    one = fetch.one(c1.at[pl.ds(0, used), :], w_ref.at[1])
    slabs = ((e0, e0, e0), (e1, e1, e1), (e2.at[0], e2.at[0], e2.at[1]), (e3.at[1], e3.at[0], e3.at[1]))
    for k, (ref, low, high) in enumerate(slabs):
        at = low[:, rows:] if low is high else jnp.concatenate([low[:, rows:], high[:, rows:]], 1)
        at = at.astype(F32)
        place = pl.ds(pl.multiple_of((member ^ k) * width, 64), width)
        for i in range(rows // length):
            x_ref[place, i * length : (i + 1) * length] = ref[:, i * length : (i + 1) * length].astype(F32) + at
    normed, inverse = normalize(jnp.transpose(x_ref[...]))
    normed_ref[...] = normed
    inverse_ref[...] = inverse
    hb_ref[...] = (normed * vec_ref[0:1, :] + vec_ref[1:2, :]).astype(BF16)
    hb = hb_ref[...]
    zero.wait()
    attention_one(length, hb, w_ref[0], b0, qkv0, lse0, ctx0)
    one.wait()
    attention_one(length, hb, w_ref[1], b1, qkv1, lse1, ctx1)


def attention_second_kernel(
    length, meta_ref, normed_ref, hb_ref, vec_ref, b2, b3, ctx0, ctx1, c0, c1, c2a, c2b, c3a, c3b,
    normed1_ref, inverse1_ref, h1b_ref, qkv2, lse2, ctx2, qkv3, lse3, ctx3, w_ref, o_ref, sems,
):
    hb = hb_ref[...]
    width = ctx0.shape[1]
    used = 3 * width
    fetch = Fetch(meta_ref, sems)
    two = fetch.block((c2a, c2b), w_ref.at[0])
    three = fetch.block((c3a, c3b), w_ref.at[1])
    others = [fetch.one(c.at[pl.ds(used, width), :], o_ref.at[n]) for n, c in enumerate((c0, c1))]
    wait(two)
    attention_one(length, hb, w_ref[0, :used, :], b2, qkv2, lse2, ctx2)
    wait(three)
    attention_one(length, hb, w_ref[1, :used, :], b3, qkv3, lse3, ctx3)
    wait(others)
    total = bdot(ctx0[...], o_ref[0]) + bdot(ctx1[...], o_ref[1])
    total = total + bdot(ctx2[...], w_ref[0, used:, :]) + bdot(ctx3[...], w_ref[1, used:, :])
    z_one = normed_ref[...] * vec_ref[0:1, :] + vec_ref[1:2, :] + (total + vec_ref[2:3, :])
    normed, inverse = normalize(z_one)
    normed1_ref[...] = normed
    inverse1_ref[...] = inverse
    h1b_ref[...] = (normed * vec_ref[3:4, :] + vec_ref[4:5, :]).astype(BF16)


def gelu_pair(x):
    inner = 0.7978845608028654 * x * (1.0 + 0.044715 * x * x)
    curve = jnp.tanh(inner)
    value = 0.5 * x * (1.0 + curve)
    slope = 0.5 * (1.0 + curve) + 0.5 * x * (1.0 - curve * curve) * (
        0.7978845608028654 * (1.0 + 3 * 0.044715 * x * x)
    )
    return value, slope


def mlp_one(h1b, up_ref, bias_ref, active_ref, slope_ref):
    first = bias_ref.shape[1] - up_ref.shape[1]
    step = 256
    for at in range(0, up_ref.shape[1], step):
        pre = bdot(h1b, up_ref[:, at : at + step]) + bias_ref[0:1, first + at : first + at + step]
        value, slope = gelu_pair(pre)
        active_ref[:, at : at + step] = value.astype(BF16)
        slope_ref[:, at : at + step] = slope


def mlp_first_kernel(meta_ref, h1b_ref, b0, b1, u0, u1, d0, d1, a0, a1, s0, s1, low_ref, w_ref, sems):
    fetch = Fetch(meta_ref, sems)
    copies = [fetch.one(ref, w_ref.at[n]) for n, ref in enumerate((u0, d0, u1, d1))]
    h1b = h1b_ref[...]
    copies[0].wait()
    mlp_one(h1b, w_ref.at[0], b0, a0, s0)
    copies[1].wait()
    low_ref[...] = bdot(a0[...], w_ref[1])
    copies[2].wait()
    mlp_one(h1b, w_ref.at[2], b1, a1, s1)
    copies[3].wait()
    low_ref[...] += bdot(a1[...], w_ref[3])


def mlp_second_kernel(
    meta_ref, h1b_ref, b2, b3, low_ref, normed1_ref, vec_ref, u2a, u2b, u3a, u3b, d2a, d2b, d3a, d3b,
    a2, a3, s2, s3, normed2_ref, inverse2_ref, h2b_ref, w_ref, sems,
):
    fetch = Fetch(meta_ref, sems)
    pieces = ((u2a, u2b), (d2a, d2b), (u3a, u3b), (d3a, d3b))
    copies = [fetch.block(piece, w_ref.at[n]) for n, piece in enumerate(pieces)]
    h1b = h1b_ref[...]
    wait(copies[0])
    mlp_one(h1b, w_ref.at[0], b2, a2, s2)
    wait(copies[1])
    normed2_ref[...] = low_ref[...] + bdot(a2[...], w_ref[1])
    wait(copies[2])
    mlp_one(h1b, w_ref.at[2], b3, a3, s3)
    wait(copies[3])
    total = normed2_ref[...] + bdot(a3[...], w_ref[3]) + vec_ref[5:6, :]
    normed, inverse = normalize(normed1_ref[...] * vec_ref[3:4, :] + vec_ref[4:5, :] + total)
    normed2_ref[...] = normed
    inverse2_ref[...] = inverse
    h2b_ref[...] = (normed * vec_ref[6:7, :] + vec_ref[7:8, :]).astype(BF16)


def head_kernel(
    own, vocab, meta_ref, live_ref, count_ref, ids_ref, slots_ref, bias_ref, vec_ref,
    h2b_ref, normed2_ref, inverse2_ref, t0, t1, t2a, t2b, t3a, t3b,
    dz_ref, dzb_ref, loss_ref, gbias_ref, gvec_ref, send_ref, keep_ref,
    table_ref, full_ref, grad_ref, sems,
):
    images, length = ids_ref.shape
    slot_count = slots_ref.shape[1]
    total = bias_ref.shape[1]
    member = meta_ref[0]
    columns = t0.shape[0]
    fetch = Fetch(meta_ref, sems)
    copies = []
    for k, pieces in enumerate(((t0,), (t1,), (t2a, t2b), (t3a, t3b))):
        copies += fetch.block(pieces, table_ref, pl.multiple_of((member ^ k) * columns, 64))
    slots_t = jnp.transpose(slots_ref[...].astype(F32))
    image_lane = lax.broadcasted_iota(jnp.int32, (slot_count, images), 1)
    slot_row = lax.broadcasted_iota(jnp.int32, (slot_count, 1), 0)
    position = lax.broadcasted_iota(jnp.int32, (1, length), 1).astype(F32)
    picks, targets, weights, picked = [], [], [], []
    for i in range(own):
        image = member * own + i
        at = jnp.sum(jnp.where(image_lane == image, slots_t, 0.0), 1, keepdims=True)
        hit = at == position
        ids = ids_ref[pl.ds(image, 1), :].astype(F32)
        targets.append(jnp.sum(jnp.where(hit, ids, 0.0), 1, keepdims=True).astype(jnp.int32))
        weights.append(jnp.where(slot_row < live_ref[image], 1.0, 0.0))
        picks.append(jnp.where(hit, 1.0, 0.0).astype(BF16))
        picked.append(bdot(picks[i], h2b_ref[i * length : (i + 1) * length, :]).astype(BF16))
    target = jnp.concatenate(targets, 0)
    weight = jnp.concatenate(weights, 0)
    rows = jnp.concatenate(picked, 0)
    wait(copies)
    lane = lax.broadcasted_iota(jnp.int32, (1, total), 1)
    logits = bdot(rows, table_ref[...]) + bias_ref[...]
    logits = jnp.where(lane < vocab, logits, -1e30)
    top = jnp.max(logits, -1, keepdims=True)
    log_total = top + jnp.log(jnp.sum(jnp.exp(logits - top), -1, keepdims=True))
    hot = jnp.where(lane == target, 1.0, 0.0)
    chosen = jnp.sum(hot * logits, -1, keepdims=True)
    loss_ref[...] = jnp.broadcast_to(jnp.sum(weight * (log_total - chosen), 0, keepdims=True), loss_ref.shape)
    d_logits = (jnp.exp(logits - log_total) - hot) * (weight / count_ref[0])
    gbias_ref[...] = jnp.sum(d_logits, 0, keepdims=True)
    dl = d_logits.astype(BF16)
    d_rows = ndot(dl, table_ref[...])
    high = d_rows.astype(BF16)
    rest = (d_rows - high.astype(F32)).astype(BF16)
    for i in range(own):
        part = slice(i * slot_count, (i + 1) * slot_count)
        grad_ref[i * length : (i + 1) * length, :] = tdot(picks[i], high[part]) + tdot(picks[i], rest[part])
    d_z2, d_gain, d_shift = norm_back(normed2_ref[...], inverse2_ref[...], vec_ref[6:7, :], grad_ref[...])
    dz_ref[...] = d_z2
    dzb_ref[...] = d_z2.astype(BF16)
    gvec_ref[0:1, :] = jnp.sum(d_z2, 0, keepdims=True)
    gvec_ref[1:2, :] = d_gain
    gvec_ref[2:3, :] = d_shift
    full_ref[...] = tdot(rows, dl).astype(BF16)
    for k, out in enumerate((keep_ref.at[0], send_ref.at[0], keep_ref.at[1], send_ref.at[1])):
        out[...] = full_ref[pl.ds(pl.multiple_of((member ^ k) * columns, 64), columns), :]


def down_send_kernel(dzb_ref, a1, a3, s1, s3, send_ref, left_ref):
    first = dzb_ref.shape[1]
    dzb = dzb_ref[...]
    for n, (active, start) in enumerate(((a1[...], s1), (a3[...], s3))):
        send_ref[n] = tdot(active, dzb).astype(BF16)
        left_ref[n] = panel(start[:8, first : 2 * first], dzb, active)


def close(n, grad, near_ref, err_ref, far_refs, part_ref):
    if n == 0:
        part_ref[...] = grad + near_ref[0].astype(F32) + err_ref[...]
    else:
        total = (grad + near_ref[1].astype(F32)).astype(BF16)
        first = 0
        for far_ref in far_refs:
            far_ref[...] = total[first : first + far_ref.shape[0]]
            first += far_ref.shape[0]


def down_keep_kernel(dzb_ref, a0, a2, s0, s2, near_ref, err_ref, far_a, far_b, part_ref, left_ref):
    first = dzb_ref.shape[1]
    dzb = dzb_ref[...]
    for n, (active, start) in ((1, (a2[...], s2)), (0, (a0[...], s0))):
        close(n, tdot(active, dzb), near_ref, err_ref, (far_a, far_b), part_ref)
        left_ref[n] = panel(start[:8, first : 2 * first], dzb, active)
    left_ref[0] += wide(ndot, s0[:8, first : 2 * first], err_ref[...])


def up_one(dzb, h1b, slope, up, down, start, hidden_ref, dpre_ref):
    step = 256
    for at in range(0, down.shape[0], step):
        d_pre = ndot(dzb, down[at : at + step, :]) * slope[:, at : at + step]
        hidden_ref[:, at : at + step] = jnp.sum(d_pre, 0, keepdims=True)
        dpre_ref[:, at : at + step] = d_pre.astype(BF16)
    d_pre = dpre_ref[...]
    return tdot(h1b, d_pre), ndot(d_pre, up[...]), panel(start[:8, : d_pre.shape[1]], d_pre, h1b)


def up_send_kernel(
    meta_ref, dzb_ref, h1b_ref, p1, p3, s1, s3, u1, u3a, u3b, d1, d3a, d3b,
    send_ref, left_ref, dh_ref, hidden_ref, dpre_ref, w_ref, sems,
):
    fetch = Fetch(meta_ref, sems)
    pieces = ((d1,), (u1,), (d3a, d3b), (u3a, u3b))
    copies = [fetch.block(piece, w_ref.at[n]) for n, piece in enumerate(pieces)]
    dzb, h1b = dzb_ref[...], h1b_ref[...]
    for n, (slope, start) in enumerate(((p1, s1), (p3, s3))):
        wait(copies[2 * n] + copies[2 * n + 1])
        grad, part, left_ref[n] = up_one(
            dzb, h1b, slope, w_ref.at[2 * n + 1], w_ref.at[2 * n], start, hidden_ref.at[n], dpre_ref
        )
        send_ref[n] = grad.astype(BF16)
        dh_ref[...] = part if n == 0 else dh_ref[...] + part


def up_keep_kernel(
    meta_ref, dz_ref, dzb_ref, h1b_ref, normed1_ref, inverse1_ref, vec_ref, dh_ref, p0, p2, s0, s2,
    near_ref, err_ref, other_ref, u0, u2a, u2b, d0, d2a, d2b,
    far_a, far_b, part_ref, left_ref, dz1_ref, dz1b_ref, gvec_ref, hidden_ref, dpre_ref, w_ref, sems,
):
    other = other_ref.shape[0]
    far_a[:other, :] = other_ref[...]
    fetch = Fetch(meta_ref, sems)
    pieces = ((d0,), (u0,), (d2a, d2b), (u2a, u2b))
    copies = [fetch.block(piece, w_ref.at[n]) for n, piece in enumerate(pieces)]
    dzb, h1b = dzb_ref[...], h1b_ref[...]
    for n, (slope, start) in ((1, (p2, s2)), (0, (p0, s0))):
        wait(copies[2 * n] + copies[2 * n + 1])
        grad, part, left_ref[n] = up_one(
            dzb, h1b, slope, w_ref.at[2 * n + 1], w_ref.at[2 * n], start, hidden_ref.at[n], dpre_ref
        )
        close(n, grad, near_ref, err_ref, (far_a.at[pl.ds(other, far_a.shape[0] - other), :], far_b), part_ref)
        dz1_ref[...] = part + (dz_ref[...] + dh_ref[...] if n == 1 else dz1_ref[...])
    left_ref[0] += wide(ndot, s0[:8, : err_ref.shape[1]], err_ref[...])
    d_z1, d_gain, d_shift = norm_back(normed1_ref[...], inverse1_ref[...], vec_ref[3:4, :], dz1_ref[...])
    dz1_ref[...] = d_z1
    dz1b_ref[...] = d_z1.astype(BF16)
    gvec_ref[0:1, :] = jnp.sum(d_z1, 0, keepdims=True)
    gvec_ref[1:2, :] = d_gain
    gvec_ref[2:3, :] = d_shift


def attention_back_one(length, dz, hb, w_ref, qkv_ref, lse_ref, ctx_ref, start_ref, pack_ref, dm_ref, dc_ref):
    width, features = ctx_ref.shape[1], dz.shape[1]
    used = 3 * width
    dc_ref[...] = ndot(dz, w_ref[used:, :]).astype(BF16)
    ctx = ctx_ref[...]
    out_grad = tdot(ctx, dz)
    pack_ref[:8, 3 * features :] = panel(start_ref[:8, 2 * features : 3 * features], dz, ctx)
    q_sum = jnp.zeros((1, width), F32)
    v_sum = jnp.zeros((1, width), F32)
    for image in range(dz.shape[0] // length):
        rows = slice(image * length, (image + 1) * length)
        q, k, v, dc = qkv_ref[0, rows, :], qkv_ref[1, rows, :], qkv_ref[2, rows, :], dc_ref[rows, :]
        d_query = jnp.zeros((length, width), F32)
        d_key = jnp.zeros((length, width), F32)
        d_value = jnp.zeros((length, width), F32)
        for head in range(width // HD):
            mask = head_mask(width, head)
            q_head, k_head, c_head = q * mask, k * mask, dc * mask
            probs = jnp.exp(ndot(q_head, k) - lse_ref[rows, head : head + 1])
            d_value = d_value + tdot(probs.astype(BF16), c_head)
            d_probs = ndot(c_head, v)
            inner = jnp.sum(d_probs * probs, -1, keepdims=True)
            d_scores = (probs * (d_probs - inner)).astype(BF16)
            d_query = d_query + bdot(d_scores, k_head)
            d_key = d_key + tdot(d_scores, q_head)
        d_query = d_query * HD ** (-0.5)
        q_sum = q_sum + jnp.sum(d_query, 0, keepdims=True)
        v_sum = v_sum + jnp.sum(d_value, 0, keepdims=True)
        dm_ref[rows, :width] = d_query.astype(BF16)
        dm_ref[rows, width : 2 * width] = d_key.astype(BF16)
        dm_ref[rows, 2 * width :] = d_value.astype(BF16)
    pack_ref[8:9, :width] = q_sum
    pack_ref[8:9, width : 2 * width] = v_sum
    dm = dm_ref[...]
    pack_ref[:8, 2 * features : 3 * features] = panel(start_ref[:8, 3 * features : 3 * features + dm_ref.shape[1]], dm, hb)
    return tdot(dm, hb), out_grad, bdot(dm, w_ref[:used, :])


def pack_rows(pack_ref, width, up, down, hidden):
    features = up.shape[1]
    pack_ref[...] = jnp.zeros_like(pack_ref)
    pack_ref[:8, :features] = up
    pack_ref[:8, features : 2 * features] = down
    pack_ref[8:9, 2 * width : 2 * width + features] = hidden


def pack_whole(pack_ref, vectors, bias, loss):
    pack_ref[9:10, : bias.shape[1]] = bias
    features = vectors[0].shape[1]
    for n, vector in enumerate(vectors + [loss]):
        row, place = 10 + n // 3, n % 3
        pack_ref[row : row + 1, place * features : place * features + vector.shape[1]] = vector


def attention_send_kernel(
    length, meta_ref, dz1b_ref, hb_ref, q1, q3, l1, l3, x1, x3, s1, s3, up_ref, down_ref, hidden_ref,
    c1, c3a, c3b, send_ref, pack_ref, dh_ref, dm_ref, dc_ref, w_ref, sems,
):
    fetch = Fetch(meta_ref, sems)
    copies = [fetch.block((c1,), w_ref.at[0]), fetch.block((c3a, c3b), w_ref.at[1])]
    dz, hb = dz1b_ref[...], hb_ref[...]
    used = dm_ref.shape[1]
    for n, (q, l, x, start) in enumerate(((q1, l1, x1, s1), (q3, l3, x3, s3))):
        wait(copies[n])
        pack_rows(pack_ref.at[n], x.shape[1], up_ref[n], down_ref[n], hidden_ref[n])
        qkv_grad, out_grad, part = attention_back_one(
            length, dz, hb, w_ref.at[n], q, l, x, start, pack_ref.at[n], dm_ref, dc_ref
        )
        send_ref[n, :used, :] = qkv_grad.astype(BF16)
        send_ref[n, used:, :] = out_grad.astype(BF16)
        dh_ref[...] = part if n == 0 else dh_ref[...] + part


def attention_keep_kernel(
    length, meta_ref, dz1b_ref, hb_ref, q0, q2, l0, l2, x0, x2, s0, s2, up_ref, down_ref, hidden_ref,
    near_ref, err_qkv, err_out, dz1_ref, dha_ref, normed_ref, inverse_ref, vec_ref, gvec1_ref, gvec2_ref, gbias_ref,
    loss_ref, send_pack_ref, c0, c2a, c2b,
    far_ref, part_ref, pack_ref, send_ref, d_far, d_near, d_own, dm_ref, dc_ref, dh_ref, w_ref, sems,
):
    fetch = Fetch(meta_ref, sems)
    copies = [fetch.block((c0,), w_ref.at[0]), fetch.block((c2a, c2b), w_ref.at[1])]
    dz, hb = dz1b_ref[...], hb_ref[...]
    used, width = dm_ref.shape[1], x0.shape[1]
    features = hb.shape[1]
    for n, (q, l, x, start) in ((1, (q2, l2, x2, s2)), (0, (q0, l0, x0, s0))):
        wait(copies[n])
        pack_rows(pack_ref.at[n], width, up_ref[n], down_ref[n], hidden_ref[n])
        qkv_grad, out_grad, part = attention_back_one(
            length, dz, hb, w_ref.at[n], q, l, x, start, pack_ref.at[n], dm_ref, dc_ref
        )
        if n == 0:
            part_ref[:used, :] = qkv_grad + near_ref[0, :used, :].astype(F32) + err_qkv[...]
            part_ref[used:, :] = out_grad + near_ref[0, used:, :].astype(F32) + err_out[...]
        else:
            far_ref[:used, :] = (qkv_grad + near_ref[1, :used, :].astype(F32)).astype(BF16)
            far_ref[used:, :] = (out_grad + near_ref[1, used:, :].astype(F32)).astype(BF16)
        dh_ref[...] = part + (dha_ref[...] + dz1_ref[...] if n == 1 else dh_ref[...])
    pack_ref[0, :8, 2 * features : 3 * features] += wide(bdot, s0[:8, 3 * features : 3 * features + used], err_qkv[...])
    pack_ref[0, :8, 3 * features :] += wide(ndot, s0[:8, 2 * features : 3 * features], err_out[...])
    d_x, d_gain, d_shift = norm_back(normed_ref[...], inverse_ref[...], vec_ref[0:1, :], dh_ref[...])
    vectors = [d_gain, d_shift] + [gvec1_ref[i : i + 1, :] for i in range(3)] + [gvec2_ref[i : i + 1, :] for i in range(3)]
    send_ref[...] = send_pack_ref[...]
    for ref in (send_ref.at[0], send_ref.at[1], pack_ref.at[0], pack_ref.at[1]):
        pack_whole(ref, vectors, gbias_ref[...], loss_ref[...])
    dh_ref[...] = d_x
    rows, columns = d_own.shape
    for t in range(4):

        @pl.when(meta_ref[0] == t)
        def _():
            for k, out in enumerate((d_own, d_near, d_far.at[0], d_far.at[1])):
                out[...] = dh_ref[:, (t ^ k) * columns : ((t ^ k) + 1) * columns].astype(BF16)


def scatter_kernel(own, vocab, ids_ref, r0, r1, r2, r3, near_ref, keep_ref, far_ref, out_ref):
    length = ids_ref.shape[0]
    total = out_ref.shape[1]
    lane = lax.broadcasted_iota(jnp.int32, (1, total), 1)
    position = lax.broadcasted_iota(jnp.int32, (length, 1), 0) + vocab
    result = keep_ref[0].astype(F32) + near_ref[0].astype(F32) + far_ref[...].astype(F32)
    for k, rows in enumerate((r0[...], r1[...], r2[0], r3[1])):
        hots = []
        for i in range(own):
            ids = ids_ref[:, k * own + i : k * own + i + 1]
            hots.append(jnp.where((ids == lane) | (position == lane), 1.0, 0.0).astype(BF16))
        result = result + tdot(rows, jnp.concatenate(hots, 0))
    out_ref[...] = result.astype(out_ref.dtype)


def joined(refs):
    parts = [ref[...].astype(F32) for ref in refs]
    return parts[0] if len(parts) == 1 else jnp.concatenate(parts, 0)


def right_mlp_kernel(part_d, got_c, both, part_u, got_b, base_ref, rest_ref, out_ref):
    size = part_d.shape[1]
    rows = part_d.shape[0]
    rest = rows - got_c.shape[0]
    got_d, got_a = both.at[pl.ds(0, rest), :], both.at[pl.ds(rest, both.shape[0] - rest), :]
    for n, (part, gots) in enumerate(((part_u, (got_a, got_b)), (part_d, (got_c, got_d)))):
        merged = part[...] + joined(gots)
        out_ref[:, n * size : (n + 1) * size] = wide(bdot, base_ref[:, n * rows : (n + 1) * rows], merged)
    out_ref[:, 2 * size :] = rest_ref[...]


def right_attention_kernel(used, part, got, base_ref, out_ref):
    features = part.shape[1]
    out_ref[:, :features] = wide(bdot, base_ref[:, 3 * features :], part[used:, :] + got[used:, :].astype(F32))
    merged = part[:used, :] + got[:used, :].astype(F32)
    out_ref[:, features:] = wide(ndot, base_ref[:, 2 * features : 3 * features], merged)


def update_kernel(replicas, part, weight, moment, first_ref, second_ref, *refs):
    gots, (weight_new, moment_new, error_new) = refs[:-3], refs[-3:]
    first, second = split3(first_ref[...] * (1.0 / replicas)), split3(second_ref[...])
    rank = first.shape[0] // 3
    parts = lambda x, order: jnp.concatenate([x[i * rank : (i + 1) * rank].astype(F32) for i in order], 0).astype(BF16)
    approx = tdot(parts(first, (0, 0, 1, 0, 2, 1)), parts(second, (0, 1, 0, 2, 0, 1)))
    new = BETA * moment[...] + approx
    moment_new[...] = new
    weight_new[...] = weight[...].astype(F32) - RATE_MAT * new
    error_new[...] = part[...] + joined(gots) - approx


def update(replicas, part, gots, first_row, weight, moment, first, second):
    rows, cols = weight.shape
    block = 256
    spec = pl.BlockSpec((rows, block), lambda i: (0, i))
    out = shape(rows, cols)
    mine = lambda size: pl.BlockSpec((size, block), lambda i: (first_row // size, i))
    rows_of = lambda size, first: pl.BlockSpec((size, block), lambda i: (first, i))
    own = [mine(rows)] if len(gots) == 1 else [rows_of(*got[1:]) for got in gots]
    gots = gots if len(gots) == 1 else [got[0] for got in gots]
    return call(
        functools.partial(update_kernel, replicas), "update", (out, out, out),
        (part, weight, moment, first, second, *gots),
        [mine(rows), spec, spec, pl.BlockSpec(first.shape, lambda i: (0, 0)),
         pl.BlockSpec((second.shape[0], block), lambda i: (0, i))] + own,
        out_specs=[spec] * 3, grid=(cols // block,),
    )


def orthonormal_kernel(sizes, panel_ref, out_ref, *outs):
    rank = panel_ref.shape[0]
    place = lax.broadcasted_iota(jnp.int32, (rank, 1), 0)
    cuts = [sum(sizes[:i]) for i in range(len(sizes) + 1)]
    panels = [panel_ref[:, a:b] for a, b in zip(cuts, cuts[1:])]
    for number in range(rank):
        for which, (a, b) in enumerate(zip(cuts, cuts[1:])):
            part = panels[which]
            column = part[number : number + 1, :]
            column = column * lax.rsqrt(jnp.sum(column * column, -1, keepdims=True) + 1e-20)
            out_ref[number : number + 1, a:b] = column
            outs[which][number : number + 1, :] = column
            if number + 1 < rank:
                along = jnp.sum(part * column, -1, keepdims=True)
                panels[which] = part - jnp.where(place > number, along, 0.0) * column


class Order:
    def __init__(self):
        self.last = None

    def __call__(self, x):
        if self.last is not None:
            x = tie(x, self.last)
        self.last = x
        return x

    def mark(self, x):
        self.last = x


def exchange(x, bit):
    return across(x, "dp", bit)


class RowSum:
    def __init__(self, x, bits):
        self.x, self.bits, self.step = x, bits, 0
        self.steps = bits[:2] + bits[2:] + bits[1::-1]
        self.place = lax.axis_index("dp")

    def send(self):
        step, bit, x = self.step, self.steps[self.step], self.x
        self.upper = (self.place & bit) != 0
        if step < 2:
            half = x.shape[0] // 2
            x = jnp.where(self.upper, x[:half], x[half:])
        self.got = across(x, "dp", bit)

    def receive(self, order):
        step, x, upper = self.step, self.x, self.upper
        got = order(self.got)
        if step < 2:
            half = x.shape[0] // 2
            x = (jnp.where(upper, x[half:], x[:half]).astype(F32) + got.astype(F32)).astype(BF16)
        elif step < len(self.bits):
            x = (x.astype(F32) + got.astype(F32)).astype(BF16)
        else:
            x = jnp.concatenate([jnp.where(upper, got, x), jnp.where(upper, x, got)], 0)
        self.x = x
        self.step += 1
        return self.step < len(self.steps)


class WholeSum:
    def __init__(self, x, bits):
        self.x, self.steps, self.step = x, bits, 0

    def send(self):
        self.got = across(self.x, "dp", self.steps[self.step])

    def receive(self, order):
        self.x = self.x + order(self.got)
        self.step += 1
        return self.step < len(self.steps)


def advance(order, *sums):
    for one in sums:
        if one.step < len(one.steps) and one.receive(order):
            one.send()


def shards(
    token_ids, masked_at, live_counts, tables, table_mom, vec_whole, vec_mom, vec_split, split_mom,
    head_bias, bias_mom, w_qkv, w_out, w_up, w_down, mom_qkv, mom_out, mom_up, mom_down,
    err_qkv, err_out, err_up, err_down, start_qkv, start_out, start_up, start_down,
):
    groups = lax.axis_size("tensor")
    replicas = lax.axis_size("dp")
    images, length = token_ids.shape
    vocab = head_bias.shape[0]
    total_rows, columns = tables.shape
    features = w_qkv.shape[0]
    width = w_qkv.shape[1] // 3
    hidden = w_up.shape[1]
    own = images // groups
    rows = own * length
    rank = start_qkv.shape[1]
    total = total_rows + -total_rows % 128
    used = 3 * width
    all_rows = used + width
    bits = [1 << i for i in range(replicas.bit_length() - 1)]
    meta = jnp.stack([lax.axis_index("tensor"), lax.axis_index("dp") & 1]).astype(jnp.int32)
    order = Order()

    bf = functools.partial(shape, dtype=BF16)
    dma = lambda n: pltpu.SemaphoreType.DMA((n,))
    vm = lambda *dims: pltpu.VMEM(dims, BF16)

    def cores(pieces):
        return tuple(core_swap(piece) for piece in pieces)

    first_own, first_half = call(
        pack_first_kernel, "pack_first", (bf(all_rows, features), bf(all_rows // 2, features)),
        (meta, w_qkv.T, w_out), [SMEM] + [ANY] * 2, [dma(2)],
    )
    order.mark(first_half)
    up_half, down_half, table_own, table_half = call(
        pack_rest_kernel, "pack_rest",
        (bf(features // 2, hidden), bf(hidden // 2, features), bf(columns, total), bf(columns // 2, total)),
        (order(meta), w_up, w_down, tables.T), [SMEM] + [ANY] * 2 + [VMEM], [dma(2)],
    )
    order.mark(table_half)
    first_far = [chip_swap(first_half)]
    part = bf(columns, rows + length)
    e_far, e_near, e_own, ids_rows = call(
        functools.partial(embed_kernel, own, vocab), "embed",
        (bf(2, columns, rows + length // 2), part, part, shape(length, images, dtype=jnp.int32)),
        (meta, live_counts, token_ids, masked_at, order(table_own)), [SMEM, SMEM, VMEM, VMEM, VMEM],
    )
    order.mark(e_far)
    first_near, up_near, down_near, table_near = cores((first_own, w_up, w_down, table_own))
    own_starts = jnp.concatenate((start_up.T, start_down.T, start_out.T, start_qkv.T), 1)
    gap = -own_starts.shape[1] % 128
    bias_row = jnp.pad(vec_split, ((0, rank - 1), (gap, 0)))
    small = [jnp.concatenate([own_starts, bias_row], 1)]
    small.append(core_swap(small[0]))
    e_one = core_swap(e_near)
    e_two = chip_swap(e_far)
    first_far[0] = order(first_far[0])
    first_far.append(exchange(first_far[0], 1))
    count = WholeSum(tie(jnp.broadcast_to(jnp.sum(live_counts).astype(F32), (8, 128)), first_far[0]), bits)
    count.send()
    e_two = order(e_two)
    up_far = [chip_swap(tie(up_half, e_two))]
    small.append(chip_swap(tie(small[0], e_two)))
    e_three = core_swap(e_two)
    advance(order, count)
    starts = splits = small

    state = (shape(rows, features), shape(rows, 1), bf(rows, features))
    block = (bf(3, rows, width), shape(rows, width // HD), bf(rows, width))
    res = call(
        functools.partial(attention_first_kernel, length), "attention_first", state + block + block,
        (tie(meta, up_near, down_near, first_near, table_near), order(e_own), e_one, e_two, e_three, vec_whole,
         small[0], small[1], first_own, first_near),
        [SMEM] + [VMEM] * 7 + [ANY] * 2, [pltpu.VMEM((features, rows), F32), vm(2, used, features), dma(2)],
    )
    normed0, inverse0, h0b = res[:3]
    order.mark(h0b)
    kept = [res[3:6], res[6:9]]
    small[2] = order(small[2])
    first_far[1] = order(first_far[1])
    first_both = cores([tie(x, first_far[1]) for x in first_far])
    small.append(core_swap(small[2]))
    up_far[0] = order(up_far[0])
    down_far = [chip_swap(tie(down_half, up_far[0]))]
    up_far.append(exchange(up_far[0], 1))
    advance(order, count)
    res = call(
        functools.partial(attention_second_kernel, length), "attention_second", state + block + block,
        (meta, order(normed0), h0b, vec_whole, splits[2], splits[3], kept[0][2], kept[1][2], first_own, first_near,
         *first_far, *first_both),
        [SMEM] + [VMEM] * 7 + [ANY] * 6, [vm(2, all_rows, features), vm(2, width, features), dma(6)],
    )
    normed1, inverse1, h1b = res[:3]
    order.mark(h1b)
    kept += [res[3:6], res[6:9]]
    while count.step < len(bits):
        advance(order, count)
    down_far[0] = order(down_far[0])
    down_far.append(exchange(down_far[0], 1))
    table_far = [chip_swap(tie(table_half, down_far[0]))]
    act = bf(rows, hidden)
    slope = shape(rows, hidden)
    a0, a1, p0, p1, low = call(
        mlp_first_kernel, "mlp_first", (act, act, slope, slope, shape(rows, features)),
        (meta, order(h1b), splits[0], splits[1], w_up, up_near, w_down, down_near),
        [SMEM] + [VMEM] * 3 + [ANY] * 4, [vm(4, features, hidden), dma(4)],
    )
    order.mark(low)
    up_far[1] = order(up_far[1])
    up_both = cores([tie(x, up_far[1]) for x in up_far])
    table_far[0] = order(table_far[0])
    table_far.append(exchange(table_far[0], 1))
    down_far[1] = order(down_far[1])
    down_both = cores([tie(x, down_far[1]) for x in down_far])
    a2, a3, p2, p3, normed2, inverse2, h2b = call(
        mlp_second_kernel, "mlp_second", (act, act, slope, slope) + state,
        (meta, order(h1b), splits[2], splits[3], low, normed1, vec_whole, *up_far, *up_both, *down_far, *down_both),
        [SMEM] + [VMEM] * 6 + [ANY] * 8, [vm(4, features, hidden), dma(8)],
    )
    order.mark(h2b)
    table_far[1] = order(table_far[1])
    table_both = cores([tie(x, table_far[1]) for x in table_far])
    count = count.x[0, :1]
    pair = lambda a, b, dtype: shape(2, a, b, dtype=dtype)
    dz2, dz2b, loss_part, g_bias, g_vec2, head_send, head_keep = call(
        functools.partial(head_kernel, own, vocab), "head",
        (
            shape(rows, features), bf(rows, features), shape(1, 128), shape(1, total),
            shape(3, features), pair(columns, total, BF16), pair(columns, total, BF16),
        ),
        (
            meta, live_counts, count, token_ids, masked_at,
            jnp.pad(head_bias, (0, total - vocab)).reshape(1, total), vec_whole, order(h2b), normed2, inverse2,
            table_own, table_near, *table_far, *table_both,
        ),
        [SMEM] * 3 + [VMEM] * 7 + [ANY] * 6,
        [vm(features, total), vm(features, total), pltpu.VMEM((rows, features), F32), dma(6)],
    )
    order.mark(dz2b)

    head_near = core_swap(head_send)
    left = shape(2, rank, features)
    down_send, left_down_a = call(
        down_send_kernel, "down_send", (pair(hidden, features, BF16), left),
        (order(dz2b), a1, a3, starts[1], starts[3]),
    )
    order.mark(down_send)
    down_got = core_swap(down_send)
    head_far = order((head_keep[1].astype(F32) + head_near[1].astype(F32)).astype(BF16))
    head_in = chip_swap(head_far)
    up_send, left_up_a, dh_a, hidden_a = call(
        up_send_kernel, "up_send",
        (pair(features, hidden, BF16), left, shape(rows, features), shape(2, 1, hidden)),
        (meta, order(dz2b), h1b, p1, p3, starts[1], starts[3], up_near, *up_both, down_near, *down_both),
        [SMEM] + [VMEM] * 6 + [ANY] * 6, [vm(rows, hidden), vm(4, features, hidden), dma(6)],
    )
    order.mark(dh_a)
    up_got = core_swap(up_send)
    down_a, down_b, down_part, left_down_b = call(
        down_keep_kernel, "down_keep",
        (bf(hidden // 2, features), bf(hidden // 2, features), shape(hidden, features), left),
        (order(dz2b), a0, a2, starts[0], starts[2], down_got, err_down[0]),
    )
    order.mark(left_down_b)
    down_in_a = chip_swap(down_a)
    both, up_b, up_part, left_up_b, dz1, dz1b, g_vec1, hidden_b = call(
        up_keep_kernel, "up_keep",
        (bf(hidden // 2 + features // 4, hidden), bf(features - features // 4, hidden), shape(features, hidden), left, shape(rows, features), bf(rows, features),
         shape(3, features), shape(2, 1, hidden)),
        (meta, dz2, order(dz2b), h1b, normed1, inverse1, vec_whole, dh_a, p0, p2, starts[0], starts[2],
         up_got, err_up[0], down_b, w_up, *up_far, w_down, *down_far),
        [SMEM] + [VMEM] * 14 + [ANY] * 6, [vm(rows, hidden), vm(4, features, hidden), dma(6)],
    )
    order.mark(dz1b)
    pack_width = 3 * features + width
    pack = shape(2, 16, pack_width)
    scratch = [vm(rows, used), vm(rows, width)]
    first_send, pack_a, dh_b = call(
        functools.partial(attention_send_kernel, length), "attention_send",
        (pair(all_rows, features, BF16), pack, shape(rows, features)),
        (meta, order(dz1b), h0b, kept[1][0], kept[3][0], kept[1][1], kept[3][1], kept[1][2], kept[3][2],
         starts[1], starts[3], left_up_a, left_down_a, hidden_a, first_near, *first_both),
        [SMEM] + [VMEM] * 13 + [ANY] * 3, scratch + [vm(2, all_rows, features), dma(3)],
    )
    order.mark(dh_b)
    head_in, down_in_a = order(head_in), order(down_in_a)
    first_got = core_swap(tie(first_send, down_in_a))
    both_in = chip_swap(tie(both, down_in_a))
    cols = bf(rows, columns)
    first_far_grad, first_part, pack_b, pack_a, d_far, d_near, d_own = call(
        functools.partial(attention_keep_kernel, length), "attention_keep",
        (bf(all_rows, features), shape(all_rows, features), pack, pack, pair(rows, columns, BF16), cols, cols),
        (meta, order(dz1b), h0b, kept[0][0], kept[2][0], kept[0][1], kept[2][1], kept[0][2], kept[2][2],
         starts[0], starts[2], left_up_b, left_down_b, hidden_b, first_got, err_qkv[0].T, err_out[0],
         dz1, dh_b, normed0, inverse0, vec_whole, g_vec1, g_vec2, g_bias, loss_part, pack_a,
         first_own, *first_far),
        [SMEM] + [VMEM] * 26 + [ANY] * 3,
        scratch + [pltpu.VMEM((rows, features), F32), vm(2, all_rows, features), dma(3)],
    )
    order.mark(d_far)

    d_two = chip_swap(d_far)
    both_in = order(both_in)
    mine = order(pack_b + core_swap(tie(pack_a, both_in)))
    d_one = core_swap(tie(d_near, both_in))
    mine_in = chip_swap(mine[1])
    mine = order(mine[0] + mine_in)
    panels = WholeSum(mine[:8], bits)
    panels.send()
    advance(order, panels)
    d_two = order(d_two)
    d_three = core_swap(d_two)
    up_in_b = chip_swap(tie(up_b, d_two))
    advance(order, panels)
    table_grad = call(
        functools.partial(scatter_kernel, own, vocab), "scatter", bf(columns, total),
        (ids_rows, order(d_own), d_one, d_two, d_three, head_near, head_keep, head_in),
    )
    order.mark(table_grad)
    table_sum = RowSum(table_grad, bits)
    table_sum.send()
    first_in = chip_swap(tie(first_far_grad, table_grad))
    while panels.step < len(bits):
        advance(order, panels)
    sizes = (features, features, features, width)
    bases, base_up, base_down, base_qkv, base_out = call(
        functools.partial(orthonormal_kernel, sizes), "orthonormal",
        (shape(rank, pack_width),) + tuple(shape(rank, size) for size in sizes), (order(panels.x),),
    )
    order.mark(bases)
    packed = call(
        right_mlp_kernel, "right_mlp", shape(rank, 2 * features + pack_width),
        (down_part, down_in_a, both_in, up_part, order(up_in_b), bases, mine[8:]),
    )
    order.mark(packed)
    packed = WholeSum(packed, bits[2:] + bits[:2])
    packed.send()
    advance(order, table_sum)
    advance(order, packed)
    advance(order, packed)
    advance(order, table_sum)
    while packed.step < len(bits):
        advance(order, packed)
    right_up, right_down = packed.x[:, :features], packed.x[:, features : 2 * features]
    rest = packed.x[:, 2 * features :]
    rights = call(
        functools.partial(right_attention_kernel, used), "right_attention", shape(rank, features + used),
        (first_part, order(first_in), bases),
    )
    order.mark(rights)
    rights = WholeSum(rights, bits[2:] + bits[:2])
    rights.send()
    advance(order, table_sum)
    down = update(replicas, down_part, [(down_in_a, hidden // 2, 0), (both_in, hidden // 2, 0)], 0, w_down, mom_down, order(base_down), right_down)
    order.mark(down[0])
    advance(order, rights)
    advance(order, table_sum)
    up = update(replicas, up_part, [(both_in, features // 4, 2 * hidden // features), (up_in_b, features - features // 4, 0)], 0, w_up, mom_up, order(base_up), right_up)
    order.mark(up[0])
    rest = tie(rest, up[0])
    while rights.step < len(bits):
        advance(order, rights)
    right_out, right_qkv = rights.x[:, :features], rights.x[:, features:]
    out = update(replicas, first_part, [first_in], used, w_out, mom_out, order(base_out), right_out)
    qkv = update(replicas, first_part, [first_in], 0, w_qkv.T, mom_qkv.T, right_qkv, base_qkv)
    order.mark(qkv[0])
    while table_sum.step < len(table_sum.steps):
        advance(order, table_sum)

    table_grad = table_sum.x[:, :total_rows].astype(F32)
    vectors = [rest[2 + n // 3, n % 3 * features : (n % 3 + 1) * features] for n in range(8)]
    results = [jnp.where(jnp.arange(2) == 0, rest[4, 2 * features : 2 * features + 1], count)]

    def momentum_step(weight, moment, grad, rate):
        new_moment = BETA * moment + grad
        return (weight.astype(F32) - rate * new_moment, new_moment)

    new = momentum_step(tables.T, table_mom.T, table_grad, RATE_TAB)
    results += [new[0].T, new[1].T]
    results += momentum_step(vec_whole, vec_mom, jnp.stack(vectors), RATE_VEC)
    results += momentum_step(vec_split, split_mom, rest[0:1, : vec_split.shape[1]], RATE_VEC)
    results += momentum_step(head_bias, bias_mom, rest[1, :vocab], RATE_VEC)
    one = 1.0 / replicas
    for (weight, moment, error), base, right, flip in (
        (qkv, base_qkv, right_qkv, True), (out, base_out, right_out, False),
        (up, base_up, right_up, False), (down, base_down, right_down, False),
    ):
        if flip:
            weight, moment, error = weight.T, moment.T, error.T
        results += [weight, moment, error[None], base.T[None], right.T * one]
    return tuple(results)


def solution(mesh):
    rows, cols = P("tensor", None), P(None, "tensor")
    batch = P("dp", None)
    in_specs = (
        batch, batch, P("dp"), cols, cols, P(), P(), rows, rows, P(), P(),
        cols, rows, cols, rows, cols, rows, cols, rows,
        P("dp", None, "tensor"), P("dp", "tensor", None), P("dp", None, "tensor"), P("dp", "tensor", None),
        rows, rows, rows, rows,
    )
    left = P("tensor", None, None)
    out_specs = (P(), cols, cols, P(), P(), rows, rows, P(), P())
    for side in (cols, rows, cols, rows):
        out_specs += (side, side, P("dp", *side), left, rows)
    return jax.shard_map(shards, mesh=mesh, in_specs=in_specs, out_specs=out_specs, check_vma=False)
```

```python
import functools

import jax
import jax.numpy as jnp
from jax import lax
from jax.experimental import pallas as pl
from jax.experimental.pallas import tpu as pltpu
from jax.sharding import PartitionSpec as P

HD = 48
EPSILON = 1e-05
BETA = 0.9
RATE_MAT = 100.0
RATE_VEC = 10.0
RATE_TAB = 100.0
HIGHEST = lax.Precision.HIGHEST
BF16 = jnp.bfloat16
F32 = jnp.float32
MIB = 1024 * 1024


def bdot(left, right):
    return jnp.dot(left, right, preferred_element_type=F32)


def tdot(left, right):
    return lax.dot_general(left, right, (((0,), (0,)), ((), ())), preferred_element_type=F32)


def ndot(left, right):
    return lax.dot_general(left, right, (((1,), (1,)), ((), ())), preferred_element_type=F32)


def across(x, axis, bit):
    size = lax.axis_size(axis)
    return lax.ppermute(x, axis, [(i, i ^ bit) for i in range(size)])


def core_swap(x):
    return across(x, "tensor", 1)


def chip_swap(x):
    return across(x, "tensor", 2)


def tie(x, *others):
    return lax.optimization_barrier((x,) + others)[0]


def head_mask(width, head):
    lane = lax.broadcasted_iota(jnp.int32, (1, width), 1)
    return ((lane >= head * HD) & (lane < (head + 1) * HD)).astype(BF16)


SCALE = 10.0
LIMITS = {
    "pack_first": (56, 2), "pack_rest": (50, 3), "embed": (8, 5), "attention_first": (10, 7), "attention_second": (10, 8), "mlp_first": (12, 7),
    "mlp_second": (14, 7), "head": (24, 9), "down_send": (8, 3), "down_keep": (14, 4), "up_send": (14, 6),
    "up_keep": (20, 8), "attention_send": (14, 13), "attention_keep": (20, 15), "scatter": (8, 5),
    "orthonormal": (4, 3), "right_mlp": (16, 3), "right_attention": (12, 2), "update": (16, 4),
}


def call(kernel, name, out_shape, operands, in_specs=None, scratch=(), out_specs=None, **grid):
    limit, cost = LIMITS[name]
    cost *= 1.0 if name in ("scatter", "orthonormal", "right_mlp", "right_attention", "update") else SCALE
    if in_specs is None:
        in_specs = [pl.BlockSpec(memory_space=pltpu.VMEM)] * len(operands)
    if out_specs is not None:
        grid["out_specs"] = out_specs
    return pl.pallas_call(
        kernel,
        out_shape=out_shape,
        in_specs=in_specs,
        scratch_shapes=list(scratch),
        compiler_params=pltpu.CompilerParams(vmem_limit_bytes=limit * MIB),
        cost_estimate=pl.CostEstimate(flops=int(cost * 1150000000), bytes_accessed=int(cost * 1000000), transcendentals=0),
        name=name,
        **grid,
    )(*operands)


VMEM = pl.BlockSpec(memory_space=pltpu.VMEM)
SMEM = pl.BlockSpec(memory_space=pltpu.SMEM)
ANY = pl.BlockSpec(memory_space=pltpu.HBM)


def shape(*dims, dtype=F32):
    return jax.ShapeDtypeStruct(dims, dtype)


def normalize(x):
    center = x - jnp.mean(x, -1, keepdims=True)
    inverse = lax.rsqrt(jnp.mean(center * center, -1, keepdims=True) + EPSILON)
    return center * inverse, inverse


def norm_back(normed, inverse, gain, grad):
    inner = grad * gain
    first = jnp.mean(inner, -1, keepdims=True)
    second = jnp.mean(inner * normed, -1, keepdims=True)
    d_x = inverse * (inner - first - normed * second)
    return d_x, jnp.sum(grad * normed, 0, keepdims=True), jnp.sum(grad, 0, keepdims=True)


def split3(x):
    high = x.astype(BF16).astype(F32)
    rest = x - high
    middle = rest.astype(BF16).astype(F32)
    return jnp.concatenate([high, middle, rest - middle], 0).astype(BF16)


def fold3(x):
    rank = x.shape[0] // 3
    return x[:rank] + x[rank : 2 * rank] + x[2 * rank :]


def panel(start, right, left):
    return fold3(bdot(split3(fold3(ndot(split3(start), right))), left))


def split2(x):
    high = x.astype(BF16)
    return high, (x - high.astype(F32)).astype(BF16)


def wide(dot, start, x):
    parts = split3(start)
    high, rest = split2(x)
    return fold3(dot(parts, high) + dot(parts, rest))


class Fetch:
    def __init__(self, meta_ref, sems):
        self.half, self.sems, self.used = meta_ref[1], sems, 0

    def one(self, source, target):
        copy = pltpu.make_async_copy(source, target, self.sems.at[self.used])
        self.used += 1
        copy.start()
        return copy

    def block(self, pieces, target, first=0):
        if len(pieces) == 1:
            return [self.one(pieces[0], target.at[pl.ds(first, pieces[0].shape[0]), :])]
        size = pieces[0].shape[0]
        spots = (first + self.half * size, first + (1 - self.half) * size)
        return [
            self.one(piece, target.at[pl.ds(pl.multiple_of(spot, 32), size), :])
            for piece, spot in zip(pieces, spots)
        ]


def wait(copies):
    for copy in copies:
        copy.wait()


def pack_first_kernel(meta_ref, qkv_ref, out_ref, first_ref, first_half, sems):
    near, rest = qkv_ref.shape[0], out_ref.shape[0]
    size = first_half.shape[0]
    fetch = Fetch(meta_ref, sems)
    wait([
        fetch.one(qkv_ref, first_ref.at[pl.ds(0, near), :]),
        fetch.one(out_ref, first_ref.at[pl.ds(near, rest), :]),
    ])
    first_half[...] = first_ref[pl.ds(pl.multiple_of(meta_ref[1] * size, 32), size), :]


def pack_rest_kernel(meta_ref, up_ref, down_ref, tables_ref, up_half, down_half, table_ref, table_half, sems):
    half = meta_ref[1]
    size = up_half.shape[0]
    at = pl.multiple_of(half * size, 32)
    fetch = Fetch(meta_ref, sems)
    copies = [
        fetch.one(up_ref.at[pl.ds(at, size), :], up_half),
        fetch.one(down_ref.at[pl.ds(at, size), :], down_half),
    ]
    total = tables_ref.shape[1]
    table_ref[...] = jnp.zeros_like(table_ref)
    table_ref[:, :total] = tables_ref[...]
    rows = table_half.shape[0]
    table_half[...] = table_ref[pl.ds(pl.multiple_of(half * rows, 32), rows), :]
    wait(copies)


def embed_kernel(own, vocab, meta_ref, live_ref, ids_ref, slots_ref, table_ref, far_ref, near_ref, own_ref, rows_ref):
    images, length = ids_ref.shape
    slot_count = slots_ref.shape[1]
    total = table_ref.shape[1]
    member = meta_ref[0]
    ids_t = jnp.transpose(ids_ref[...].astype(F32))
    image_lane = lax.broadcasted_iota(jnp.int32, (length, images), 1)
    position = lax.broadcasted_iota(jnp.int32, (length, 1), 0)
    slot_lane = lax.broadcasted_iota(jnp.int32, (1, slot_count), 1)
    table_lane = lax.broadcasted_iota(jnp.int32, (1, total), 1)
    table = table_ref[...]

    def rows_of(ids):
        hot = jnp.where(ids == table_lane, 1.0, 0.0).astype(BF16)
        return ndot(table, hot).astype(BF16)

    targets = {
        0: (own_ref, 0), 1: (near_ref, 0), 2: (far_ref.at[0], 0), 3: (far_ref.at[1], 0),
    }
    for k in range(4):
        for i in range(own):
            image = (member ^ k) * own + i
            hit = (slots_ref[pl.ds(image, 1), :] == position) & (slot_lane < live_ref[image])
            masked = jnp.max(jnp.where(hit, 1.0, 0.0), 1, keepdims=True)
            ids = jnp.sum(jnp.where(image_lane == image, ids_t, 0.0), 1, keepdims=True)
            ids = jnp.where(masked > 0, float(vocab - 1), ids).astype(jnp.int32)
            place = k * own + i
            rows_ref[:, place : place + 1] = ids
            ref, first = targets[k]
            ref[:, first + i * length : first + (i + 1) * length] = rows_of(ids)
    at = rows_of(position + vocab)
    own_ref[:, own * length :] = at
    near_ref[:, own * length :] = at
    far_ref[0, :, own * length :] = at[:, : length // 2]
    far_ref[1, :, own * length :] = at[:, length // 2 :]


def attention_one(length, hb, w, bias_ref, qkv_ref, lse_ref, ctx_ref):
    width = ctx_ref.shape[1]
    mixed = ndot(hb, w)
    first = bias_ref.shape[1] - 6 * width
    q_bias = bias_ref[0:1, first : first + width]
    v_bias = bias_ref[0:1, first + width : first + 2 * width]
    qkv_ref[0] = ((mixed[:, :width] + q_bias) * HD ** (-0.5)).astype(BF16)
    qkv_ref[1] = mixed[:, width : 2 * width].astype(BF16)
    qkv_ref[2] = (mixed[:, 2 * width :] + v_bias).astype(BF16)
    for image in range(hb.shape[0] // length):
        rows = slice(image * length, (image + 1) * length)
        q, k, v = qkv_ref[0, rows, :], qkv_ref[1, rows, :], qkv_ref[2, rows, :]
        total = jnp.zeros((length, width), F32)
        for head in range(width // HD):
            mask = head_mask(width, head)
            scores = ndot(q * mask, k)
            top = jnp.max(scores, -1, keepdims=True)
            powers = jnp.exp(scores - top)
            weight = jnp.sum(powers, -1, keepdims=True)
            lse_ref[rows, head : head + 1] = top + jnp.log(weight)
            probs = (powers * (1.0 / weight)).astype(BF16)
            total = total + bdot(probs, v * mask)
        ctx_ref[rows, :] = total.astype(BF16)


def attention_first_kernel(
    length, meta_ref, e0, e1, e2, e3, vec_ref, b0, b1, c0, c1,
    normed_ref, inverse_ref, hb_ref, qkv0, lse0, ctx0, qkv1, lse1, ctx1, x_ref, w_ref, sems,
):
    rows, width = hb_ref.shape[0], e0.shape[0]
    member = meta_ref[0]
    fetch = Fetch(meta_ref, sems)
    used = 3 * width
    zero = fetch.one(c0.at[pl.ds(0, used), :], w_ref.at[0])
    one = fetch.one(c1.at[pl.ds(0, used), :], w_ref.at[1])
    slabs = ((e0, e0, e0), (e1, e1, e1), (e2.at[0], e2.at[0], e2.at[1]), (e3.at[1], e3.at[0], e3.at[1]))
    for k, (ref, low, high) in enumerate(slabs):
        at = low[:, rows:] if low is high else jnp.concatenate([low[:, rows:], high[:, rows:]], 1)
        at = at.astype(F32)
        place = pl.ds(pl.multiple_of((member ^ k) * width, 64), width)
        for i in range(rows // length):
            x_ref[place, i * length : (i + 1) * length] = ref[:, i * length : (i + 1) * length].astype(F32) + at
    normed, inverse = normalize(jnp.transpose(x_ref[...]))
    normed_ref[...] = normed
    inverse_ref[...] = inverse
    hb_ref[...] = (normed * vec_ref[0:1, :] + vec_ref[1:2, :]).astype(BF16)
    hb = hb_ref[...]
    zero.wait()
    attention_one(length, hb, w_ref[0], b0, qkv0, lse0, ctx0)
    one.wait()
    attention_one(length, hb, w_ref[1], b1, qkv1, lse1, ctx1)


def attention_second_kernel(
    length, meta_ref, normed_ref, hb_ref, vec_ref, b2, b3, ctx0, ctx1, c0, c1, c2a, c2b, c3a, c3b,
    normed1_ref, inverse1_ref, h1b_ref, qkv2, lse2, ctx2, qkv3, lse3, ctx3, w_ref, o_ref, sems,
):
    hb = hb_ref[...]
    width = ctx0.shape[1]
    used = 3 * width
    fetch = Fetch(meta_ref, sems)
    two = fetch.block((c2a, c2b), w_ref.at[0])
    three = fetch.block((c3a, c3b), w_ref.at[1])
    others = [fetch.one(c.at[pl.ds(used, width), :], o_ref.at[n]) for n, c in enumerate((c0, c1))]
    wait(two)
    attention_one(length, hb, w_ref[0, :used, :], b2, qkv2, lse2, ctx2)
    wait(three)
    attention_one(length, hb, w_ref[1, :used, :], b3, qkv3, lse3, ctx3)
    wait(others)
    total = bdot(ctx0[...], o_ref[0]) + bdot(ctx1[...], o_ref[1])
    total = total + bdot(ctx2[...], w_ref[0, used:, :]) + bdot(ctx3[...], w_ref[1, used:, :])
    z_one = normed_ref[...] * vec_ref[0:1, :] + vec_ref[1:2, :] + (total + vec_ref[2:3, :])
    normed, inverse = normalize(z_one)
    normed1_ref[...] = normed
    inverse1_ref[...] = inverse
    h1b_ref[...] = (normed * vec_ref[3:4, :] + vec_ref[4:5, :]).astype(BF16)


def gelu_pair(x):
    inner = 0.7978845608028654 * x * (1.0 + 0.044715 * x * x)
    curve = jnp.tanh(inner)
    value = 0.5 * x * (1.0 + curve)
    slope = 0.5 * (1.0 + curve) + 0.5 * x * (1.0 - curve * curve) * (
        0.7978845608028654 * (1.0 + 3 * 0.044715 * x * x)
    )
    return value, slope


def mlp_one(h1b, up_ref, bias_ref, active_ref, slope_ref):
    first = bias_ref.shape[1] - up_ref.shape[1]
    step = 256
    for at in range(0, up_ref.shape[1], step):
        pre = bdot(h1b, up_ref[:, at : at + step]) + bias_ref[0:1, first + at : first + at + step]
        value, slope = gelu_pair(pre)
        active_ref[:, at : at + step] = value.astype(BF16)
        slope_ref[:, at : at + step] = slope


def mlp_first_kernel(meta_ref, h1b_ref, b0, b1, u0, u1, d0, d1, a0, a1, s0, s1, low_ref, w_ref, sems):
    fetch = Fetch(meta_ref, sems)
    copies = [fetch.one(ref, w_ref.at[n]) for n, ref in enumerate((u0, d0, u1, d1))]
    h1b = h1b_ref[...]
    copies[0].wait()
    mlp_one(h1b, w_ref.at[0], b0, a0, s0)
    copies[1].wait()
    low_ref[...] = bdot(a0[...], w_ref[1])
    copies[2].wait()
    mlp_one(h1b, w_ref.at[2], b1, a1, s1)
    copies[3].wait()
    low_ref[...] += bdot(a1[...], w_ref[3])


def mlp_second_kernel(
    meta_ref, h1b_ref, b2, b3, low_ref, normed1_ref, vec_ref, u2a, u2b, u3a, u3b, d2a, d2b, d3a, d3b,
    a2, a3, s2, s3, normed2_ref, inverse2_ref, h2b_ref, w_ref, sems,
):
    fetch = Fetch(meta_ref, sems)
    pieces = ((u2a, u2b), (d2a, d2b), (u3a, u3b), (d3a, d3b))
    copies = [fetch.block(piece, w_ref.at[n]) for n, piece in enumerate(pieces)]
    h1b = h1b_ref[...]
    wait(copies[0])
    mlp_one(h1b, w_ref.at[0], b2, a2, s2)
    wait(copies[1])
    normed2_ref[...] = low_ref[...] + bdot(a2[...], w_ref[1])
    wait(copies[2])
    mlp_one(h1b, w_ref.at[2], b3, a3, s3)
    wait(copies[3])
    total = normed2_ref[...] + bdot(a3[...], w_ref[3]) + vec_ref[5:6, :]
    normed, inverse = normalize(normed1_ref[...] * vec_ref[3:4, :] + vec_ref[4:5, :] + total)
    normed2_ref[...] = normed
    inverse2_ref[...] = inverse
    h2b_ref[...] = (normed * vec_ref[6:7, :] + vec_ref[7:8, :]).astype(BF16)


def head_kernel(
    own, vocab, meta_ref, live_ref, count_ref, ids_ref, slots_ref, bias_ref, vec_ref,
    h2b_ref, normed2_ref, inverse2_ref, t0, t1, t2a, t2b, t3a, t3b,
    dz_ref, dzb_ref, loss_ref, gbias_ref, gvec_ref, send_ref, keep_ref,
    table_ref, full_ref, grad_ref, sems,
):
    images, length = ids_ref.shape
    slot_count = slots_ref.shape[1]
    total = bias_ref.shape[1]
    member = meta_ref[0]
    columns = t0.shape[0]
    fetch = Fetch(meta_ref, sems)
    copies = []
    for k, pieces in enumerate(((t0,), (t1,), (t2a, t2b), (t3a, t3b))):
        copies += fetch.block(pieces, table_ref, pl.multiple_of((member ^ k) * columns, 64))
    slots_t = jnp.transpose(slots_ref[...].astype(F32))
    image_lane = lax.broadcasted_iota(jnp.int32, (slot_count, images), 1)
    slot_row = lax.broadcasted_iota(jnp.int32, (slot_count, 1), 0)
    position = lax.broadcasted_iota(jnp.int32, (1, length), 1).astype(F32)
    picks, targets, weights, picked = [], [], [], []
    for i in range(own):
        image = member * own + i
        at = jnp.sum(jnp.where(image_lane == image, slots_t, 0.0), 1, keepdims=True)
        hit = at == position
        ids = ids_ref[pl.ds(image, 1), :].astype(F32)
        targets.append(jnp.sum(jnp.where(hit, ids, 0.0), 1, keepdims=True).astype(jnp.int32))
        weights.append(jnp.where(slot_row < live_ref[image], 1.0, 0.0))
        picks.append(jnp.where(hit, 1.0, 0.0).astype(BF16))
        picked.append(bdot(picks[i], h2b_ref[i * length : (i + 1) * length, :]).astype(BF16))
    target = jnp.concatenate(targets, 0)
    weight = jnp.concatenate(weights, 0)
    rows = jnp.concatenate(picked, 0)
    wait(copies)
    lane = lax.broadcasted_iota(jnp.int32, (1, total), 1)
    logits = bdot(rows, table_ref[...]) + bias_ref[...]
    logits = jnp.where(lane < vocab, logits, -1e30)
    top = jnp.max(logits, -1, keepdims=True)
    log_total = top + jnp.log(jnp.sum(jnp.exp(logits - top), -1, keepdims=True))
    hot = jnp.where(lane == target, 1.0, 0.0)
    chosen = jnp.sum(hot * logits, -1, keepdims=True)
    loss_ref[...] = jnp.broadcast_to(jnp.sum(weight * (log_total - chosen), 0, keepdims=True), loss_ref.shape)
    d_logits = (jnp.exp(logits - log_total) - hot) * (weight / count_ref[0])
    gbias_ref[...] = jnp.sum(d_logits, 0, keepdims=True)
    dl = d_logits.astype(BF16)
    d_rows = ndot(dl, table_ref[...])
    high = d_rows.astype(BF16)
    rest = (d_rows - high.astype(F32)).astype(BF16)
    for i in range(own):
        part = slice(i * slot_count, (i + 1) * slot_count)
        grad_ref[i * length : (i + 1) * length, :] = tdot(picks[i], high[part]) + tdot(picks[i], rest[part])
    d_z2, d_gain, d_shift = norm_back(normed2_ref[...], inverse2_ref[...], vec_ref[6:7, :], grad_ref[...])
    dz_ref[...] = d_z2
    dzb_ref[...] = d_z2.astype(BF16)
    gvec_ref[0:1, :] = jnp.sum(d_z2, 0, keepdims=True)
    gvec_ref[1:2, :] = d_gain
    gvec_ref[2:3, :] = d_shift
    full_ref[...] = tdot(rows, dl).astype(BF16)
    for k, out in enumerate((keep_ref.at[0], send_ref.at[0], keep_ref.at[1], send_ref.at[1])):
        out[...] = full_ref[pl.ds(pl.multiple_of((member ^ k) * columns, 64), columns), :]


def down_send_kernel(dzb_ref, a1, a3, s1, s3, send_ref, left_ref):
    first = dzb_ref.shape[1]
    dzb = dzb_ref[...]
    for n, (active, start) in enumerate(((a1[...], s1), (a3[...], s3))):
        send_ref[n] = tdot(active, dzb).astype(BF16)
        left_ref[n] = panel(start[:8, first : 2 * first], dzb, active)


def close(n, grad, near_ref, err_ref, far_refs, part_ref):
    if n == 0:
        part_ref[...] = grad + near_ref[0].astype(F32) + err_ref[...]
    else:
        total = (grad + near_ref[1].astype(F32)).astype(BF16)
        first = 0
        for far_ref in far_refs:
            far_ref[...] = total[first : first + far_ref.shape[0]]
            first += far_ref.shape[0]


def down_keep_kernel(dzb_ref, a0, a2, s0, s2, near_ref, err_ref, far_a, far_b, part_ref, left_ref):
    first = dzb_ref.shape[1]
    dzb = dzb_ref[...]
    for n, (active, start) in ((1, (a2[...], s2)), (0, (a0[...], s0))):
        close(n, tdot(active, dzb), near_ref, err_ref, (far_a, far_b), part_ref)
        left_ref[n] = panel(start[:8, first : 2 * first], dzb, active)
    left_ref[0] += wide(ndot, s0[:8, first : 2 * first], err_ref[...])


def up_one(dzb, h1b, slope, up, down, start, hidden_ref, dpre_ref):
    step = 256
    for at in range(0, down.shape[0], step):
        d_pre = ndot(dzb, down[at : at + step, :]) * slope[:, at : at + step]
        hidden_ref[:, at : at + step] = jnp.sum(d_pre, 0, keepdims=True)
        dpre_ref[:, at : at + step] = d_pre.astype(BF16)
    d_pre = dpre_ref[...]
    return tdot(h1b, d_pre), ndot(d_pre, up[...]), panel(start[:8, : d_pre.shape[1]], d_pre, h1b)


def up_send_kernel(
    meta_ref, dzb_ref, h1b_ref, p1, p3, s1, s3, u1, u3a, u3b, d1, d3a, d3b,
    send_ref, left_ref, dh_ref, hidden_ref, dpre_ref, w_ref, sems,
):
    fetch = Fetch(meta_ref, sems)
    pieces = ((d1,), (u1,), (d3a, d3b), (u3a, u3b))
    copies = [fetch.block(piece, w_ref.at[n]) for n, piece in enumerate(pieces)]
    dzb, h1b = dzb_ref[...], h1b_ref[...]
    for n, (slope, start) in enumerate(((p1, s1), (p3, s3))):
        wait(copies[2 * n] + copies[2 * n + 1])
        grad, part, left_ref[n] = up_one(
            dzb, h1b, slope, w_ref.at[2 * n + 1], w_ref.at[2 * n], start, hidden_ref.at[n], dpre_ref
        )
        send_ref[n] = grad.astype(BF16)
        dh_ref[...] = part if n == 0 else dh_ref[...] + part


def up_keep_kernel(
    meta_ref, dz_ref, dzb_ref, h1b_ref, normed1_ref, inverse1_ref, vec_ref, dh_ref, p0, p2, s0, s2,
    near_ref, err_ref, other_ref, u0, u2a, u2b, d0, d2a, d2b,
    far_a, far_b, part_ref, left_ref, dz1_ref, dz1b_ref, gvec_ref, hidden_ref, dpre_ref, w_ref, sems,
):
    other = other_ref.shape[0]
    far_a[:other, :] = other_ref[...]
    fetch = Fetch(meta_ref, sems)
    pieces = ((d0,), (u0,), (d2a, d2b), (u2a, u2b))
    copies = [fetch.block(piece, w_ref.at[n]) for n, piece in enumerate(pieces)]
    dzb, h1b = dzb_ref[...], h1b_ref[...]
    for n, (slope, start) in ((1, (p2, s2)), (0, (p0, s0))):
        wait(copies[2 * n] + copies[2 * n + 1])
        grad, part, left_ref[n] = up_one(
            dzb, h1b, slope, w_ref.at[2 * n + 1], w_ref.at[2 * n], start, hidden_ref.at[n], dpre_ref
        )
        close(n, grad, near_ref, err_ref, (far_a.at[pl.ds(other, far_a.shape[0] - other), :], far_b), part_ref)
        dz1_ref[...] = part + (dz_ref[...] + dh_ref[...] if n == 1 else dz1_ref[...])
    left_ref[0] += wide(ndot, s0[:8, : err_ref.shape[1]], err_ref[...])
    d_z1, d_gain, d_shift = norm_back(normed1_ref[...], inverse1_ref[...], vec_ref[3:4, :], dz1_ref[...])
    dz1_ref[...] = d_z1
    dz1b_ref[...] = d_z1.astype(BF16)
    gvec_ref[0:1, :] = jnp.sum(d_z1, 0, keepdims=True)
    gvec_ref[1:2, :] = d_gain
    gvec_ref[2:3, :] = d_shift


def attention_back_one(length, dz, hb, w_ref, qkv_ref, lse_ref, ctx_ref, start_ref, pack_ref, dm_ref, dc_ref):
    width, features = ctx_ref.shape[1], dz.shape[1]
    used = 3 * width
    dc_ref[...] = ndot(dz, w_ref[used:, :]).astype(BF16)
    ctx = ctx_ref[...]
    out_grad = tdot(ctx, dz)
    pack_ref[:8, 3 * features :] = panel(start_ref[:8, 2 * features : 3 * features], dz, ctx)
    q_sum = jnp.zeros((1, width), F32)
    v_sum = jnp.zeros((1, width), F32)
    for image in range(dz.shape[0] // length):
        rows = slice(image * length, (image + 1) * length)
        q, k, v, dc = qkv_ref[0, rows, :], qkv_ref[1, rows, :], qkv_ref[2, rows, :], dc_ref[rows, :]
        d_query = jnp.zeros((length, width), F32)
        d_key = jnp.zeros((length, width), F32)
        d_value = jnp.zeros((length, width), F32)
        for head in range(width // HD):
            mask = head_mask(width, head)
            q_head, k_head, c_head = q * mask, k * mask, dc * mask
            probs = jnp.exp(ndot(q_head, k) - lse_ref[rows, head : head + 1])
            d_value = d_value + tdot(probs.astype(BF16), c_head)
            d_probs = ndot(c_head, v)
            inner = jnp.sum(d_probs * probs, -1, keepdims=True)
            d_scores = (probs * (d_probs - inner)).astype(BF16)
            d_query = d_query + bdot(d_scores, k_head)
            d_key = d_key + tdot(d_scores, q_head)
        d_query = d_query * HD ** (-0.5)
        q_sum = q_sum + jnp.sum(d_query, 0, keepdims=True)
        v_sum = v_sum + jnp.sum(d_value, 0, keepdims=True)
        dm_ref[rows, :width] = d_query.astype(BF16)
        dm_ref[rows, width : 2 * width] = d_key.astype(BF16)
        dm_ref[rows, 2 * width :] = d_value.astype(BF16)
    pack_ref[8:9, :width] = q_sum
    pack_ref[8:9, width : 2 * width] = v_sum
    dm = dm_ref[...]
    pack_ref[:8, 2 * features : 3 * features] = panel(start_ref[:8, 3 * features : 3 * features + dm_ref.shape[1]], dm, hb)
    return tdot(dm, hb), out_grad, bdot(dm, w_ref[:used, :])


def pack_rows(pack_ref, width, up, down, hidden):
    features = up.shape[1]
    pack_ref[...] = jnp.zeros_like(pack_ref)
    pack_ref[:8, :features] = up
    pack_ref[:8, features : 2 * features] = down
    pack_ref[8:9, 2 * width : 2 * width + features] = hidden


def pack_whole(pack_ref, vectors, bias, loss):
    pack_ref[9:10, : bias.shape[1]] = bias
    features = vectors[0].shape[1]
    for n, vector in enumerate(vectors + [loss]):
        row, place = 10 + n // 3, n % 3
        pack_ref[row : row + 1, place * features : place * features + vector.shape[1]] = vector


def attention_send_kernel(
    length, meta_ref, dz1b_ref, hb_ref, q1, q3, l1, l3, x1, x3, s1, s3, up_ref, down_ref, hidden_ref,
    c1, c3a, c3b, send_ref, pack_ref, dh_ref, dm_ref, dc_ref, w_ref, sems,
):
    fetch = Fetch(meta_ref, sems)
    copies = [fetch.block((c1,), w_ref.at[0]), fetch.block((c3a, c3b), w_ref.at[1])]
    dz, hb = dz1b_ref[...], hb_ref[...]
    used = dm_ref.shape[1]
    for n, (q, l, x, start) in enumerate(((q1, l1, x1, s1), (q3, l3, x3, s3))):
        wait(copies[n])
        pack_rows(pack_ref.at[n], x.shape[1], up_ref[n], down_ref[n], hidden_ref[n])
        qkv_grad, out_grad, part = attention_back_one(
            length, dz, hb, w_ref.at[n], q, l, x, start, pack_ref.at[n], dm_ref, dc_ref
        )
        send_ref[n, :used, :] = qkv_grad.astype(BF16)
        send_ref[n, used:, :] = out_grad.astype(BF16)
        dh_ref[...] = part if n == 0 else dh_ref[...] + part


def attention_keep_kernel(
    length, meta_ref, dz1b_ref, hb_ref, q0, q2, l0, l2, x0, x2, s0, s2, up_ref, down_ref, hidden_ref,
    near_ref, err_qkv, err_out, dz1_ref, dha_ref, normed_ref, inverse_ref, vec_ref, gvec1_ref, gvec2_ref, gbias_ref,
    loss_ref, send_pack_ref, c0, c2a, c2b,
    far_ref, part_ref, pack_ref, send_ref, d_far, d_near, d_own, dm_ref, dc_ref, dh_ref, w_ref, sems,
):
    fetch = Fetch(meta_ref, sems)
    copies = [fetch.block((c0,), w_ref.at[0]), fetch.block((c2a, c2b), w_ref.at[1])]
    dz, hb = dz1b_ref[...], hb_ref[...]
    used, width = dm_ref.shape[1], x0.shape[1]
    features = hb.shape[1]
    for n, (q, l, x, start) in ((1, (q2, l2, x2, s2)), (0, (q0, l0, x0, s0))):
        wait(copies[n])
        pack_rows(pack_ref.at[n], width, up_ref[n], down_ref[n], hidden_ref[n])
        qkv_grad, out_grad, part = attention_back_one(
            length, dz, hb, w_ref.at[n], q, l, x, start, pack_ref.at[n], dm_ref, dc_ref
        )
        if n == 0:
            part_ref[:used, :] = qkv_grad + near_ref[0, :used, :].astype(F32) + err_qkv[...]
            part_ref[used:, :] = out_grad + near_ref[0, used:, :].astype(F32) + err_out[...]
        else:
            far_ref[:used, :] = (qkv_grad + near_ref[1, :used, :].astype(F32)).astype(BF16)
            far_ref[used:, :] = (out_grad + near_ref[1, used:, :].astype(F32)).astype(BF16)
        dh_ref[...] = part + (dha_ref[...] + dz1_ref[...] if n == 1 else dh_ref[...])
    pack_ref[0, :8, 2 * features : 3 * features] += wide(bdot, s0[:8, 3 * features : 3 * features + used], err_qkv[...])
    pack_ref[0, :8, 3 * features :] += wide(ndot, s0[:8, 2 * features : 3 * features], err_out[...])
    d_x, d_gain, d_shift = norm_back(normed_ref[...], inverse_ref[...], vec_ref[0:1, :], dh_ref[...])
    vectors = [d_gain, d_shift] + [gvec1_ref[i : i + 1, :] for i in range(3)] + [gvec2_ref[i : i + 1, :] for i in range(3)]
    send_ref[...] = send_pack_ref[...]
    for ref in (send_ref.at[0], send_ref.at[1], pack_ref.at[0], pack_ref.at[1]):
        pack_whole(ref, vectors, gbias_ref[...], loss_ref[...])
    dh_ref[...] = d_x
    rows, columns = d_own.shape
    for t in range(4):

        @pl.when(meta_ref[0] == t)
        def _():
            for k, out in enumerate((d_own, d_near, d_far.at[0], d_far.at[1])):
                out[...] = dh_ref[:, (t ^ k) * columns : ((t ^ k) + 1) * columns].astype(BF16)


def scatter_kernel(own, vocab, ids_ref, r0, r1, r2, r3, near_ref, keep_ref, far_ref, out_ref):
    length = ids_ref.shape[0]
    total = out_ref.shape[1]
    lane = lax.broadcasted_iota(jnp.int32, (1, total), 1)
    position = lax.broadcasted_iota(jnp.int32, (length, 1), 0) + vocab
    result = keep_ref[0].astype(F32) + near_ref[0].astype(F32) + far_ref[...].astype(F32)
    for k, rows in enumerate((r0[...], r1[...], r2[0], r3[1])):
        hots = []
        for i in range(own):
            ids = ids_ref[:, k * own + i : k * own + i + 1]
            hots.append(jnp.where((ids == lane) | (position == lane), 1.0, 0.0).astype(BF16))
        result = result + tdot(rows, jnp.concatenate(hots, 0))
    out_ref[...] = result.astype(out_ref.dtype)


def joined(refs):
    parts = [ref[...].astype(F32) for ref in refs]
    return parts[0] if len(parts) == 1 else jnp.concatenate(parts, 0)


def right_mlp_kernel(part_d, got_c, both, part_u, got_b, base_ref, rest_ref, out_ref):
    size = part_d.shape[1]
    rows = part_d.shape[0]
    rest = rows - got_c.shape[0]
    got_d, got_a = both.at[pl.ds(0, rest), :], both.at[pl.ds(rest, both.shape[0] - rest), :]
    for n, (part, gots) in enumerate(((part_u, (got_a, got_b)), (part_d, (got_c, got_d)))):
        merged = part[...] + joined(gots)
        out_ref[:, n * size : (n + 1) * size] = wide(bdot, base_ref[:, n * rows : (n + 1) * rows], merged)
    out_ref[:, 2 * size :] = rest_ref[...]


def right_attention_kernel(used, part, got, base_ref, out_ref):
    features = part.shape[1]
    out_ref[:, :features] = wide(bdot, base_ref[:, 3 * features :], part[used:, :] + got[used:, :].astype(F32))
    merged = part[:used, :] + got[:used, :].astype(F32)
    out_ref[:, features:] = wide(ndot, base_ref[:, 2 * features : 3 * features], merged)


def update_kernel(replicas, part, weight, moment, first_ref, second_ref, *refs):
    gots, (weight_new, moment_new, error_new) = refs[:-3], refs[-3:]
    first, second = split3(first_ref[...] * (1.0 / replicas)), split3(second_ref[...])
    rank = first.shape[0] // 3
    parts = lambda x, order: jnp.concatenate([x[i * rank : (i + 1) * rank].astype(F32) for i in order], 0).astype(BF16)
    approx = tdot(parts(first, (0, 0, 1, 0, 2, 1)), parts(second, (0, 1, 0, 2, 0, 1)))
    new = BETA * moment[...] + approx
    moment_new[...] = new
    weight_new[...] = weight[...].astype(F32) - RATE_MAT * new
    error_new[...] = part[...] + joined(gots) - approx


def update(replicas, part, gots, first_row, weight, moment, first, second):
    rows, cols = weight.shape
    block = 128
    spec = pl.BlockSpec((rows, block), lambda i: (0, i))
    out = shape(rows, cols)
    mine = lambda size: pl.BlockSpec((size, block), lambda i: (first_row // size, i))
    rows_of = lambda size, first: pl.BlockSpec((size, block), lambda i: (first, i))
    own = [mine(rows)] if len(gots) == 1 else [rows_of(*got[1:]) for got in gots]
    gots = gots if len(gots) == 1 else [got[0] for got in gots]
    return call(
        functools.partial(update_kernel, replicas), "update", (out, out, out),
        (part, weight, moment, first, second, *gots),
        [mine(rows), spec, spec, pl.BlockSpec(first.shape, lambda i: (0, 0)),
         pl.BlockSpec((second.shape[0], block), lambda i: (0, i))] + own,
        out_specs=[spec] * 3, grid=(cols // block,),
    )


def orthonormal_kernel(sizes, panel_ref, out_ref, *outs):
    rank = panel_ref.shape[0]
    place = lax.broadcasted_iota(jnp.int32, (rank, 1), 0)
    cuts = [sum(sizes[:i]) for i in range(len(sizes) + 1)]
    panels = [panel_ref[:, a:b] for a, b in zip(cuts, cuts[1:])]
    for number in range(rank):
        for which, (a, b) in enumerate(zip(cuts, cuts[1:])):
            part = panels[which]
            column = part[number : number + 1, :]
            column = column * lax.rsqrt(jnp.sum(column * column, -1, keepdims=True) + 1e-20)
            out_ref[number : number + 1, a:b] = column
            outs[which][number : number + 1, :] = column
            if number + 1 < rank:
                along = jnp.sum(part * column, -1, keepdims=True)
                panels[which] = part - jnp.where(place > number, along, 0.0) * column


class Order:
    def __init__(self):
        self.last = None

    def __call__(self, x):
        if self.last is not None:
            x = tie(x, self.last)
        self.last = x
        return x

    def mark(self, x):
        self.last = x


def exchange(x, bit):
    return across(x, "dp", bit)


class RowSum:
    def __init__(self, x, bits):
        self.x, self.bits, self.step = x, bits, 0
        self.steps = bits[:2] + bits[2:] + bits[1::-1]
        self.place = lax.axis_index("dp")

    def send(self):
        step, bit, x = self.step, self.steps[self.step], self.x
        self.upper = (self.place & bit) != 0
        if step < 2:
            half = x.shape[0] // 2
            x = jnp.where(self.upper, x[:half], x[half:])
        self.got = across(x, "dp", bit)

    def receive(self, order):
        step, x, upper = self.step, self.x, self.upper
        got = order(self.got)
        if step < 2:
            half = x.shape[0] // 2
            x = (jnp.where(upper, x[half:], x[:half]).astype(F32) + got.astype(F32)).astype(BF16)
        elif step < len(self.bits):
            x = (x.astype(F32) + got.astype(F32)).astype(BF16)
        else:
            x = jnp.concatenate([jnp.where(upper, got, x), jnp.where(upper, x, got)], 0)
        self.x = x
        self.step += 1
        return self.step < len(self.steps)


class WholeSum:
    def __init__(self, x, bits):
        self.x, self.steps, self.step = x, bits, 0

    def send(self):
        self.got = across(self.x, "dp", self.steps[self.step])

    def receive(self, order):
        self.x = self.x + order(self.got)
        self.step += 1
        return self.step < len(self.steps)


def advance(order, *sums):
    for one in sums:
        if one.step < len(one.steps) and one.receive(order):
            one.send()


def shards(
    token_ids, masked_at, live_counts, tables, table_mom, vec_whole, vec_mom, vec_split, split_mom,
    head_bias, bias_mom, w_qkv, w_out, w_up, w_down, mom_qkv, mom_out, mom_up, mom_down,
    err_qkv, err_out, err_up, err_down, start_qkv, start_out, start_up, start_down,
):
    groups = lax.axis_size("tensor")
    replicas = lax.axis_size("dp")
    images, length = token_ids.shape
    vocab = head_bias.shape[0]
    total_rows, columns = tables.shape
    features = w_qkv.shape[0]
    width = w_qkv.shape[1] // 3
    hidden = w_up.shape[1]
    own = images // groups
    rows = own * length
    rank = start_qkv.shape[1]
    total = total_rows + -total_rows % 128
    used = 3 * width
    all_rows = used + width
    bits = [1 << i for i in range(replicas.bit_length() - 1)]
    meta = jnp.stack([lax.axis_index("tensor"), lax.axis_index("dp") & 1]).astype(jnp.int32)
    order = Order()

    bf = functools.partial(shape, dtype=BF16)
    dma = lambda n: pltpu.SemaphoreType.DMA((n,))
    vm = lambda *dims: pltpu.VMEM(dims, BF16)

    def cores(pieces):
        return tuple(core_swap(piece) for piece in pieces)

    first_own, first_half = call(
        pack_first_kernel, "pack_first", (bf(all_rows, features), bf(all_rows // 2, features)),
        (meta, w_qkv.T, w_out), [SMEM] + [ANY] * 2, [dma(2)],
    )
    order.mark(first_half)
    up_half, down_half, table_own, table_half = call(
        pack_rest_kernel, "pack_rest",
        (bf(features // 2, hidden), bf(hidden // 2, features), bf(columns, total), bf(columns // 2, total)),
        (order(meta), w_up, w_down, tables.T), [SMEM] + [ANY] * 2 + [VMEM], [dma(2)],
    )
    order.mark(table_half)
    first_far = [chip_swap(first_half)]
    part = bf(columns, rows + length)
    e_far, e_near, e_own, ids_rows = call(
        functools.partial(embed_kernel, own, vocab), "embed",
        (bf(2, columns, rows + length // 2), part, part, shape(length, images, dtype=jnp.int32)),
        (meta, live_counts, token_ids, masked_at, order(table_own)), [SMEM, SMEM, VMEM, VMEM, VMEM],
    )
    order.mark(e_far)
    first_near, up_near, down_near, table_near = cores((first_own, w_up, w_down, table_own))
    own_starts = jnp.concatenate((start_up.T, start_down.T, start_out.T, start_qkv.T), 1)
    gap = -own_starts.shape[1] % 128
    bias_row = jnp.pad(vec_split, ((0, rank - 1), (gap, 0)))
    small = [jnp.concatenate([own_starts, bias_row], 1)]
    small.append(core_swap(small[0]))
    e_one = core_swap(e_near)
    e_two = chip_swap(e_far)
    first_far[0] = order(first_far[0])
    first_far.append(exchange(first_far[0], 1))
    count = WholeSum(tie(jnp.broadcast_to(jnp.sum(live_counts).astype(F32), (8, 128)), first_far[0]), bits)
    count.send()
    e_two = order(e_two)
    up_far = [chip_swap(tie(up_half, e_two))]
    small.append(chip_swap(tie(small[0], e_two)))
    e_three = core_swap(e_two)
    advance(order, count)
    starts = splits = small

    state = (shape(rows, features), shape(rows, 1), bf(rows, features))
    block = (bf(3, rows, width), shape(rows, width // HD), bf(rows, width))
    res = call(
        functools.partial(attention_first_kernel, length), "attention_first", state + block + block,
        (tie(meta, up_near, down_near, first_near, table_near), order(e_own), e_one, e_two, e_three, vec_whole,
         small[0], small[1], first_own, first_near),
        [SMEM] + [VMEM] * 7 + [ANY] * 2, [pltpu.VMEM((features, rows), F32), vm(2, used, features), dma(2)],
    )
    normed0, inverse0, h0b = res[:3]
    order.mark(h0b)
    kept = [res[3:6], res[6:9]]
    small[2] = order(small[2])
    first_far[1] = order(first_far[1])
    first_both = cores([tie(x, first_far[1]) for x in first_far])
    small.append(core_swap(small[2]))
    up_far[0] = order(up_far[0])
    down_far = [chip_swap(tie(down_half, up_far[0]))]
    up_far.append(exchange(up_far[0], 1))
    advance(order, count)
    res = call(
        functools.partial(attention_second_kernel, length), "attention_second", state + block + block,
        (meta, order(normed0), h0b, vec_whole, splits[2], splits[3], kept[0][2], kept[1][2], first_own, first_near,
         *first_far, *first_both),
        [SMEM] + [VMEM] * 7 + [ANY] * 6, [vm(2, all_rows, features), vm(2, width, features), dma(6)],
    )
    normed1, inverse1, h1b = res[:3]
    order.mark(h1b)
    kept += [res[3:6], res[6:9]]
    while count.step < len(bits):
        advance(order, count)
    down_far[0] = order(down_far[0])
    down_far.append(exchange(down_far[0], 1))
    table_far = [chip_swap(tie(table_half, down_far[0]))]
    act = bf(rows, hidden)
    slope = shape(rows, hidden)
    a0, a1, p0, p1, low = call(
        mlp_first_kernel, "mlp_first", (act, act, slope, slope, shape(rows, features)),
        (meta, order(h1b), splits[0], splits[1], w_up, up_near, w_down, down_near),
        [SMEM] + [VMEM] * 3 + [ANY] * 4, [vm(4, features, hidden), dma(4)],
    )
    order.mark(low)
    up_far[1] = order(up_far[1])
    up_both = cores([tie(x, up_far[1]) for x in up_far])
    table_far[0] = order(table_far[0])
    table_far.append(exchange(table_far[0], 1))
    down_far[1] = order(down_far[1])
    down_both = cores([tie(x, down_far[1]) for x in down_far])
    a2, a3, p2, p3, normed2, inverse2, h2b = call(
        mlp_second_kernel, "mlp_second", (act, act, slope, slope) + state,
        (meta, order(h1b), splits[2], splits[3], low, normed1, vec_whole, *up_far, *up_both, *down_far, *down_both),
        [SMEM] + [VMEM] * 6 + [ANY] * 8, [vm(4, features, hidden), dma(8)],
    )
    order.mark(h2b)
    table_far[1] = order(table_far[1])
    table_both = cores([tie(x, table_far[1]) for x in table_far])
    count = count.x[0, :1]
    pair = lambda a, b, dtype: shape(2, a, b, dtype=dtype)
    dz2, dz2b, loss_part, g_bias, g_vec2, head_send, head_keep = call(
        functools.partial(head_kernel, own, vocab), "head",
        (
            shape(rows, features), bf(rows, features), shape(1, 128), shape(1, total),
            shape(3, features), pair(columns, total, BF16), pair(columns, total, BF16),
        ),
        (
            meta, live_counts, count, token_ids, masked_at,
            jnp.pad(head_bias, (0, total - vocab)).reshape(1, total), vec_whole, order(h2b), normed2, inverse2,
            table_own, table_near, *table_far, *table_both,
        ),
        [SMEM] * 3 + [VMEM] * 7 + [ANY] * 6,
        [vm(features, total), vm(features, total), pltpu.VMEM((rows, features), F32), dma(6)],
    )
    order.mark(dz2b)

    head_near = core_swap(head_send)
    left = shape(2, rank, features)
    down_send, left_down_a = call(
        down_send_kernel, "down_send", (pair(hidden, features, BF16), left),
        (order(dz2b), a1, a3, starts[1], starts[3]),
    )
    order.mark(down_send)
    down_got = core_swap(down_send)
    head_far = order((head_keep[1].astype(F32) + head_near[1].astype(F32)).astype(BF16))
    head_in = chip_swap(head_far)
    up_send, left_up_a, dh_a, hidden_a = call(
        up_send_kernel, "up_send",
        (pair(features, hidden, BF16), left, shape(rows, features), shape(2, 1, hidden)),
        (meta, order(dz2b), h1b, p1, p3, starts[1], starts[3], up_near, *up_both, down_near, *down_both),
        [SMEM] + [VMEM] * 6 + [ANY] * 6, [vm(rows, hidden), vm(4, features, hidden), dma(6)],
    )
    order.mark(dh_a)
    up_got = core_swap(up_send)
    down_a, down_b, down_part, left_down_b = call(
        down_keep_kernel, "down_keep",
        (bf(hidden // 2, features), bf(hidden // 2, features), shape(hidden, features), left),
        (order(dz2b), a0, a2, starts[0], starts[2], down_got, err_down[0]),
    )
    order.mark(left_down_b)
    down_in_a = chip_swap(down_a)
    both, up_b, up_part, left_up_b, dz1, dz1b, g_vec1, hidden_b = call(
        up_keep_kernel, "up_keep",
        (bf(hidden // 2 + features // 4, hidden), bf(features - features // 4, hidden), shape(features, hidden), left, shape(rows, features), bf(rows, features),
         shape(3, features), shape(2, 1, hidden)),
        (meta, dz2, order(dz2b), h1b, normed1, inverse1, vec_whole, dh_a, p0, p2, starts[0], starts[2],
         up_got, err_up[0], down_b, w_up, *up_far, w_down, *down_far),
        [SMEM] + [VMEM] * 14 + [ANY] * 6, [vm(rows, hidden), vm(4, features, hidden), dma(6)],
    )
    order.mark(dz1b)
    pack_width = 3 * features + width
    pack = shape(2, 16, pack_width)
    scratch = [vm(rows, used), vm(rows, width)]
    first_send, pack_a, dh_b = call(
        functools.partial(attention_send_kernel, length), "attention_send",
        (pair(all_rows, features, BF16), pack, shape(rows, features)),
        (meta, order(dz1b), h0b, kept[1][0], kept[3][0], kept[1][1], kept[3][1], kept[1][2], kept[3][2],
         starts[1], starts[3], left_up_a, left_down_a, hidden_a, first_near, *first_both),
        [SMEM] + [VMEM] * 13 + [ANY] * 3, scratch + [vm(2, all_rows, features), dma(3)],
    )
    order.mark(dh_b)
    head_in, down_in_a = order(head_in), order(down_in_a)
    first_got = core_swap(tie(first_send, down_in_a))
    both_in = chip_swap(tie(both, down_in_a))
    cols = bf(rows, columns)
    first_far_grad, first_part, pack_b, pack_a, d_far, d_near, d_own = call(
        functools.partial(attention_keep_kernel, length), "attention_keep",
        (bf(all_rows, features), shape(all_rows, features), pack, pack, pair(rows, columns, BF16), cols, cols),
        (meta, order(dz1b), h0b, kept[0][0], kept[2][0], kept[0][1], kept[2][1], kept[0][2], kept[2][2],
         starts[0], starts[2], left_up_b, left_down_b, hidden_b, first_got, err_qkv[0].T, err_out[0],
         dz1, dh_b, normed0, inverse0, vec_whole, g_vec1, g_vec2, g_bias, loss_part, pack_a,
         first_own, *first_far),
        [SMEM] + [VMEM] * 26 + [ANY] * 3,
        scratch + [pltpu.VMEM((rows, features), F32), vm(2, all_rows, features), dma(3)],
    )
    order.mark(d_far)

    d_two = chip_swap(d_far)
    both_in = order(both_in)
    mine = order(pack_b + core_swap(tie(pack_a, both_in)))
    d_one = core_swap(tie(d_near, both_in))
    mine_in = chip_swap(mine[1])
    mine = order(mine[0] + mine_in)
    panels = WholeSum(mine[:8], bits)
    panels.send()
    advance(order, panels)
    d_two = order(d_two)
    d_three = core_swap(d_two)
    up_in_b = chip_swap(tie(up_b, d_two))
    advance(order, panels)
    table_grad = call(
        functools.partial(scatter_kernel, own, vocab), "scatter", bf(columns, total),
        (ids_rows, order(d_own), d_one, d_two, d_three, head_near, head_keep, head_in),
    )
    order.mark(table_grad)
    table_sum = RowSum(table_grad, bits)
    table_sum.send()
    first_in = chip_swap(tie(first_far_grad, table_grad))
    while panels.step < len(bits):
        advance(order, panels)
    sizes = (features, features, features, width)
    bases, base_up, base_down, base_qkv, base_out = call(
        functools.partial(orthonormal_kernel, sizes), "orthonormal",
        (shape(rank, pack_width),) + tuple(shape(rank, size) for size in sizes), (order(panels.x),),
    )
    order.mark(bases)
    packed = call(
        right_mlp_kernel, "right_mlp", shape(rank, 2 * features + pack_width),
        (down_part, down_in_a, both_in, up_part, order(up_in_b), bases, mine[8:]),
    )
    order.mark(packed)
    packed = WholeSum(packed, bits[2:] + bits[:2])
    packed.send()
    advance(order, table_sum)
    advance(order, packed)
    advance(order, packed)
    advance(order, table_sum)
    while packed.step < len(bits):
        advance(order, packed)
    right_up, right_down = packed.x[:, :features], packed.x[:, features : 2 * features]
    rest = packed.x[:, 2 * features :]
    rights = call(
        functools.partial(right_attention_kernel, used), "right_attention", shape(rank, features + used),
        (first_part, order(first_in), bases),
    )
    order.mark(rights)
    rights = WholeSum(rights, bits[2:] + bits[:2])
    rights.send()
    advance(order, table_sum)
    down = update(replicas, down_part, [(down_in_a, hidden // 2, 0), (both_in, hidden // 2, 0)], 0, w_down, mom_down, order(base_down), right_down)
    order.mark(down[0])
    advance(order, rights)
    advance(order, table_sum)
    up = update(replicas, up_part, [(both_in, features // 4, 2 * hidden // features), (up_in_b, features - features // 4, 0)], 0, w_up, mom_up, order(base_up), right_up)
    order.mark(up[0])
    rest = tie(rest, up[0])
    while rights.step < len(bits):
        advance(order, rights)
    right_out, right_qkv = rights.x[:, :features], rights.x[:, features:]
    out = update(replicas, first_part, [first_in], used, w_out, mom_out, order(base_out), right_out)
    qkv = update(replicas, first_part, [first_in], 0, w_qkv.T, mom_qkv.T, right_qkv, base_qkv)
    order.mark(qkv[0])
    while table_sum.step < len(table_sum.steps):
        advance(order, table_sum)

    table_grad = table_sum.x[:, :total_rows].astype(F32)
    vectors = [rest[2 + n // 3, n % 3 * features : (n % 3 + 1) * features] for n in range(8)]
    results = [jnp.where(jnp.arange(2) == 0, rest[4, 2 * features : 2 * features + 1], count)]

    def momentum_step(weight, moment, grad, rate):
        new_moment = BETA * moment + grad
        return (weight.astype(F32) - rate * new_moment, new_moment)

    new = momentum_step(tables.T, table_mom.T, table_grad, RATE_TAB)
    results += [new[0].T, new[1].T]
    results += momentum_step(vec_whole, vec_mom, jnp.stack(vectors), RATE_VEC)
    results += momentum_step(vec_split, split_mom, rest[0:1, : vec_split.shape[1]], RATE_VEC)
    results += momentum_step(head_bias, bias_mom, rest[1, :vocab], RATE_VEC)
    one = 1.0 / replicas
    for (weight, moment, error), base, right, flip in (
        (qkv, base_qkv, right_qkv, True), (out, base_out, right_out, False),
        (up, base_up, right_up, False), (down, base_down, right_down, False),
    ):
        if flip:
            weight, moment, error = weight.T, moment.T, error.T
        results += [weight, moment, error[None], base.T[None], right.T * one]
    return tuple(results)


def solution(mesh):
    rows, cols = P("tensor", None), P(None, "tensor")
    batch = P("dp", None)
    in_specs = (
        batch, batch, P("dp"), cols, cols, P(), P(), rows, rows, P(), P(),
        cols, rows, cols, rows, cols, rows, cols, rows,
        P("dp", None, "tensor"), P("dp", "tensor", None), P("dp", None, "tensor"), P("dp", "tensor", None),
        rows, rows, rows, rows,
    )
    left = P("tensor", None, None)
    out_specs = (P(), cols, cols, P(), P(), rows, rows, P(), P())
    for side in (cols, rows, cols, rows):
        out_specs += (side, side, P("dp", *side), left, rows)
    return jax.shard_map(shards, mesh=mesh, in_specs=in_specs, out_specs=out_specs, check_vma=False)
```
